32 devices in a mesh: groups: 2 (over y), dp: 8 (over z, x), tensor: 2 (over core).
Axes of the slice: x: 2, y: 2, z: 4, core: 2. Of those that a mesh axis runs over, the one named last changes fastest.
Arguments:
- activations: bfloat16 [16, 384, 5120], P(('groups', 'dp'), None, 'tensor'), parts along dimension 0, may hold values from -6 to 6
- out_grads: bfloat16 [16, 384, 5120], P(('groups', 'dp'), None, 'tensor'), parts along dimension 0, may hold values from -6 to 6
- projections: bfloat16 [5120, 128], P('tensor'), may hold values from -0.078125 to 0.078125
- sample_index: int32 [16, 256], P(('groups', 'dp')), parts along dimension 0, may hold values from 0 to 383
- queries: bfloat16 [512, 4096], P(('groups', 'dp'), 'tensor'), parts along dimension 0, may hold values from -0.005859375 to 0.005859375
Outputs:
- scores: float32 [16, 256], P(('groups', 'dp'), 'tensor'), parts along dimension 0
The draws below stay inside these ranges and needn't reach their ends.
There are 2 independent parts, one for each index of `groups`. The reference program is written for one: setup_inputs(seed, part) draws one part's arguments, and reference() takes and returns one part's arrays. A program takes and returns all parts, laid end to end along the dimension named above; an argument that names none is the same for every part. Nothing has to cross between parts.
All inputs are finite; a program needn't handle non-finite values.
Results may differ from the reference program's by a relative error of at most 0.003.
Values may be sent and summed in bfloat16 or wider, within the bound.
No kernel may reach another device: no remote copies, remote signals or barrier semaphores. Data moves between devices by JAX's collectives and lax.ppermute only.
A program may use at most 64 MiB of HBM per device.

```python
import jax
import jax.numpy as jnp
from jax import lax

D = 5120
R = 64
SAMPLE = 256
POOL = 384
QUERIES = 256
CLIPS = 8


def place_ends(values, rng, least, largest):
    extent = values.shape
    spot = [jax.random.randint(jax.random.fold_in(rng, axis), (), 0, extent[axis]) for axis in range(len(extent))]
    values = values.at[tuple(spot)].set(least)
    longest = extent.index(max(extent))
    spot[longest] = (spot[longest] + 1) % extent[longest]
    return values.at[tuple(spot)].set(largest)


def level_of(rng, extent, cuts, least, top_value):
    level, own = 1.0, jax.random.fold_in(rng, 6)
    for axis_at, parts in cuts:
        draws = jnp.exp(jax.random.uniform(jax.random.fold_in(own, axis_at), (parts,), jnp.float32, least / len(cuts), top_value / len(cuts)))
        level = level * jnp.repeat(draws, extent[axis_at] // parts).reshape([-1 if axis == axis_at else 1 for axis in range(len(extent))])
    return level


def bell_draw(key, dims, deviation, reach, shards=(), held_as=jnp.bfloat16):
    array = jax.random.normal(key, dims, jnp.float32) * deviation
    if len(shards) > 0:
        array = level_of(key, dims, shards, -0.22, 0.18) * array
    return jnp.clip(array, min=-reach, max=reach).astype(held_as)


def setup_inputs(seed: int = 0, part: int = 0) -> dict:
    streams_of = jax.random.split(jax.random.key(seed), 6)
    own_keys = jax.random.split(jax.random.fold_in(streams_of[5], part), 6)
    activations = bell_draw(own_keys[0], (CLIPS, POOL, D), 1.0, 6.0, ((0, 8), (2, 2)))
    out_grads = bell_draw(own_keys[1], (CLIPS, POOL, D), 1.0, 6.0, ((0, 8), (2, 2)))
    projections = bell_draw(streams_of[2], (D, 2 * R), D ** -0.5, 0.078125, ((0, 2),))
    sample_index = place_ends(jax.random.randint(own_keys[3], (CLIPS, SAMPLE), 0, POOL), jax.random.fold_in(own_keys[3], 1), 0, POOL - 1).astype(jnp.int32)
    queries = bell_draw(own_keys[4], (QUERIES, R * R), (R * R * SAMPLE) ** -0.5, 0.005859375, ((0, 8), (1, 2)))
    return {"activations": activations, "out_grads": out_grads, "projections": projections, "sample_index": sample_index, "queries": queries}


def reference(activations, out_grads, projections, sample_index, queries):
    left_proj = projections[:, 0:R].astype(jnp.float32)
    right_proj = projections[:, R:2 * R].astype(jnp.float32)

    def one_clip(items):
        clip_in, clip_grad, picks = items
        picked_in = jnp.take(clip_in, picks.astype(jnp.int32), axis=0).astype(jnp.float32)
        picked_grad = jnp.take(clip_grad, picks.astype(jnp.int32), axis=0).astype(jnp.float32)
        left = jnp.dot(picked_in, left_proj, precision=lax.Precision.HIGHEST)
        right = jnp.dot(picked_grad, right_proj, precision=lax.Precision.HIGHEST)
        sketch = jnp.dot(right.T, left, precision=lax.Precision.HIGHEST)
        return sketch.astype(jnp.bfloat16).reshape(R * R)

    sketches = lax.map(one_clip, (activations, out_grads, sample_index))
    return jnp.dot(sketches, queries.T, preferred_element_type=jnp.float32)
```

```python
import functools

import jax
import jax.numpy as jnp
from jax import lax
from jax.experimental import pallas as pl
from jax.experimental.pallas import tpu as pltpu
from jax.sharding import PartitionSpec as P

F32 = jnp.float32
BF16 = jnp.bfloat16
LANES = 128


def project_kernel(rank, picks_ref, acts_ref, grads_ref, proj_ref, out_ref):
    rows = acts_ref.shape[0]
    samples = picks_ref.shape[1]
    token = lax.broadcasted_iota(jnp.int32, (rows, samples), 0) + pl.program_id(0) * rows
    hits = jnp.where(token == picks_ref[...], 1.0, 0.0).astype(BF16)
    count = jnp.dot(hits, jnp.ones((samples, 2 * rank), BF16), preferred_element_type=F32)
    left = jnp.dot(acts_ref[...], proj_ref[...], preferred_element_type=F32)
    right = jnp.dot(grads_ref[...], proj_ref[...], preferred_element_type=F32)
    column = lax.broadcasted_iota(jnp.int32, (rows, 2 * rank), 1)
    out_ref[...] = jnp.where(column < rank, left * count, right)


def sketch_kernel(rank, place_ref, own_ref, other_ref, out_ref, held):
    total = own_ref[...] + other_ref[...]
    held[...] = lax.dot_general(
        total[:, rank : 2 * rank],
        total[:, 0:rank],
        (((0,), (0,)), ((), ())),
        precision=lax.Precision.HIGHEST,
        preferred_element_type=F32,
    )
    pairs = out_ref.shape[1]
    start = place_ref[0] * (2 * pairs)
    even = held[pl.ds(start, pairs, stride=2), :]
    odd = held[pl.ds(start + 1, pairs, stride=2), :]
    rows = jnp.concatenate([even, odd], axis=1).astype(BF16)
    out_ref[...] = jnp.broadcast_to(rows[None], out_ref.shape)


def score_kernel(place_ref, sketches_ref, queries_ref, out_ref, wide, padded):
    clips, pairs, _ = sketches_ref.shape
    queries = queries_ref.shape[0]
    wide[...] = sketches_ref[...].astype(F32).reshape(clips * pairs, LANES)
    padded[...] = jnp.zeros_like(padded)
    first = pl.multiple_of(place_ref[1] * queries, queries)
    padded[pl.ds(first, queries), :] = queries_ref[...]
    flat = jnp.concatenate(
        [wide[pl.ds(j, clips, stride=pairs), :] for j in range(pairs)], axis=1
    ).astype(BF16)
    scores = lax.dot_general(
        flat, padded[...], (((1,), (1,)), ((), ())), preferred_element_type=F32
    )
    for half in range(2):
        out_ref[:, half, :] = jnp.where(place_ref[2] == half, scores, 0.0)


def on_device(activations, out_grads, projections, sample_index, queries):
    clips = lax.axis_size("dp")
    tokens, units = activations.shape[1:]
    rank = projections.shape[1] // 2
    samples = sample_index.shape[1]
    own_queries, entries = queries.shape
    pairs = entries // LANES
    per_row = LANES // own_queries
    out_rows = clips // 2 // per_row
    spot = lax.axis_index("dp")
    half = lax.axis_index("tensor")
    place = jnp.stack([half, spot % per_row, spot // (clips // 2)]).astype(jnp.int32)
    smem = pl.BlockSpec(memory_space=pltpu.SMEM)
    vmem = pl.BlockSpec(memory_space=pltpu.VMEM)

    tile = LANES
    partial = pl.pallas_call(
        functools.partial(project_kernel, rank),
        grid=(tokens // tile,),
        in_specs=[
            pl.BlockSpec((1, samples), lambda i: (0, 0)),
            pl.BlockSpec((None, tile, units), lambda i: (0, i, 0)),
            pl.BlockSpec((None, tile, units), lambda i: (0, i, 0)),
            pl.BlockSpec((units, 2 * rank), lambda i: (0, 0)),
        ],
        out_specs=pl.BlockSpec((tile, 2 * rank), lambda i: (i, 0)),
        out_shape=jax.ShapeDtypeStruct((tokens, 2 * rank), F32),
        name="project",
    )(sample_index, activations, out_grads, projections)

    other = lax.ppermute(partial, "tensor", [(0, 1), (1, 0)])
    sketch = pl.pallas_call(
        functools.partial(sketch_kernel, rank),
        in_specs=[smem, vmem, vmem],
        out_specs=vmem,
        out_shape=jax.ShapeDtypeStruct((clips, pairs, LANES), BF16),
        scratch_shapes=[pltpu.VMEM((rank, rank), F32)],
        name="sketch",
    )(place, partial, other)

    sketches = lax.all_to_all(sketch, "dp", split_axis=0, concat_axis=0, tiled=True)
    scored = pl.pallas_call(
        score_kernel,
        in_specs=[smem, vmem, vmem],
        out_specs=vmem,
        out_shape=jax.ShapeDtypeStruct((clips, 2, LANES), F32),
        scratch_shapes=[
            pltpu.VMEM((clips * pairs, LANES), F32),
            pltpu.VMEM((LANES, entries), BF16),
        ],
        name="score",
    )(place, sketches, queries)

    back = lax.all_to_all(
        scored.reshape(2 * clips, LANES), ("dp", "tensor"), split_axis=0, concat_axis=0, tiled=True
    )
    summed = back.reshape(2, out_rows, 2 * per_row, LANES).sum(axis=(0, 2))
    return summed.reshape(1, out_rows * LANES)


def solution(mesh):
    in_specs = (
        P(("groups", "dp"), None, "tensor"),
        P(("groups", "dp"), None, "tensor"),
        P("tensor", None),
        P(("groups", "dp"), None),
        P(("groups", "dp"), "tensor"),
    )
    out_specs = P(("groups", "dp"), "tensor")
    return jax.shard_map(
        on_device, mesh=mesh, in_specs=in_specs, out_specs=out_specs, check_vma=False
    )
```

```python
import functools

import jax
import jax.numpy as jnp
from jax import lax
from jax.experimental import pallas as pl
from jax.experimental.pallas import tpu as pltpu
from jax.sharding import PartitionSpec as P

F32 = jnp.float32
BF16 = jnp.bfloat16
LANES = 128
CHUNK = 512


def project_kernel(rank, picks_ref, acts_ref, grads_ref, proj_ref, out_ref, acts, grads, proj, sems):
    tokens, units = acts.shape
    samples = picks_ref.shape[1]
    copies = []
    for i in range(units // CHUNK):
        part = pl.ds(i * CHUNK, CHUNK)
        three = (
            pltpu.make_async_copy(proj_ref.at[part, :], proj.at[part, :], sems.at[i, 0]),
            pltpu.make_async_copy(acts_ref.at[0, :, part], acts.at[:, part], sems.at[i, 1]),
            pltpu.make_async_copy(grads_ref.at[0, :, part], grads.at[:, part], sems.at[i, 2]),
        )
        for copy in three:
            copy.start()
        copies.append(three)

    token = lax.broadcasted_iota(jnp.int32, (tokens, samples), 0)
    hits = jnp.where(token == picks_ref[...], 1.0, 0.0).astype(BF16)
    count = jnp.dot(hits, jnp.ones((samples, 2 * rank), BF16), preferred_element_type=F32)
    column = lax.broadcasted_iota(jnp.int32, (tokens, 2 * rank), 1)
    count = jnp.where(column < rank, count, 1.0)

    is_left = lax.broadcasted_iota(jnp.int32, (CHUNK, 2 * rank), 1) < rank
    total = None
    for i, three in enumerate(copies):
        for copy in three:
            copy.wait()
        part = pl.ds(i * CHUNK, CHUNK)
        weights = proj[part, :]
        zero = jnp.zeros_like(weights)
        both = jnp.concatenate(
            [jnp.where(is_left, weights, zero), jnp.where(is_left, zero, weights)], axis=0
        )
        term = jnp.dot(
            jnp.concatenate([acts[:, part], grads[:, part]], axis=1), both, preferred_element_type=F32
        )
        total = term if total is None else total + term
    out_ref[...] = total * count


def sketch_kernel(rank, own_ref, other_ref, out_ref, held):
    total = own_ref[...] + other_ref[...]
    held[...] = lax.dot_general(
        total[:, rank : 2 * rank],
        total[:, 0:rank],
        (((0,), (0,)), ((), ())),
        precision=lax.Precision.HIGHEST,
        preferred_element_type=F32,
    )
    pairs = out_ref.shape[0]
    even = held[pl.ds(0, pairs, stride=2), :]
    odd = held[pl.ds(1, pairs, stride=2), :]
    out_ref[...] = jnp.concatenate([even, odd], axis=1).astype(BF16)


def score_kernel(rounds, *refs):
    sketches, (own_ref, other_ref), outs, wide = (
        refs[:rounds],
        refs[rounds : rounds + 2],
        refs[rounds + 2 : -1],
        refs[-1],
    )
    pairs = sketches[0].shape[0]
    queries = own_ref.shape[0]
    slots = wide.shape[0] // pairs
    wide[...] = jnp.zeros_like(wide)
    for r in range(rounds):
        wide[pl.ds(r, pairs, stride=slots), :] = sketches[r][...].astype(F32)
    half = lax.axis_index("tensor")
    scores = None
    for side, ref in ((half, own_ref), (1 - half, other_ref)):
        start = side * (slots * pairs // 2)
        flat = jnp.concatenate(
            [
                wide[pl.ds(pl.multiple_of(start + j * slots, slots), slots), :]
                for j in range(pairs // 2)
            ],
            axis=1,
        ).astype(BF16)
        term = lax.dot_general(
            flat, ref[...], (((1,), (1,)), ((), ())), preferred_element_type=F32
        )
        scores = term if scores is None else scores + term
    low = lax.rem(lax.axis_index("dp"), rounds)
    spread = jnp.concatenate([scores] * rounds, axis=1)
    block = lax.broadcasted_iota(jnp.int32, spread.shape, 1) // queries
    spread = jnp.where(block == low, spread, 0.0)
    for r in range(rounds):
        outs[r][...] = spread[r : r + 1, :]


def on_device(activations, out_grads, projections, sample_index, queries):
    clips = lax.axis_size("dp")
    tokens, units = activations.shape[1:]
    rank = projections.shape[1] // 2
    own_queries, entries = queries.shape
    pairs = 2 * entries // LANES
    rounds = clips // 2
    slots = -(-rounds // 8) * 8
    vmem = pl.BlockSpec(memory_space=pltpu.VMEM)
    hbm = pl.BlockSpec(memory_space=pl.ANY)
    swap = [(0, 1), (1, 0)]

    def place(a, l, t):
        return (a * rounds + l) * 2 + t

    there = [
        [
            (place(a, l, t), place(t, (l + r) % rounds, a))
            for a in range(2)
            for l in range(rounds)
            for t in range(2)
        ]
        for r in range(rounds)
    ]
    back = [[(dst, src) for src, dst in perm] for perm in there]

    other_queries = lax.ppermute(queries, "tensor", swap)
    partial = pl.pallas_call(
        functools.partial(project_kernel, rank),
        in_specs=[vmem, hbm, hbm, hbm],
        out_specs=vmem,
        out_shape=jax.ShapeDtypeStruct((tokens, 2 * rank), F32),
        scratch_shapes=[
            pltpu.VMEM((tokens, units), BF16),
            pltpu.VMEM((tokens, units), BF16),
            pltpu.VMEM((units, 2 * rank), BF16),
            pltpu.SemaphoreType.DMA((units // CHUNK, 3)),
        ],
        compiler_params=pltpu.CompilerParams(vmem_limit_bytes=16 << 20),
        name="project",
    )(sample_index, activations, out_grads, projections)

    other = lax.ppermute(partial, "tensor", swap)
    sketch = pl.pallas_call(
        functools.partial(sketch_kernel, rank),
        in_specs=[vmem, vmem],
        out_specs=vmem,
        out_shape=jax.ShapeDtypeStruct((pairs, LANES), BF16),
        scratch_shapes=[pltpu.VMEM((rank, rank), F32)],
        compiler_params=pltpu.CompilerParams(vmem_limit_bytes=8 << 20),
        name="sketch",
    )(partial, other)

    sketches = [lax.ppermute(sketch, ("dp", "tensor"), perm) for perm in there]
    width = rounds * own_queries
    scored = pl.pallas_call(
        functools.partial(score_kernel, rounds),
        in_specs=[vmem] * (rounds + 2),
        out_specs=[vmem] * rounds,
        out_shape=[jax.ShapeDtypeStruct((1, width), F32)] * rounds,
        scratch_shapes=[pltpu.VMEM((pairs * slots, LANES), F32)],
        compiler_params=pltpu.CompilerParams(vmem_limit_bytes=16 << 20),
        name="score",
    )(*sketches, queries, other_queries)

    parts = [lax.ppermute(s, ("dp", "tensor"), perm) for s, perm in zip(scored, back)]
    return functools.reduce(jnp.add, parts)


def solution(mesh):
    in_specs = (
        P(("groups", "dp"), None, "tensor"),
        P(("groups", "dp"), None, "tensor"),
        P("tensor", None),
        P(("groups", "dp"), None),
        P(("groups", "dp"), "tensor"),
    )
    out_specs = P(("groups", "dp"), "tensor")
    return jax.shard_map(
        on_device, mesh=mesh, in_specs=in_specs, out_specs=out_specs, check_vma=False
    )
```

```python
import functools

import jax
import jax.numpy as jnp
from jax import lax
from jax.experimental import pallas as pl
from jax.experimental.pallas import tpu as pltpu
from jax.sharding import PartitionSpec as P

F32 = jnp.float32
BF16 = jnp.bfloat16
LANES = 128
CHUNK = 512


def project_kernel(rank, acts_ref, grads_ref, proj_ref, out_ref, both, proj, sems):
    tokens, units = acts_ref.shape[1:]
    copies = []
    for i in range(units // CHUNK):
        part = pl.ds(i * CHUNK, CHUNK)
        three = (
            pltpu.make_async_copy(proj_ref.at[part, :], proj.at[part, :], sems.at[i, 0]),
            pltpu.make_async_copy(
                acts_ref.at[0, :, part], both.at[pl.ds(0, tokens), part], sems.at[i, 1]
            ),
            pltpu.make_async_copy(
                grads_ref.at[0, :, part], both.at[pl.ds(tokens, tokens), part], sems.at[i, 2]
            ),
        )
        for copy in three:
            copy.start()
        copies.append(three)

    total = None
    for i, three in enumerate(copies):
        for copy in three:
            copy.wait()
        part = pl.ds(i * CHUNK, CHUNK)
        term = jnp.dot(both[:, part], proj[part, :], preferred_element_type=F32)
        total = term if total is None else total + term
    column = lax.broadcasted_iota(jnp.int32, (tokens, 2 * rank), 1)
    out_ref[...] = jnp.where(column < rank, total[0:tokens], total[tokens:])


def count_kernel(picks_ref, out_ref):
    tokens, width = out_ref.shape
    samples = picks_ref.shape[1]
    token = lax.broadcasted_iota(jnp.int32, (tokens, samples), 0)
    hits = jnp.where(token == picks_ref[...], 1.0, 0.0).astype(BF16)
    out_ref[...] = jnp.dot(hits, jnp.ones((samples, width), BF16), preferred_element_type=F32)


def sketch_kernel(rank, count_ref, own_ref, other_ref, out_ref, held):
    total = own_ref[...] + other_ref[...]
    held[...] = lax.dot_general(
        total[:, rank : 2 * rank],
        total[:, 0:rank] * count_ref[...],
        (((0,), (0,)), ((), ())),
        precision=lax.Precision.HIGHEST,
        preferred_element_type=F32,
    )
    pairs = out_ref.shape[0]
    even = held[pl.ds(0, pairs, stride=2), :]
    odd = held[pl.ds(1, pairs, stride=2), :]
    out_ref[...] = jnp.concatenate([even, odd], axis=1).astype(BF16)


def score_kernel(rounds, *refs):
    sketches, queries, outs, wide = refs[:rounds], refs[rounds : rounds + 4], refs[rounds + 4 : -1], refs[-1]
    pairs = sketches[0].shape[0]
    own_queries = queries[0].shape[0]
    slots = wide.shape[0] // pairs
    wide[...] = jnp.zeros_like(wide)
    for r in range(rounds):
        wide[pl.ds(r, pairs, stride=slots), :] = sketches[r][...].astype(F32)
    half = lax.axis_index("tensor")
    flats = []
    for side in (half, 1 - half):
        start = side * (slots * pairs // 2)
        flats.append(
            jnp.concatenate(
                [
                    wide[pl.ds(pl.multiple_of(start + j * slots, slots), slots), :]
                    for j in range(pairs // 2)
                ],
                axis=1,
            ).astype(BF16)
        )
    spot = lax.axis_index("dp")
    block = lax.broadcasted_iota(jnp.int32, (slots, 2 * rounds * own_queries), 1) // own_queries
    spread = jnp.zeros(block.shape, F32)
    for k, member in ((0, spot), (1, spot + 1 - 2 * lax.rem(spot, 2))):
        scores = sum(
            lax.dot_general(
                flat, queries[2 * k + i][...], (((1,), (1,)), ((), ())), preferred_element_type=F32
            )
            for i, flat in enumerate(flats)
        )
        here = block == lax.rem(member, 2 * rounds)
        spread = jnp.where(here, jnp.concatenate([scores] * (2 * rounds), axis=1), spread)
    for r in range(rounds):
        outs[r][...] = spread[r : r + 1, :]


def on_device(activations, out_grads, projections, sample_index, queries):
    clips = lax.axis_size("dp")
    tokens, units = activations.shape[1:]
    rank = projections.shape[1] // 2
    own_queries, entries = queries.shape
    pairs = 2 * entries // LANES
    rounds = clips // 4
    slots = -(-rounds // 8) * 8
    vmem = pl.BlockSpec(memory_space=pltpu.VMEM)
    hbm = pl.BlockSpec(memory_space=pl.ANY)
    swap = [(0, 1), (1, 0)]

    def place(a, l, b, t):
        return ((a * rounds + l) * 2 + b) * 2 + t

    there = [
        [
            (place(a, l, b, t), place(t, (l + r) % rounds, b, a))
            for a in range(2)
            for l in range(rounds)
            for b in range(2)
            for t in range(2)
        ]
        for r in range(rounds)
    ]
    back = [[(dst, src) for src, dst in perm] for perm in there]

    pair_queries = lax.ppermute(queries, "dp", [(d, d ^ 1) for d in range(clips)])
    other_queries = lax.ppermute(queries, "tensor", swap)
    other_pair_queries = lax.ppermute(pair_queries, "tensor", swap)
    partial = pl.pallas_call(
        functools.partial(project_kernel, rank),
        in_specs=[hbm] * 3,
        out_specs=vmem,
        out_shape=jax.ShapeDtypeStruct((tokens, 2 * rank), F32),
        scratch_shapes=[
            pltpu.VMEM((2 * tokens, units), BF16),
            pltpu.VMEM((units, 2 * rank), BF16),
            pltpu.SemaphoreType.DMA((units // CHUNK, 3)),
        ],
        compiler_params=pltpu.CompilerParams(vmem_limit_bytes=55000 << 10),
        cost_estimate=pl.CostEstimate(
            flops=8 * tokens * units * rank, bytes_accessed=4 * tokens * units, transcendentals=0
        ),
        name="project",
    )(activations, out_grads, projections)

    other = lax.ppermute(partial, "tensor", swap)
    count = pl.pallas_call(
        count_kernel,
        in_specs=[vmem],
        out_specs=vmem,
        out_shape=jax.ShapeDtypeStruct((tokens, rank), F32),
        compiler_params=pltpu.CompilerParams(vmem_limit_bytes=8 << 20),
        name="count",
    )(sample_index)
    sketch = pl.pallas_call(
        functools.partial(sketch_kernel, rank),
        in_specs=[vmem] * 3,
        out_specs=vmem,
        out_shape=jax.ShapeDtypeStruct((pairs, LANES), BF16),
        scratch_shapes=[pltpu.VMEM((rank, rank), F32)],
        compiler_params=pltpu.CompilerParams(vmem_limit_bytes=8 << 20),
        name="sketch",
    )(count, partial, other)

    sketches = [lax.ppermute(sketch, ("dp", "tensor"), perm) for perm in there]
    width = 2 * rounds * own_queries
    scored = pl.pallas_call(
        functools.partial(score_kernel, rounds),
        in_specs=[vmem] * (rounds + 4),
        out_specs=[vmem] * rounds,
        out_shape=[jax.ShapeDtypeStruct((1, width), F32)] * rounds,
        scratch_shapes=[pltpu.VMEM((pairs * slots, LANES), F32)],
        compiler_params=pltpu.CompilerParams(vmem_limit_bytes=16 << 20),
        name="score",
    )(*sketches, queries, other_queries, pair_queries, other_pair_queries)

    parts = [lax.ppermute(s, ("dp", "tensor"), perm) for s, perm in zip(scored, back)]
    return functools.reduce(jnp.add, parts)


def solution(mesh):
    in_specs = (
        P(("groups", "dp"), None, "tensor"),
        P(("groups", "dp"), None, "tensor"),
        P("tensor", None),
        P(("groups", "dp"), None),
        P(("groups", "dp"), "tensor"),
    )
    out_specs = P(("groups", "dp"), "tensor")
    return jax.shard_map(
        on_device, mesh=mesh, in_specs=in_specs, out_specs=out_specs, check_vma=False
    )
```

```python
import functools

import jax
import jax.numpy as jnp
from jax import lax
from jax.experimental import pallas as pl
from jax.experimental.pallas import tpu as pltpu
from jax.sharding import PartitionSpec as P

F32 = jnp.float32
BF16 = jnp.bfloat16
LANES = 128
CHUNK = 512


def project_kernel(rank, acts_ref, grads_ref, proj_ref, out_ref, both, proj, sems):
    tokens, units = acts_ref.shape[1:]
    copies = []
    for i in range(units // CHUNK):
        part = pl.ds(i * CHUNK, CHUNK)
        three = (
            pltpu.make_async_copy(proj_ref.at[part, :], proj.at[part, :], sems.at[i, 0]),
            pltpu.make_async_copy(
                acts_ref.at[0, :, part], both.at[pl.ds(0, tokens), part], sems.at[i, 1]
            ),
            pltpu.make_async_copy(
                grads_ref.at[0, :, part], both.at[pl.ds(tokens, tokens), part], sems.at[i, 2]
            ),
        )
        for k, copy in enumerate(three):
            copy.start(priority=(i + k) % 2)
        copies.append(three)

    total = None
    for i, three in enumerate(copies):
        for copy in three:
            copy.wait()
        part = pl.ds(i * CHUNK, CHUNK)
        term = jnp.dot(both[:, part], proj[part, :], preferred_element_type=F32)
        total = term if total is None else total + term
    column = lax.broadcasted_iota(jnp.int32, (tokens, 2 * rank), 1)
    out_ref[...] = jnp.where(column < rank, total[0:tokens], total[tokens:])


def count_kernel(picks_ref, out_ref):
    tokens, width = out_ref.shape
    samples = picks_ref.shape[1]
    token = lax.broadcasted_iota(jnp.int32, (tokens, samples), 0)
    hits = jnp.where(token == picks_ref[...], 1.0, 0.0).astype(BF16)
    out_ref[...] = jnp.dot(hits, jnp.ones((samples, width), BF16), preferred_element_type=F32)


def sketch_kernel(rank, count_ref, own_ref, other_ref, out_ref, held):
    total = own_ref[...] + other_ref[...]
    held[...] = lax.dot_general(
        total[:, rank : 2 * rank],
        total[:, 0:rank] * count_ref[...],
        (((0,), (0,)), ((), ())),
        precision=lax.Precision.HIGHEST,
        preferred_element_type=F32,
    )
    pairs = out_ref.shape[0]
    even = held[pl.ds(0, pairs, stride=2), :]
    odd = held[pl.ds(1, pairs, stride=2), :]
    out_ref[...] = jnp.concatenate([even, odd], axis=1).astype(BF16)


def score_kernel(rounds, *refs):
    sketches, queries, outs, wide = refs[:rounds], refs[rounds : rounds + 2], refs[rounds + 2 : -1], refs[-1]
    pairs = sketches[0].shape[0]
    own_queries = queries[0].shape[0]
    slots = wide.shape[0] // pairs
    wide[...] = jnp.zeros_like(wide)
    for r in range(rounds):
        wide[pl.ds(r, pairs, stride=slots), :] = sketches[r][...].astype(F32)
    spot = lax.axis_index("dp")
    upper = spot // rounds
    scores = None
    for ref, half in zip(queries, (upper, 1 - upper)):
        start = half * (slots * pairs // 2)
        flat = jnp.concatenate(
            [
                wide[pl.ds(pl.multiple_of(start + j * slots, slots), slots), :]
                for j in range(pairs // 2)
            ],
            axis=1,
        ).astype(BF16)
        term = lax.dot_general(
            flat, ref[...], (((1,), (1,)), ((), ())), preferred_element_type=F32
        )
        scores = term if scores is None else scores + term
    spread = jnp.concatenate([scores] * rounds, axis=1)
    block = lax.broadcasted_iota(jnp.int32, spread.shape, 1) // own_queries
    spread = jnp.where(block == lax.rem(spot, rounds), spread, 0.0)
    for r in range(rounds):
        outs[r][...] = spread[r : r + 1, :]


def on_device(activations, out_grads, projections, sample_index, queries):
    clips = lax.axis_size("dp")
    tokens, units = activations.shape[1:]
    rank = projections.shape[1] // 2
    own_queries, entries = queries.shape
    pairs = 2 * entries // LANES
    rounds = clips // 2
    slots = -(-rounds // 8) * 8
    vmem = pl.BlockSpec(memory_space=pltpu.VMEM)
    hbm = pl.BlockSpec(memory_space=pl.ANY)
    swap = [(0, 1), (1, 0)]

    def place(a, m, t):
        return (a * rounds + m) * 2 + t

    taken = [
        lax.ppermute(
            queries,
            ("dp", "tensor"),
            [
                (place(t, m, a ^ j), place(a, m, t))
                for a in range(2)
                for m in range(rounds)
                for t in range(2)
            ],
        )
        for j in range(2)
    ]
    across = [
        [(a * rounds + m, a * rounds + (m ^ r)) for a in range(2) for m in range(rounds)]
        for r in range(1, rounds)
    ]
    partial = pl.pallas_call(
        functools.partial(project_kernel, rank),
        in_specs=[hbm] * 3,
        out_specs=vmem,
        out_shape=jax.ShapeDtypeStruct((tokens, 2 * rank), F32),
        scratch_shapes=[
            pltpu.VMEM((2 * tokens, units), BF16),
            pltpu.VMEM((units, 2 * rank), BF16),
            pltpu.SemaphoreType.DMA((units // CHUNK, 3)),
        ],
        compiler_params=pltpu.CompilerParams(vmem_limit_bytes=55000 << 10),
        cost_estimate=pl.CostEstimate(
            flops=8 * tokens * units * rank, bytes_accessed=4 * tokens * units, transcendentals=0
        ),
        name="project",
    )(activations, out_grads, projections)

    other = lax.ppermute(partial, "tensor", swap)
    count = pl.pallas_call(
        count_kernel,
        in_specs=[vmem],
        out_specs=vmem,
        out_shape=jax.ShapeDtypeStruct((tokens, rank), F32),
        compiler_params=pltpu.CompilerParams(vmem_limit_bytes=8 << 20),
        name="count",
    )(sample_index)
    sketch = pl.pallas_call(
        functools.partial(sketch_kernel, rank),
        in_specs=[vmem] * 3,
        out_specs=vmem,
        out_shape=jax.ShapeDtypeStruct((pairs, LANES), BF16),
        scratch_shapes=[pltpu.VMEM((rank, rank), F32)],
        compiler_params=pltpu.CompilerParams(vmem_limit_bytes=8 << 20),
        name="sketch",
    )(count, partial, other)

    sketches = [sketch] + [lax.ppermute(sketch, "dp", perm) for perm in across]
    width = rounds * own_queries
    scored = pl.pallas_call(
        functools.partial(score_kernel, rounds),
        in_specs=[vmem] * (rounds + 2),
        out_specs=[vmem] * rounds,
        out_shape=[jax.ShapeDtypeStruct((1, width), F32)] * rounds,
        scratch_shapes=[pltpu.VMEM((pairs * slots, LANES), F32)],
        compiler_params=pltpu.CompilerParams(vmem_limit_bytes=16 << 20),
        name="score",
    )(*sketches, *taken)

    parts = [lax.ppermute(s, "dp", perm) for s, perm in zip(scored[1:], across)]
    return functools.reduce(jnp.add, parts, scored[0])


def solution(mesh):
    in_specs = (
        P(("groups", "dp"), None, "tensor"),
        P(("groups", "dp"), None, "tensor"),
        P("tensor", None),
        P(("groups", "dp"), None),
        P(("groups", "dp"), "tensor"),
    )
    out_specs = P(("groups", "dp"), "tensor")
    return jax.shard_map(
        on_device, mesh=mesh, in_specs=in_specs, out_specs=out_specs, check_vma=False
    )
```

```python
import functools

import jax
import jax.numpy as jnp
from jax import lax
from jax.experimental import pallas as pl
from jax.experimental.pallas import tpu as pltpu
from jax.sharding import PartitionSpec as P

F32 = jnp.float32
BF16 = jnp.bfloat16
LANES = 128
CHUNK = 512


def project_kernel(rank, acts_ref, grads_ref, proj_ref, out_ref, both, proj, sems):
    tokens, units = acts_ref.shape[1:]
    copies = []
    for i in range(units // CHUNK):
        part = pl.ds(i * CHUNK, CHUNK)
        three = (
            pltpu.make_async_copy(proj_ref.at[part, :], proj.at[part, :], sems.at[i, 0]),
            pltpu.make_async_copy(
                acts_ref.at[0, :, part], both.at[pl.ds(0, tokens), part], sems.at[i, 1]
            ),
            pltpu.make_async_copy(
                grads_ref.at[0, :, part], both.at[pl.ds(tokens, tokens), part], sems.at[i, 2]
            ),
        )
        for copy in three:
            copy.start()
        copies.append(three)

    total = None
    for i, three in enumerate(copies):
        for copy in three:
            copy.wait()
        part = pl.ds(i * CHUNK, CHUNK)
        term = jnp.dot(both[:, part], proj[part, :], preferred_element_type=F32)
        total = term if total is None else total + term
    column = lax.broadcasted_iota(jnp.int32, (tokens, 2 * rank), 1)
    out_ref[...] = jnp.where(column < rank, total[0:tokens], total[tokens:])


def count_kernel(picks_ref, out_ref):
    tokens, width = out_ref.shape
    samples = picks_ref.shape[1]
    token = lax.broadcasted_iota(jnp.int32, (tokens, samples), 0)
    hits = jnp.where(token == picks_ref[...], 1.0, 0.0).astype(BF16)
    out_ref[...] = jnp.dot(hits, jnp.ones((samples, width), BF16), preferred_element_type=F32)


def sketch_kernel(rank, count_ref, own_ref, other_ref, out_ref, held):
    total = own_ref[...] + other_ref[...]
    held[...] = lax.dot_general(
        total[:, rank : 2 * rank],
        total[:, 0:rank] * count_ref[...],
        (((0,), (0,)), ((), ())),
        precision=lax.Precision.HIGHEST,
        preferred_element_type=F32,
    )
    pairs = out_ref.shape[0]
    even = held[pl.ds(0, pairs, stride=2), :]
    odd = held[pl.ds(1, pairs, stride=2), :]
    out_ref[...] = jnp.concatenate([even, odd], axis=1).astype(BF16)


def score_kernel(rounds, *refs):
    sketches, queries, outs, wide = refs[:rounds], refs[rounds : rounds + 4], refs[rounds + 4 : -1], refs[-1]
    pairs = sketches[0].shape[0]
    own_queries = queries[0].shape[0]
    slots = wide.shape[0] // pairs
    wide[...] = jnp.zeros_like(wide)
    for r in range(rounds):
        wide[pl.ds(r, pairs, stride=slots), :] = sketches[r][...].astype(F32)
    spot = lax.axis_index("dp")
    core = lax.axis_index("tensor")
    near = spot // rounds == core
    scores = None
    for i, half in enumerate((core, 1 - core)):
        entries = jnp.where(near, queries[2 * i][...], queries[2 * i + 1][...])
        start = half * (slots * pairs // 2)
        flat = jnp.concatenate(
            [
                wide[pl.ds(pl.multiple_of(start + j * slots, slots), slots), :]
                for j in range(pairs // 2)
            ],
            axis=1,
        ).astype(BF16)
        term = lax.dot_general(
            flat, entries, (((1,), (1,)), ((), ())), preferred_element_type=F32
        )
        scores = term if scores is None else scores + term
    spread = jnp.concatenate([scores] * rounds, axis=1)
    block = lax.broadcasted_iota(jnp.int32, spread.shape, 1) // own_queries
    spread = jnp.where(block == lax.rem(spot, rounds), spread, 0.0)
    for r in range(rounds):
        outs[r][...] = spread[r : r + 1, :]


def on_device(activations, out_grads, projections, sample_index, queries):
    clips = lax.axis_size("dp")
    tokens, units = activations.shape[1:]
    rank = projections.shape[1] // 2
    own_queries, entries = queries.shape
    pairs = 2 * entries // LANES
    rounds = clips // 2
    slots = -(-rounds // 8) * 8
    vmem = pl.BlockSpec(memory_space=pltpu.VMEM)
    hbm = pl.BlockSpec(memory_space=pl.ANY)
    swap = [(0, 1), (1, 0)]

    far = lax.ppermute(queries, "dp", [(d, (d + rounds) % clips) for d in range(clips)])
    core_own = lax.ppermute(queries, "tensor", swap)
    core_far = lax.ppermute(far, "tensor", swap)
    across = [
        [(a * rounds + m, a * rounds + (m ^ r)) for a in range(2) for m in range(rounds)]
        for r in range(1, rounds)
    ]
    partial = pl.pallas_call(
        functools.partial(project_kernel, rank),
        in_specs=[hbm] * 3,
        out_specs=vmem,
        out_shape=jax.ShapeDtypeStruct((tokens, 2 * rank), F32),
        scratch_shapes=[
            pltpu.VMEM((2 * tokens, units), BF16),
            pltpu.VMEM((units, 2 * rank), BF16),
            pltpu.SemaphoreType.DMA((units // CHUNK, 3)),
        ],
        compiler_params=pltpu.CompilerParams(vmem_limit_bytes=55000 << 10),
        cost_estimate=pl.CostEstimate(
            flops=8 * tokens * units * rank, bytes_accessed=4 * tokens * units, transcendentals=0
        ),
        name="project",
    )(activations, out_grads, projections)

    other = lax.ppermute(partial, "tensor", swap)
    count = pl.pallas_call(
        count_kernel,
        in_specs=[vmem],
        out_specs=vmem,
        out_shape=jax.ShapeDtypeStruct((tokens, rank), F32),
        compiler_params=pltpu.CompilerParams(vmem_limit_bytes=8 << 20),
        name="count",
    )(sample_index)
    sketch = pl.pallas_call(
        functools.partial(sketch_kernel, rank),
        in_specs=[vmem] * 3,
        out_specs=vmem,
        out_shape=jax.ShapeDtypeStruct((pairs, LANES), BF16),
        scratch_shapes=[pltpu.VMEM((rank, rank), F32)],
        compiler_params=pltpu.CompilerParams(vmem_limit_bytes=8 << 20),
        name="sketch",
    )(count, partial, other)

    sketches = [sketch] + [lax.ppermute(sketch, "dp", perm) for perm in across]
    width = rounds * own_queries
    scored = pl.pallas_call(
        functools.partial(score_kernel, rounds),
        in_specs=[vmem] * (rounds + 4),
        out_specs=[vmem] * rounds,
        out_shape=[jax.ShapeDtypeStruct((1, width), F32)] * rounds,
        scratch_shapes=[pltpu.VMEM((pairs * slots, LANES), F32)],
        compiler_params=pltpu.CompilerParams(vmem_limit_bytes=16 << 20),
        name="score",
    )(*sketches, queries, far, core_own, core_far)

    parts = [lax.ppermute(s, "dp", perm) for s, perm in zip(scored[1:], across)]
    return functools.reduce(jnp.add, parts, scored[0])


def solution(mesh):
    in_specs = (
        P(("groups", "dp"), None, "tensor"),
        P(("groups", "dp"), None, "tensor"),
        P("tensor", None),
        P(("groups", "dp"), None),
        P(("groups", "dp"), "tensor"),
    )
    out_specs = P(("groups", "dp"), "tensor")
    return jax.shard_map(
        on_device, mesh=mesh, in_specs=in_specs, out_specs=out_specs, check_vma=False
    )
```

```python
import functools

import jax
import jax.numpy as jnp
from jax import lax
from jax.experimental import pallas as pl
from jax.experimental.pallas import tpu as pltpu
from jax.sharding import PartitionSpec as P

F32 = jnp.float32
BF16 = jnp.bfloat16
LANES = 128
CHUNK = 512


def project_kernel(rank, acts_ref, grads_ref, proj_ref, out_ref, both, proj, sems):
    tokens, units = acts_ref.shape[1:]
    copies = []
    for i in range(units // CHUNK):
        part = pl.ds(i * CHUNK, CHUNK)
        three = (
            pltpu.make_async_copy(proj_ref.at[part, :], proj.at[part, :], sems.at[i, 0]),
            pltpu.make_async_copy(
                acts_ref.at[0, :, part], both.at[pl.ds(0, tokens), part], sems.at[i, 1]
            ),
            pltpu.make_async_copy(
                grads_ref.at[0, :, part], both.at[pl.ds(tokens, tokens), part], sems.at[i, 2]
            ),
        )
        for copy in three:
            copy.start()
        copies.append(three)

    total = None
    for i, three in enumerate(copies):
        for copy in three:
            copy.wait()
        part = pl.ds(i * CHUNK, CHUNK)
        term = jnp.dot(both[:, part], proj[part, :], preferred_element_type=F32)
        total = term if total is None else total + term
    column = lax.broadcasted_iota(jnp.int32, (tokens, 2 * rank), 1)
    out_ref[...] = jnp.where(column < rank, total[0:tokens], total[tokens:])


def count_kernel(picks_ref, out_ref):
    tokens, width = out_ref.shape
    samples = picks_ref.shape[1]
    token = lax.broadcasted_iota(jnp.int32, (tokens, samples), 0)
    hits = jnp.where(token == picks_ref[...], 1.0, 0.0).astype(BF16)
    out_ref[...] = jnp.dot(hits, jnp.ones((samples, width), BF16), preferred_element_type=F32)


def sketch_kernel(rank, count_ref, own_ref, other_ref, out_ref, held):
    total = own_ref[...] + other_ref[...]
    held[...] = lax.dot_general(
        total[:, rank : 2 * rank],
        total[:, 0:rank] * count_ref[...],
        (((0,), (0,)), ((), ())),
        precision=lax.Precision.HIGHEST,
        preferred_element_type=F32,
    )
    pairs = out_ref.shape[1]
    even = held[pl.ds(0, pairs, stride=2), :]
    odd = held[pl.ds(1, pairs, stride=2), :]
    rows = jnp.concatenate([even, odd], axis=1).astype(BF16)
    out_ref[...] = jnp.broadcast_to(rows[None], out_ref.shape)


def score_kernel(sketches_ref, *refs):
    queries, out_ref, wide = refs[:4], refs[4], refs[5]
    rounds, pairs, _ = sketches_ref.shape
    own_queries = queries[0].shape[0]
    slots = wide.shape[0] // pairs
    wide[...] = jnp.zeros_like(wide)
    for r in range(rounds):
        wide[pl.ds(r, pairs, stride=slots), :] = sketches_ref[r].astype(F32)
    spot = lax.axis_index("dp")
    core = lax.axis_index("tensor")
    near = spot // rounds == core
    scores = None
    for i, half in enumerate((core, 1 - core)):
        entries = jnp.where(near, queries[2 * i][...], queries[2 * i + 1][...])
        start = half * (slots * pairs // 2)
        flat = jnp.concatenate(
            [
                wide[pl.ds(pl.multiple_of(start + j * slots, slots), slots), :]
                for j in range(pairs // 2)
            ],
            axis=1,
        ).astype(BF16)
        term = lax.dot_general(
            flat, entries, (((1,), (1,)), ((), ())), preferred_element_type=F32
        )
        scores = term if scores is None else scores + term
    spread = jnp.concatenate([scores] * rounds, axis=1)
    block = lax.broadcasted_iota(jnp.int32, spread.shape, 1) // own_queries
    spread = jnp.where(block == lax.rem(spot, rounds), spread, 0.0)
    out_ref[...] = spread[0:rounds]


def on_device(activations, out_grads, projections, sample_index, queries):
    clips = lax.axis_size("dp")
    tokens, units = activations.shape[1:]
    rank = projections.shape[1] // 2
    own_queries, entries = queries.shape
    pairs = 2 * entries // LANES
    rounds = clips // 2
    slots = -(-rounds // 8) * 8
    vmem = pl.BlockSpec(memory_space=pltpu.VMEM)
    hbm = pl.BlockSpec(memory_space=pl.ANY)
    swap = [(0, 1), (1, 0)]

    far = lax.ppermute(queries, "dp", [(d, (d + rounds) % clips) for d in range(clips)])
    core_own = lax.ppermute(queries, "tensor", swap)
    core_far = lax.ppermute(far, "tensor", swap)
    halves = [list(range(a * rounds, (a + 1) * rounds)) for a in range(2)]
    partial = pl.pallas_call(
        functools.partial(project_kernel, rank),
        in_specs=[hbm] * 3,
        out_specs=vmem,
        out_shape=jax.ShapeDtypeStruct((tokens, 2 * rank), F32),
        scratch_shapes=[
            pltpu.VMEM((2 * tokens, units), BF16),
            pltpu.VMEM((units, 2 * rank), BF16),
            pltpu.SemaphoreType.DMA((units // CHUNK, 3)),
        ],
        compiler_params=pltpu.CompilerParams(vmem_limit_bytes=55000 << 10),
        cost_estimate=pl.CostEstimate(
            flops=8 * tokens * units * rank, bytes_accessed=4 * tokens * units, transcendentals=0
        ),
        name="project",
    )(activations, out_grads, projections)

    other = lax.ppermute(partial, "tensor", swap)
    count = pl.pallas_call(
        count_kernel,
        in_specs=[vmem],
        out_specs=vmem,
        out_shape=jax.ShapeDtypeStruct((tokens, rank), F32),
        compiler_params=pltpu.CompilerParams(vmem_limit_bytes=8 << 20),
        name="count",
    )(sample_index)
    sketch = pl.pallas_call(
        functools.partial(sketch_kernel, rank),
        in_specs=[vmem] * 3,
        out_specs=vmem,
        out_shape=jax.ShapeDtypeStruct((rounds, pairs, LANES), BF16),
        scratch_shapes=[pltpu.VMEM((rank, rank), F32)],
        compiler_params=pltpu.CompilerParams(vmem_limit_bytes=8 << 20),
        name="sketch",
    )(count, partial, other)

    sketches = lax.all_to_all(sketch, "dp", 0, 0, axis_index_groups=halves, tiled=True)
    width = rounds * own_queries
    scored = pl.pallas_call(
        score_kernel,
        in_specs=[vmem] * 5,
        out_specs=vmem,
        out_shape=jax.ShapeDtypeStruct((rounds, width), F32),
        scratch_shapes=[pltpu.VMEM((pairs * slots, LANES), F32)],
        compiler_params=pltpu.CompilerParams(vmem_limit_bytes=16 << 20),
        name="score",
    )(sketches, queries, far, core_own, core_far)

    parts = lax.all_to_all(scored, "dp", 0, 0, axis_index_groups=halves, tiled=True)
    return parts.sum(axis=0, keepdims=True)


def solution(mesh):
    in_specs = (
        P(("groups", "dp"), None, "tensor"),
        P(("groups", "dp"), None, "tensor"),
        P("tensor", None),
        P(("groups", "dp"), None),
        P(("groups", "dp"), "tensor"),
    )
    out_specs = P(("groups", "dp"), "tensor")
    return jax.shard_map(
        on_device, mesh=mesh, in_specs=in_specs, out_specs=out_specs, check_vma=False
    )
```

```python
import functools

import jax
import jax.numpy as jnp
from jax import lax
from jax.experimental import pallas as pl
from jax.experimental.pallas import tpu as pltpu
from jax.sharding import PartitionSpec as P

F32 = jnp.float32
BF16 = jnp.bfloat16
LANES = 128
CHUNK = 128


def project_kernel(rank, acts_ref, grads_ref, proj_ref, out_ref, both, proj, sems):
    chunks = both.shape[0]
    weights = pltpu.make_async_copy(proj_ref, proj, sems.at[chunks, 0])
    weights.start()
    copies = []
    for i in range(chunks):
        part = pl.ds(i * CHUNK, CHUNK)
        two = (
            pltpu.make_async_copy(
                acts_ref.at[0, part, :], both.at[i, pl.ds(0, CHUNK), :], sems.at[i, 0]
            ),
            pltpu.make_async_copy(
                grads_ref.at[0, part, :], both.at[i, pl.ds(CHUNK, CHUNK), :], sems.at[i, 1]
            ),
        )
        for copy in two:
            copy.start()
        copies.append(two)

    weights.wait()
    column = lax.broadcasted_iota(jnp.int32, (CHUNK, 2 * rank), 1)
    for i, two in enumerate(copies):
        for copy in two:
            copy.wait()
        term = jnp.dot(both[i], proj[...], preferred_element_type=F32)
        out_ref[pl.ds(i * CHUNK, CHUNK), :] = jnp.where(column < rank, term[0:CHUNK], term[CHUNK:])


def count_kernel(picks_ref, out_ref):
    tokens, width = out_ref.shape
    samples = picks_ref.shape[1]
    token = lax.broadcasted_iota(jnp.int32, (tokens, samples), 0)
    hits = jnp.where(token == picks_ref[...], 1.0, 0.0).astype(BF16)
    out_ref[...] = jnp.dot(hits, jnp.ones((samples, width), BF16), preferred_element_type=F32)


def sketch_kernel(rank, count_ref, own_ref, other_ref, out_ref, held):
    total = own_ref[...] + other_ref[...]
    held[...] = lax.dot_general(
        total[:, rank : 2 * rank],
        total[:, 0:rank] * count_ref[...],
        (((0,), (0,)), ((), ())),
        precision=lax.Precision.HIGHEST,
        preferred_element_type=F32,
    )
    pairs = out_ref.shape[0]
    even = held[pl.ds(0, pairs, stride=2), :]
    odd = held[pl.ds(1, pairs, stride=2), :]
    out_ref[...] = jnp.concatenate([even, odd], axis=1).astype(BF16)


def score_kernel(clips, *refs):
    sketches, queries, outs, wide = refs[:clips], refs[clips : clips + 4], refs[clips + 4 : -1], refs[-1]
    pairs = sketches[0].shape[0]
    own_queries = queries[0].shape[0]
    blocks = outs[0].shape[1] // own_queries
    slots = wide.shape[0] // pairs
    wide[...] = jnp.zeros_like(wide)
    for r in range(clips):
        wide[pl.ds(r, pairs, stride=slots), :] = sketches[r][...].astype(F32)
    spot = lax.axis_index("dp")
    core = lax.axis_index("tensor")
    flats = []
    for half in (core, 1 - core):
        start = half * (slots * pairs // 2)
        flats.append(
            jnp.concatenate(
                [
                    wide[pl.ds(pl.multiple_of(start + j * slots, slots), slots), :]
                    for j in range(pairs // 2)
                ],
                axis=1,
            ).astype(BF16)
        )
    block = lax.broadcasted_iota(jnp.int32, (slots, blocks * own_queries), 1) // own_queries
    spread = jnp.zeros(block.shape, F32)
    for k, member in ((0, spot), (1, spot + 1 - 2 * lax.rem(spot, 2))):
        scores = sum(
            lax.dot_general(
                flat, queries[2 * k + i][...], (((1,), (1,)), ((), ())), preferred_element_type=F32
            )
            for i, flat in enumerate(flats)
        )
        here = block == lax.rem(member, blocks)
        spread = jnp.where(here, jnp.concatenate([scores] * blocks, axis=1), spread)
    spread = jnp.where(spot // blocks == core, spread, 0.0)
    for r in range(clips):
        outs[r][...] = spread[r : r + 1, :]


def on_device(activations, out_grads, projections, sample_index, queries):
    clips = lax.axis_size("dp")
    tokens, units = activations.shape[1:]
    rank = projections.shape[1] // 2
    own_queries, entries = queries.shape
    pairs = 2 * entries // LANES
    rounds = clips // 4
    slots = -(-2 * rounds // 8) * 8
    vmem = pl.BlockSpec(memory_space=pltpu.VMEM)
    hbm = pl.BlockSpec(memory_space=pl.ANY)
    swap = [(0, 1), (1, 0)]
    both = ("dp", "tensor")

    def place(a, l, b, t):
        return ((a * rounds + l) * 2 + b) * 2 + t

    spots = [(a, l, b) for a in range(2) for l in range(rounds) for b in range(2)]
    far = [
        [(place(a, l, b, 1 - a), place(1 - a, (l + r) % rounds, b, 1 - a)) for a, l, b in spots]
        for r in range(rounds)
    ]
    near = [
        [(place(a, l, b, a), place(a, (l + r) % rounds, b, a)) for a, l, b in spots]
        for r in range(1, rounds)
    ]
    moves = far + near
    returns = [[(dst, src) for src, dst in perm] for perm in moves]
    to_worker = [(place(a, l, b, 1 - a), place(a, l, b, a)) for a, l, b in spots]

    pair_queries = lax.ppermute(queries, "dp", [(d, d ^ 1) for d in range(clips)])
    other_queries = lax.ppermute(queries, both, to_worker)
    other_pair_queries = lax.ppermute(pair_queries, both, to_worker)
    partial = pl.pallas_call(
        functools.partial(project_kernel, rank),
        in_specs=[hbm] * 3,
        out_specs=vmem,
        out_shape=jax.ShapeDtypeStruct((tokens, 2 * rank), F32),
        scratch_shapes=[
            pltpu.VMEM((tokens // CHUNK, 2 * CHUNK, units), BF16),
            pltpu.VMEM((units, 2 * rank), BF16),
            pltpu.SemaphoreType.DMA((tokens // CHUNK + 1, 2)),
        ],
        compiler_params=pltpu.CompilerParams(vmem_limit_bytes=55000 << 10),
        cost_estimate=pl.CostEstimate(
            flops=8 * tokens * units * rank, bytes_accessed=4 * tokens * units, transcendentals=0
        ),
        name="project",
    )(activations, out_grads, projections)

    other = lax.ppermute(partial, "tensor", swap)
    count = pl.pallas_call(
        count_kernel,
        in_specs=[vmem],
        out_specs=vmem,
        out_shape=jax.ShapeDtypeStruct((tokens, rank), F32),
        compiler_params=pltpu.CompilerParams(vmem_limit_bytes=8 << 20),
        name="count",
    )(sample_index)
    sketch = pl.pallas_call(
        functools.partial(sketch_kernel, rank),
        in_specs=[vmem] * 3,
        out_specs=vmem,
        out_shape=jax.ShapeDtypeStruct((pairs, LANES), BF16),
        scratch_shapes=[pltpu.VMEM((rank, rank), F32)],
        compiler_params=pltpu.CompilerParams(vmem_limit_bytes=8 << 20),
        name="sketch",
    )(count, partial, other)

    sketches = [sketch] + [lax.ppermute(sketch, both, perm) for perm in moves]
    width = 2 * rounds * own_queries
    scored = pl.pallas_call(
        functools.partial(score_kernel, 2 * rounds),
        in_specs=[vmem] * (2 * rounds + 4),
        out_specs=[vmem] * (2 * rounds),
        out_shape=[jax.ShapeDtypeStruct((1, width), F32)] * (2 * rounds),
        scratch_shapes=[pltpu.VMEM((pairs * slots, LANES), F32)],
        compiler_params=pltpu.CompilerParams(vmem_limit_bytes=16 << 20),
        name="score",
    )(*sketches, queries, other_queries, pair_queries, other_pair_queries)

    parts = [lax.ppermute(s, both, perm) for s, perm in zip(scored[1:], returns)]
    return functools.reduce(jnp.add, parts, scored[0])


def solution(mesh):
    in_specs = (
        P(("groups", "dp"), None, "tensor"),
        P(("groups", "dp"), None, "tensor"),
        P("tensor", None),
        P(("groups", "dp"), None),
        P(("groups", "dp"), "tensor"),
    )
    out_specs = P(("groups", "dp"), "tensor")
    return jax.shard_map(
        on_device, mesh=mesh, in_specs=in_specs, out_specs=out_specs, check_vma=False
    )
```

```python
import functools

import jax
import jax.numpy as jnp
from jax import lax
from jax.experimental import pallas as pl
from jax.experimental.pallas import tpu as pltpu
from jax.sharding import PartitionSpec as P

F32 = jnp.float32
BF16 = jnp.bfloat16
LANES = 128
CHUNK = 64


def project_kernel(rank, acts_ref, grads_ref, proj_ref, out_ref, both, proj, sems):
    chunks = both.shape[0]
    weights = pltpu.make_async_copy(proj_ref, proj, sems.at[chunks, 0])
    weights.start()
    copies = []
    for i in range(chunks):
        part = pl.ds(i * CHUNK, CHUNK)
        two = (
            pltpu.make_async_copy(
                acts_ref.at[0, part, :], both.at[i, pl.ds(0, CHUNK), :], sems.at[i, 0]
            ),
            pltpu.make_async_copy(
                grads_ref.at[0, part, :], both.at[i, pl.ds(CHUNK, CHUNK), :], sems.at[i, 1]
            ),
        )
        for copy in two:
            copy.start()
        copies.append(two)

    weights.wait()
    column = lax.broadcasted_iota(jnp.int32, (CHUNK, 2 * rank), 1)
    for i, two in enumerate(copies):
        for copy in two:
            copy.wait()
        term = jnp.dot(both[i], proj[...], preferred_element_type=F32)
        out_ref[pl.ds(i * CHUNK, CHUNK), :] = jnp.where(column < rank, term[0:CHUNK], term[CHUNK:])


def count_kernel(picks_ref, out_ref):
    tokens, width = out_ref.shape
    samples = picks_ref.shape[1]
    token = lax.broadcasted_iota(jnp.int32, (tokens, samples), 0)
    hits = jnp.where(token == picks_ref[...], 1.0, 0.0).astype(BF16)
    out_ref[...] = jnp.dot(hits, jnp.ones((samples, width), BF16), preferred_element_type=F32)


def sketch_kernel(rank, count_ref, own_ref, other_ref, out_ref, held):
    total = own_ref[...] + other_ref[...]
    held[...] = lax.dot_general(
        total[:, rank : 2 * rank],
        total[:, 0:rank] * count_ref[...],
        (((0,), (0,)), ((), ())),
        precision=lax.Precision.HIGHEST,
        preferred_element_type=F32,
    )
    pairs = out_ref.shape[0]
    even = held[pl.ds(0, pairs, stride=2), :]
    odd = held[pl.ds(1, pairs, stride=2), :]
    out_ref[...] = jnp.concatenate([even, odd], axis=1).astype(BF16)


def score_kernel(mates, own_ref, far_ref, *refs):
    queries, (out_ref, back_ref, wide) = refs[: 2 * mates], refs[2 * mates :]
    pairs = own_ref.shape[0]
    own_queries = queries[0].shape[0]
    slots = wide.shape[0] // pairs
    wide[...] = jnp.zeros_like(wide)
    wide[pl.ds(0, pairs, stride=slots), :] = own_ref[...].astype(F32)
    wide[pl.ds(1, pairs, stride=slots), :] = far_ref[...].astype(F32)
    spot = lax.axis_index("dp")
    core = lax.axis_index("tensor")
    flats = []
    for half in (core, 1 - core):
        start = half * (slots * pairs // 2)
        flats.append(
            jnp.concatenate(
                [
                    wide[pl.ds(pl.multiple_of(start + j * slots, slots), slots), :]
                    for j in range(pairs // 2)
                ],
                axis=1,
            ).astype(BF16)
        )
    block = lax.broadcasted_iota(jnp.int32, (slots, mates * own_queries), 1) // own_queries
    spread = jnp.zeros(block.shape, F32)
    for r in range(mates):
        scores = sum(
            lax.dot_general(
                flat, queries[2 * r + i][...], (((1,), (1,)), ((), ())), preferred_element_type=F32
            )
            for i, flat in enumerate(flats)
        )
        here = block == lax.rem(spot, mates) ^ r
        spread = jnp.where(here, jnp.concatenate([scores] * mates, axis=1), spread)
    spread = jnp.where(spot // mates == core, spread, 0.0)
    out_ref[...] = spread[0:1, :]
    back_ref[...] = spread[1:2, :]


def on_device(activations, out_grads, projections, sample_index, queries):
    clips = lax.axis_size("dp")
    tokens, units = activations.shape[1:]
    rank = projections.shape[1] // 2
    own_queries, entries = queries.shape
    pairs = 2 * entries // LANES
    mates = clips // 2
    slots = 8
    vmem = pl.BlockSpec(memory_space=pltpu.VMEM)
    hbm = pl.BlockSpec(memory_space=pl.ANY)
    swap = [(0, 1), (1, 0)]
    both = ("dp", "tensor")

    def place(a, m, t):
        return (a * mates + m) * 2 + t

    spots = [(a, m) for a in range(2) for m in range(mates)]
    there = [(place(a, m, 1 - a), place(1 - a, m, 1 - a)) for a, m in spots]
    there += [(place(a, m, a), place(a, m, 1 - a)) for a, m in spots]
    back = [(dst, src) for src, dst in there]

    taken = []
    for r in range(mates):
        half = lax.ppermute(queries, "dp", [(d, d ^ r) for d in range(clips)]) if r else queries
        taken += [half, lax.ppermute(half, "tensor", swap)]
    partial = pl.pallas_call(
        functools.partial(project_kernel, rank),
        in_specs=[hbm] * 3,
        out_specs=vmem,
        out_shape=jax.ShapeDtypeStruct((tokens, 2 * rank), F32),
        scratch_shapes=[
            pltpu.VMEM((tokens // CHUNK, 2 * CHUNK, units), BF16),
            pltpu.VMEM((units, 2 * rank), BF16),
            pltpu.SemaphoreType.DMA((tokens // CHUNK + 1, 2)),
        ],
        compiler_params=pltpu.CompilerParams(vmem_limit_bytes=55000 << 10),
        cost_estimate=pl.CostEstimate(
            flops=8 * tokens * units * rank, bytes_accessed=4 * tokens * units, transcendentals=0
        ),
        name="project",
    )(activations, out_grads, projections)

    other = lax.ppermute(partial, "tensor", swap)
    count = pl.pallas_call(
        count_kernel,
        in_specs=[vmem],
        out_specs=vmem,
        out_shape=jax.ShapeDtypeStruct((tokens, rank), F32),
        compiler_params=pltpu.CompilerParams(vmem_limit_bytes=8 << 20),
        name="count",
    )(sample_index)
    sketch = pl.pallas_call(
        functools.partial(sketch_kernel, rank),
        in_specs=[vmem] * 3,
        out_specs=vmem,
        out_shape=jax.ShapeDtypeStruct((pairs, LANES), BF16),
        scratch_shapes=[pltpu.VMEM((rank, rank), F32)],
        compiler_params=pltpu.CompilerParams(vmem_limit_bytes=8 << 20),
        name="sketch",
    )(count, partial, other)

    far_sketch = lax.ppermute(sketch, both, there)
    width = mates * own_queries
    near_scores, far_scores = pl.pallas_call(
        functools.partial(score_kernel, mates),
        in_specs=[vmem] * (2 * mates + 2),
        out_specs=[vmem] * 2,
        out_shape=[jax.ShapeDtypeStruct((1, width), F32)] * 2,
        scratch_shapes=[pltpu.VMEM((pairs * slots, LANES), F32)],
        compiler_params=pltpu.CompilerParams(vmem_limit_bytes=(16 + mates // 2) << 20),
        name="score",
    )(sketch, far_sketch, *taken)

    return near_scores + lax.ppermute(far_scores, both, back)


def solution(mesh):
    in_specs = (
        P(("groups", "dp"), None, "tensor"),
        P(("groups", "dp"), None, "tensor"),
        P("tensor", None),
        P(("groups", "dp"), None),
        P(("groups", "dp"), "tensor"),
    )
    out_specs = P(("groups", "dp"), "tensor")
    return jax.shard_map(
        on_device, mesh=mesh, in_specs=in_specs, out_specs=out_specs, check_vma=False
    )
```

```python
import functools

import jax
import jax.numpy as jnp
from jax import lax
from jax.experimental import pallas as pl
from jax.experimental.pallas import tpu as pltpu
from jax.sharding import PartitionSpec as P

F32 = jnp.float32
BF16 = jnp.bfloat16
LANES = 128
CHUNK = 128
PIECES = 2


def project_kernel(rank, acts_ref, grads_ref, proj_ref, *refs):
    outs, (both, proj, sems) = refs[:-3], refs[-3:]
    chunks = both.shape[0]
    weights = pltpu.make_async_copy(proj_ref, proj, sems.at[chunks, 0])
    weights.start()
    copies = []
    for i in range(chunks):
        part = pl.ds(i * CHUNK, CHUNK)
        two = (
            pltpu.make_async_copy(
                acts_ref.at[0, part, :], both.at[i, pl.ds(0, CHUNK), :], sems.at[i, 0]
            ),
            pltpu.make_async_copy(
                grads_ref.at[0, part, :], both.at[i, pl.ds(CHUNK, CHUNK), :], sems.at[i, 1]
            ),
        )
        for copy in two:
            copy.start()
        copies.append(two)

    weights.wait()
    rows = outs[0].shape[0]
    column = lax.broadcasted_iota(jnp.int32, (CHUNK, 2 * rank), 1)
    for i, two in enumerate(copies):
        for copy in two:
            copy.wait()
        term = jnp.dot(both[i], proj[...], preferred_element_type=F32)
        term = jnp.where(column < rank, term[0:CHUNK], term[CHUNK:])
        done = 0
        while done < CHUNK:
            piece, first = divmod(i * CHUNK + done, rows)
            size = min(CHUNK - done, rows - first)
            outs[piece][pl.ds(first, size), :] = term[done : done + size]
            done += size


def count_kernel(picks_ref, out_ref):
    tokens, width = out_ref.shape
    samples = picks_ref.shape[1]
    token = lax.broadcasted_iota(jnp.int32, (tokens, samples), 0)
    hits = jnp.where(token == picks_ref[...], 1.0, 0.0).astype(BF16)
    out_ref[...] = jnp.dot(hits, jnp.ones((samples, width), BF16), preferred_element_type=F32)


def sketch_kernel(rank, count_ref, *refs):
    parts, (out_ref, held) = refs[:-2], refs[-2:]
    chunks = len(parts) // 2
    total = jnp.concatenate([parts[i][...] + parts[chunks + i][...] for i in range(chunks)], axis=0)
    held[...] = lax.dot_general(
        total[:, rank : 2 * rank],
        total[:, 0:rank] * count_ref[...],
        (((0,), (0,)), ((), ())),
        precision=lax.Precision.HIGHEST,
        preferred_element_type=F32,
    )
    pairs = out_ref.shape[0]
    even = held[pl.ds(0, pairs, stride=2), :]
    odd = held[pl.ds(1, pairs, stride=2), :]
    out_ref[...] = jnp.concatenate([even, odd], axis=1).astype(BF16)


def flatten_kernel(mates, own_ref, far_ref, first_ref, second_ref, wide):
    pairs = own_ref.shape[0]
    slots = first_ref.shape[0]
    core = lax.axis_index("tensor")
    wide[...] = jnp.zeros_like(wide)
    sketch = jnp.where(lax.axis_index("dp") // mates == core, far_ref[...], own_ref[...])
    wide[pl.ds(0, pairs, stride=slots), :] = sketch.astype(F32)
    for out_ref, half in ((first_ref, core), (second_ref, 1 - core)):
        start = half * (slots * pairs // 2)
        for j in range(pairs // 2):
            rows = wide[pl.ds(pl.multiple_of(start + j * slots, slots), slots), :]
            out_ref[:, j * LANES : (j + 1) * LANES] = rows.astype(BF16)


def score_kernel(mates, first_ref, second_ref, *refs):
    queries, out_ref = refs[:-1], refs[-1]
    own_queries = queries[0].shape[0]
    slots = first_ref.shape[0]
    flats = (first_ref[...], second_ref[...])
    block = lax.broadcasted_iota(jnp.int32, (slots, mates * own_queries), 1) // own_queries
    spot = lax.axis_index("dp")
    spread = jnp.zeros(block.shape, F32)
    for r in range(mates):
        scores = sum(
            lax.dot_general(
                flat, queries[2 * r + i][...], (((1,), (1,)), ((), ())), preferred_element_type=F32
            )
            for i, flat in enumerate(flats)
        )
        here = block == lax.rem(spot, mates) ^ r
        spread = jnp.where(here, jnp.concatenate([scores] * mates, axis=1), spread)
    out_ref[...] = spread[0:1, :]


def on_device(activations, out_grads, projections, sample_index, queries):
    clips = lax.axis_size("dp")
    tokens, units = activations.shape[1:]
    rank = projections.shape[1] // 2
    own_queries, entries = queries.shape
    pairs = 2 * entries // LANES
    mates = clips // 2
    slots = 8
    vmem = pl.BlockSpec(memory_space=pltpu.VMEM)
    hbm = pl.BlockSpec(memory_space=pl.ANY)
    swap = [(0, 1), (1, 0)]
    both = ("dp", "tensor")

    def place(a, m, t):
        return (a * mates + m) * 2 + t

    spots = [(a, m) for a in range(2) for m in range(mates)]
    there = [(place(a, m, 1 - a), place(1 - a, m, 1 - a)) for a, m in spots]
    there += [(place(a, m, a), place(a, m, 1 - a)) for a, m in spots]
    back = [(dst, src) for src, dst in there]

    halves = [queries]
    for r in range(1, mates):
        halves.append(lax.ppermute(queries, "dp", [(d, d ^ r) for d in range(clips)]))
    partial = pl.pallas_call(
        functools.partial(project_kernel, rank),
        in_specs=[hbm] * 3,
        out_specs=[vmem] * PIECES,
        out_shape=[jax.ShapeDtypeStruct((tokens // PIECES, 2 * rank), F32)] * PIECES,
        scratch_shapes=[
            pltpu.VMEM((tokens // CHUNK, 2 * CHUNK, units), BF16),
            pltpu.VMEM((units, 2 * rank), BF16),
            pltpu.SemaphoreType.DMA((tokens // CHUNK + 1, 2)),
        ],
        compiler_params=pltpu.CompilerParams(vmem_limit_bytes=55000 << 10),
        cost_estimate=pl.CostEstimate(
            flops=8 * tokens * units * rank, bytes_accessed=4 * tokens * units, transcendentals=0
        ),
        name="project",
    )(activations, out_grads, projections)

    other = [lax.ppermute(part, "tensor", swap) for part in partial]
    count = pl.pallas_call(
        count_kernel,
        in_specs=[vmem],
        out_specs=vmem,
        out_shape=jax.ShapeDtypeStruct((tokens, rank), F32),
        compiler_params=pltpu.CompilerParams(vmem_limit_bytes=8 << 20),
        cost_estimate=pl.CostEstimate(flops=1, bytes_accessed=1, transcendentals=0),
        name="count",
    )(sample_index)
    sketch = pl.pallas_call(
        functools.partial(sketch_kernel, rank),
        in_specs=[vmem] * (1 + 2 * len(partial)),
        out_specs=vmem,
        out_shape=jax.ShapeDtypeStruct((pairs, LANES), BF16),
        scratch_shapes=[pltpu.VMEM((rank, rank), F32)],
        compiler_params=pltpu.CompilerParams(vmem_limit_bytes=8 << 20),
        cost_estimate=pl.CostEstimate(flops=1, bytes_accessed=1, transcendentals=0),
        name="sketch",
    )(count, *partial, *other)

    far_sketch = lax.ppermute(sketch, both, there)
    halves, sketch = lax.optimization_barrier((halves, sketch))
    taken = []
    for half in halves:
        taken += [half, lax.ppermute(half, "tensor", swap)]
    width = mates * own_queries
    flats = pl.pallas_call(
        functools.partial(flatten_kernel, mates),
        in_specs=[vmem] * 2,
        out_specs=[vmem] * 2,
        out_shape=[jax.ShapeDtypeStruct((slots, entries), BF16)] * 2,
        scratch_shapes=[pltpu.VMEM((pairs * slots, LANES), F32)],
        compiler_params=pltpu.CompilerParams(vmem_limit_bytes=8 << 20),
        cost_estimate=pl.CostEstimate(flops=1 << 34, bytes_accessed=64 << 20, transcendentals=0),
        name="flatten",
    )(sketch, far_sketch)
    scores = pl.pallas_call(
        functools.partial(score_kernel, mates),
        in_specs=[vmem] * (2 * mates + 2),
        out_specs=vmem,
        out_shape=jax.ShapeDtypeStruct((1, width), F32),
        compiler_params=pltpu.CompilerParams(vmem_limit_bytes=(16 + mates // 2) << 20),
        name="score",
    )(*flats, *taken)
    return lax.ppermute(scores, both, back)


def solution(mesh):
    in_specs = (
        P(("groups", "dp"), None, "tensor"),
        P(("groups", "dp"), None, "tensor"),
        P("tensor", None),
        P(("groups", "dp"), None),
        P(("groups", "dp"), "tensor"),
    )
    out_specs = P(("groups", "dp"), "tensor")
    return jax.shard_map(
        on_device, mesh=mesh, in_specs=in_specs, out_specs=out_specs, check_vma=False
    )
```

```python
import functools

import jax
import jax.numpy as jnp
from jax import lax
from jax.experimental import pallas as pl
from jax.experimental.pallas import tpu as pltpu
from jax.sharding import PartitionSpec as P

F32 = jnp.float32
BF16 = jnp.bfloat16
LANES = 128
PIECES = 2


def first_kernel(out_ref):
    out_ref[...] = jnp.zeros_like(out_ref)


def project_kernel(rank, first_ref, acts_ref, grads_ref, proj_ref, *outs):
    rows = outs[0].shape[0]
    column = lax.broadcasted_iota(jnp.int32, (rows, 2 * rank), 1)
    for i, out_ref in enumerate(outs):
        part = slice(i * rows, (i + 1) * rows)
        term = jnp.dot(
            jnp.concatenate([acts_ref[0, part, :], grads_ref[0, part, :]], axis=0),
            proj_ref[...],
            preferred_element_type=F32,
        )
        out_ref[...] = jnp.where(column < rank, term[0:rows], term[rows:])


def count_kernel(picks_ref, out_ref):
    tokens, width = out_ref.shape
    samples = picks_ref.shape[1]
    token = lax.broadcasted_iota(jnp.int32, (tokens, samples), 0)
    hits = jnp.where(token == picks_ref[...], 1.0, 0.0).astype(BF16)
    out_ref[...] = jnp.dot(hits, jnp.ones((samples, width), BF16), preferred_element_type=F32)


def sketch_kernel(rank, count_ref, *refs):
    parts, (out_ref, held) = refs[:-2], refs[-2:]
    chunks = len(parts) // 2
    total = jnp.concatenate([parts[i][...] + parts[chunks + i][...] for i in range(chunks)], axis=0)
    held[...] = lax.dot_general(
        total[:, rank : 2 * rank],
        total[:, 0:rank] * count_ref[...],
        (((0,), (0,)), ((), ())),
        precision=lax.Precision.HIGHEST,
        preferred_element_type=F32,
    )
    pairs = out_ref.shape[0]
    even = held[pl.ds(0, pairs, stride=2), :]
    odd = held[pl.ds(1, pairs, stride=2), :]
    out_ref[...] = jnp.concatenate([even, odd], axis=1).astype(BF16)


def flatten_kernel(mates, own_ref, far_ref, first_ref, second_ref, wide):
    pairs = own_ref.shape[0]
    slots = first_ref.shape[0]
    core = lax.axis_index("tensor")
    wide[...] = jnp.zeros_like(wide)
    sketch = jnp.where(lax.axis_index("dp") // mates == core, far_ref[...], own_ref[...])
    wide[pl.ds(0, pairs, stride=slots), :] = sketch.astype(F32)
    for out_ref, half in ((first_ref, core), (second_ref, 1 - core)):
        start = half * (slots * pairs // 2)
        for j in range(pairs // 2):
            rows = wide[pl.ds(pl.multiple_of(start + j * slots, slots), slots), :]
            out_ref[:, j * LANES : (j + 1) * LANES] = rows.astype(BF16)


def score_kernel(mates, first_ref, second_ref, *refs):
    queries, out_ref = refs[:-1], refs[-1]
    own_queries = queries[0].shape[0]
    flats = (first_ref[...], second_ref[...])
    scores = sum(
        lax.dot_general(
            flat,
            jnp.concatenate([queries[2 * r + i][...] for r in range(mates)], axis=0),
            (((1,), (1,)), ((), ())),
            preferred_element_type=F32,
        )
        for i, flat in enumerate(flats)
    )
    member = lax.rem(lax.axis_index("dp"), mates)
    width = scores.shape[1]
    block = lax.broadcasted_iota(jnp.int32, scores.shape, 1) // own_queries
    step = 1
    while step < mates:
        up = pltpu.roll(scores, step * own_queries, 1)
        down = pltpu.roll(scores, width - step * own_queries, 1)
        swapped = jnp.where(block & step == 0, down, up)
        scores = jnp.where(member & step == 0, scores, swapped)
        step *= 2
    out_ref[...] = scores[0:1, :]


def on_device(activations, out_grads, projections, sample_index, queries):
    clips = lax.axis_size("dp")
    tokens, units = activations.shape[1:]
    rank = projections.shape[1] // 2
    own_queries, entries = queries.shape
    pairs = 2 * entries // LANES
    mates = clips // 2
    slots = 8
    vmem = pl.BlockSpec(memory_space=pltpu.VMEM)
    swap = [(0, 1), (1, 0)]
    both = ("dp", "tensor")

    def place(a, m, t):
        return (a * mates + m) * 2 + t

    spots = [(a, m) for a in range(2) for m in range(mates)]
    there = [(place(a, m, 1 - a), place(1 - a, m, 1 - a)) for a, m in spots]
    there += [(place(a, m, a), place(a, m, 1 - a)) for a, m in spots]
    back = [(dst, src) for src, dst in there]

    first = pl.pallas_call(
        first_kernel,
        out_specs=vmem,
        out_shape=jax.ShapeDtypeStruct((8, LANES), F32),
        compiler_params=pltpu.CompilerParams(vmem_limit_bytes=1 << 20),
        cost_estimate=pl.CostEstimate(flops=1 << 32, bytes_accessed=1, transcendentals=0),
        name="first",
    )()
    queries, first = lax.optimization_barrier((queries, first))
    halves = [queries]
    for r in range(1, mates):
        halves.append(lax.ppermute(queries, "dp", [(d, d ^ r) for d in range(clips)]))
    partial = pl.pallas_call(
        functools.partial(project_kernel, rank),
        in_specs=[vmem] * 4,
        out_specs=[vmem] * PIECES,
        out_shape=[jax.ShapeDtypeStruct((tokens // PIECES, 2 * rank), F32)] * PIECES,
        compiler_params=pltpu.CompilerParams(vmem_limit_bytes=16 << 20),
        cost_estimate=pl.CostEstimate(
            flops=8 * tokens * units * rank, bytes_accessed=4 * tokens * units, transcendentals=0
        ),
        name="project",
    )(first, activations, out_grads, projections)

    other = [lax.ppermute(part, "tensor", swap) for part in partial]
    count = pl.pallas_call(
        count_kernel,
        in_specs=[vmem],
        out_specs=vmem,
        out_shape=jax.ShapeDtypeStruct((tokens, rank), F32),
        compiler_params=pltpu.CompilerParams(vmem_limit_bytes=8 << 20),
        cost_estimate=pl.CostEstimate(flops=1, bytes_accessed=1, transcendentals=0),
        name="count",
    )(sample_index)
    sketch = pl.pallas_call(
        functools.partial(sketch_kernel, rank),
        in_specs=[vmem] * (1 + 2 * len(partial)),
        out_specs=vmem,
        out_shape=jax.ShapeDtypeStruct((pairs, LANES), BF16),
        scratch_shapes=[pltpu.VMEM((rank, rank), F32)],
        compiler_params=pltpu.CompilerParams(vmem_limit_bytes=8 << 20),
        cost_estimate=pl.CostEstimate(flops=1, bytes_accessed=1, transcendentals=0),
        name="sketch",
    )(count, *partial, *other)

    far_sketch = lax.ppermute(sketch, both, there)
    halves, sketch = lax.optimization_barrier((halves, sketch))
    taken = []
    for half in halves:
        taken += [half, lax.ppermute(half, "tensor", swap)]
    width = mates * own_queries
    flats = pl.pallas_call(
        functools.partial(flatten_kernel, mates),
        in_specs=[vmem] * 2,
        out_specs=[vmem] * 2,
        out_shape=[jax.ShapeDtypeStruct((slots, entries), BF16)] * 2,
        scratch_shapes=[pltpu.VMEM((pairs * slots, LANES), F32)],
        compiler_params=pltpu.CompilerParams(vmem_limit_bytes=8 << 20),
        cost_estimate=pl.CostEstimate(flops=1 << 34, bytes_accessed=64 << 20, transcendentals=0),
        name="flatten",
    )(sketch, far_sketch)
    scores = pl.pallas_call(
        functools.partial(score_kernel, mates),
        in_specs=[vmem] * (2 * mates + 2),
        out_specs=vmem,
        out_shape=jax.ShapeDtypeStruct((1, width), F32),
        compiler_params=pltpu.CompilerParams(vmem_limit_bytes=(16 + mates // 2) << 20),
        name="score",
    )(*flats, *taken)
    return lax.ppermute(scores, both, back)


def solution(mesh):
    in_specs = (
        P(("groups", "dp"), None, "tensor"),
        P(("groups", "dp"), None, "tensor"),
        P("tensor", None),
        P(("groups", "dp"), None),
        P(("groups", "dp"), "tensor"),
    )
    out_specs = P(("groups", "dp"), "tensor")
    return jax.shard_map(
        on_device, mesh=mesh, in_specs=in_specs, out_specs=out_specs, check_vma=False
    )
```

```python
import functools

import jax
import jax.numpy as jnp
from jax import lax
from jax.experimental import pallas as pl
from jax.experimental.pallas import tpu as pltpu
from jax.sharding import PartitionSpec as P

F32 = jnp.float32
BF16 = jnp.bfloat16
LANES = 128
PIECES = 2


def first_kernel(out_ref):
    out_ref[...] = jnp.zeros_like(out_ref)


def project_kernel(rank, first_ref, ready_ref, acts_ref, grads_ref, proj_ref, *outs):
    rows = outs[0].shape[0]
    column = lax.broadcasted_iota(jnp.int32, (rows, 2 * rank), 1)
    for i, out_ref in enumerate(outs):
        part = slice(i * rows, (i + 1) * rows)
        term = jnp.dot(
            jnp.concatenate([acts_ref[0, part, :], grads_ref[0, part, :]], axis=0),
            proj_ref[...],
            preferred_element_type=F32,
        )
        out_ref[...] = jnp.where(column < rank, term[0:rows], term[rows:])


def count_kernel(rank, picks_ref, out_ref):
    tokens, width = out_ref.shape
    samples = picks_ref.shape[1]
    token = lax.broadcasted_iota(jnp.int32, (tokens, samples), 0)
    hits = jnp.where(token == picks_ref[...], 1.0, 0.0).astype(BF16)
    count = jnp.dot(hits, jnp.ones((samples, width), BF16), preferred_element_type=F32)
    column = lax.broadcasted_iota(jnp.int32, (tokens, width), 1)
    out_ref[...] = jnp.where(column < rank, count, 1.0)


def sketch_kernel(rank, count_ref, *refs):
    parts, (out_ref, held) = refs[:-2], refs[-2:]
    chunks = len(parts) // 2
    total = jnp.concatenate([parts[i][...] + parts[chunks + i][...] for i in range(chunks)], axis=0)
    total = total * count_ref[...]
    high = total.astype(BF16)
    low = (total - high.astype(F32)).astype(BF16)
    gram = lax.dot_general(
        jnp.concatenate([high, high, low], axis=0),
        jnp.concatenate([high, low, high], axis=0),
        (((0,), (0,)), ((), ())),
        preferred_element_type=F32,
    )
    held[...] = gram[rank : 2 * rank, 0:rank]
    pairs = out_ref.shape[0]
    even = held[pl.ds(0, pairs, stride=2), :]
    odd = held[pl.ds(1, pairs, stride=2), :]
    out_ref[...] = jnp.concatenate([even, odd], axis=1).astype(BF16)


def flatten_kernel(mates, own_ref, far_ref, first_ref, second_ref, wide):
    pairs = own_ref.shape[0]
    slots = first_ref.shape[0]
    core = lax.axis_index("tensor")
    wide[...] = jnp.zeros_like(wide)
    sketch = jnp.where(lax.axis_index("dp") // mates == core, far_ref[...], own_ref[...])
    wide[pl.ds(0, pairs, stride=slots), :] = sketch.astype(F32)
    for out_ref, half in ((first_ref, core), (second_ref, 1 - core)):
        start = half * (slots * pairs // 2)
        for j in range(pairs // 2):
            rows = wide[pl.ds(pl.multiple_of(start + j * slots, slots), slots), :]
            out_ref[:, j * LANES : (j + 1) * LANES] = rows.astype(BF16)


def score_kernel(mates, first_ref, second_ref, *refs):
    queries, out_ref = refs[:-1], refs[-1]
    own_queries = queries[0].shape[0]
    scores = sum(
        lax.dot_general(
            jnp.concatenate([queries[2 * r + i][...] for r in range(mates)], axis=0),
            flat_ref[...],
            (((1,), (1,)), ((), ())),
            preferred_element_type=F32,
        )
        for i, flat_ref in enumerate((first_ref, second_ref))
    ).T
    member = lax.rem(lax.axis_index("dp"), mates)
    width = scores.shape[1]
    block = lax.broadcasted_iota(jnp.int32, scores.shape, 1) // own_queries
    step = 1
    while step < mates:
        up = pltpu.roll(scores, step * own_queries, 1)
        down = pltpu.roll(scores, width - step * own_queries, 1)
        swapped = jnp.where(block & step == 0, down, up)
        scores = jnp.where(member & step == 0, scores, swapped)
        step *= 2
    out_ref[...] = scores[0:1, :]


def on_device(activations, out_grads, projections, sample_index, queries):
    clips = lax.axis_size("dp")
    tokens, units = activations.shape[1:]
    rank = projections.shape[1] // 2
    own_queries, entries = queries.shape
    pairs = 2 * entries // LANES
    mates = clips // 2
    slots = 8
    vmem = pl.BlockSpec(memory_space=pltpu.VMEM)
    swap = [(0, 1), (1, 0)]
    both = ("dp", "tensor")

    def place(a, m, t):
        return (a * mates + m) * 2 + t

    spots = [(a, m) for a in range(2) for m in range(mates)]
    there = [(place(a, m, 1 - a), place(1 - a, m, 1 - a)) for a, m in spots]
    there += [(place(a, m, a), place(a, m, 1 - a)) for a, m in spots]
    back = [(dst, src) for src, dst in there]

    first = pl.pallas_call(
        first_kernel,
        out_specs=vmem,
        out_shape=jax.ShapeDtypeStruct((8, LANES), F32),
        compiler_params=pltpu.CompilerParams(vmem_limit_bytes=1 << 20),
        cost_estimate=pl.CostEstimate(flops=1 << 30, bytes_accessed=1, transcendentals=0),
        name="first",
    )()
    sent, first = lax.optimization_barrier((queries, first))
    own_swapped = lax.ppermute(sent, "tensor", swap)
    halves = [queries]
    for r in range(1, mates):
        halves.append(lax.ppermute(sent, "dp", [(d, d ^ r) for d in range(clips)]))
    partial = pl.pallas_call(
        functools.partial(project_kernel, rank),
        in_specs=[vmem] * 5,
        out_specs=[vmem] * PIECES,
        out_shape=[jax.ShapeDtypeStruct((tokens // PIECES, 2 * rank), F32)] * PIECES,
        compiler_params=pltpu.CompilerParams(vmem_limit_bytes=16 << 20),
        cost_estimate=pl.CostEstimate(
            flops=8 * tokens * units * rank, bytes_accessed=4 * tokens * units, transcendentals=0
        ),
        name="project",
    )(first, own_swapped, activations, out_grads, projections)

    other = [lax.ppermute(part, "tensor", swap) for part in partial]
    count = pl.pallas_call(
        functools.partial(count_kernel, rank),
        in_specs=[vmem],
        out_specs=vmem,
        out_shape=jax.ShapeDtypeStruct((tokens, 2 * rank), F32),
        compiler_params=pltpu.CompilerParams(vmem_limit_bytes=8 << 20),
        cost_estimate=pl.CostEstimate(flops=1, bytes_accessed=1, transcendentals=0),
        name="count",
    )(sample_index)
    sketch = pl.pallas_call(
        functools.partial(sketch_kernel, rank),
        in_specs=[vmem] * (1 + 2 * len(partial)),
        out_specs=vmem,
        out_shape=jax.ShapeDtypeStruct((pairs, LANES), BF16),
        scratch_shapes=[pltpu.VMEM((rank, rank), F32)],
        compiler_params=pltpu.CompilerParams(vmem_limit_bytes=8 << 20),
        cost_estimate=pl.CostEstimate(flops=1, bytes_accessed=1, transcendentals=0),
        name="sketch",
    )(count, *partial, *other)

    far_sketch = lax.ppermute(sketch, both, there)
    taken = [queries, own_swapped]
    for half in halves[1:]:
        half, sketch = lax.optimization_barrier((half, sketch))
        taken += [half, lax.ppermute(half, "tensor", swap)]
    width = mates * own_queries
    flats = pl.pallas_call(
        functools.partial(flatten_kernel, mates),
        in_specs=[vmem] * 2,
        out_specs=[vmem] * 2,
        out_shape=[jax.ShapeDtypeStruct((slots, entries), BF16)] * 2,
        scratch_shapes=[pltpu.VMEM((pairs * slots, LANES), F32)],
        compiler_params=pltpu.CompilerParams(vmem_limit_bytes=8 << 20),
        cost_estimate=pl.CostEstimate(flops=1 << 34, bytes_accessed=64 << 20, transcendentals=0),
        name="flatten",
    )(sketch, far_sketch)
    scores = pl.pallas_call(
        functools.partial(score_kernel, mates),
        in_specs=[vmem] * (2 * mates + 2),
        out_specs=vmem,
        out_shape=jax.ShapeDtypeStruct((1, width), F32),
        compiler_params=pltpu.CompilerParams(vmem_limit_bytes=(16 + mates // 2) << 20),
        name="score",
    )(*flats, *taken)
    return lax.ppermute(scores, both, back)


def solution(mesh):
    in_specs = (
        P(("groups", "dp"), None, "tensor"),
        P(("groups", "dp"), None, "tensor"),
        P("tensor", None),
        P(("groups", "dp"), None),
        P(("groups", "dp"), "tensor"),
    )
    out_specs = P(("groups", "dp"), "tensor")
    return jax.shard_map(
        on_device, mesh=mesh, in_specs=in_specs, out_specs=out_specs, check_vma=False
    )
```

```python
import functools

import jax
import jax.numpy as jnp
from jax import lax
from jax.experimental import pallas as pl
from jax.experimental.pallas import tpu as pltpu
from jax.sharding import PartitionSpec as P

F32 = jnp.float32
BF16 = jnp.bfloat16
LANES = 128
PIECES = 2


def first_kernel(out_ref):
    out_ref[...] = jnp.zeros_like(out_ref)


def project_kernel(rank, first_ref, acts_ref, grads_ref, proj_ref, *outs):
    rows = outs[0].shape[0]
    column = lax.broadcasted_iota(jnp.int32, (rows, 2 * rank), 1)
    for i, out_ref in enumerate(outs):
        part = slice(i * rows, (i + 1) * rows)
        term = jnp.dot(
            jnp.concatenate([acts_ref[0, part, :], grads_ref[0, part, :]], axis=0),
            proj_ref[...],
            preferred_element_type=F32,
        )
        out_ref[...] = jnp.where(column < rank, term[0:rows], term[rows:])


def count_kernel(rank, picks_ref, out_ref):
    tokens, width = out_ref.shape
    samples = picks_ref.shape[1]
    token = lax.broadcasted_iota(jnp.int32, (tokens, samples), 0)
    hits = jnp.where(token == picks_ref[...], 1.0, 0.0).astype(BF16)
    count = jnp.dot(hits, jnp.ones((samples, width), BF16), preferred_element_type=F32)
    column = lax.broadcasted_iota(jnp.int32, (tokens, width), 1)
    out_ref[...] = jnp.where(column < rank, count, 1.0)


def sketch_kernel(rank, count_ref, *refs):
    parts, (out_ref, held) = refs[:-2], refs[-2:]
    chunks = len(parts) // 2
    total = jnp.concatenate([parts[i][...] + parts[chunks + i][...] for i in range(chunks)], axis=0)
    total = total * count_ref[...]
    high = total.astype(BF16)
    low = (total - high.astype(F32)).astype(BF16)
    gram = lax.dot_general(
        jnp.concatenate([high, high, low], axis=0),
        jnp.concatenate([high, low, high], axis=0),
        (((0,), (0,)), ((), ())),
        preferred_element_type=F32,
    )
    held[...] = gram[rank : 2 * rank, 0:rank]
    pairs = out_ref.shape[0]
    start = lax.axis_index("tensor") * (2 * pairs)
    even = held[pl.ds(start, pairs, stride=2), :]
    odd = held[pl.ds(start + 1, pairs, stride=2), :]
    out_ref[...] = jnp.concatenate([even, odd], axis=1).astype(BF16)


def mark_kernel(*refs):
    refs[-1][...] = jnp.zeros_like(refs[-1])


def flatten_kernel(mark_ref, own_ref, far_ref, out_ref, wide):
    pairs = own_ref.shape[0]
    slots = out_ref.shape[0]
    wide[...] = jnp.zeros_like(wide)
    wide[pl.ds(0, pairs, stride=slots), :] = own_ref[...].astype(F32)
    wide[pl.ds(1, pairs, stride=slots), :] = far_ref[...].astype(F32)
    for j in range(pairs):
        out_ref[:, j * LANES : (j + 1) * LANES] = wide[j * slots : (j + 1) * slots, :].astype(BF16)


def score_kernel(flat_ref, *refs):
    queries, (keep_ref, send_ref) = refs[:-2], refs[-2:]
    mates = len(queries)
    own_queries = queries[0].shape[0]
    scores = jnp.concatenate(
        [
            lax.dot_general(
                flat_ref[...], query[...], (((1,), (1,)), ((), ())), preferred_element_type=F32
            )
            for query in queries
        ],
        axis=1,
    )
    spot = lax.axis_index("dp")
    member = lax.rem(spot, mates)
    width = scores.shape[1]
    block = lax.broadcasted_iota(jnp.int32, scores.shape, 1) // own_queries
    step = 1
    while step < mates:
        up = pltpu.roll(scores, step * own_queries, 1)
        down = pltpu.roll(scores, width - step * own_queries, 1)
        swapped = jnp.where(block & step == 0, down, up)
        scores = jnp.where(member & step == 0, scores, swapped)
        step *= 2
    worker = spot // mates == lax.axis_index("tensor")
    own, far = scores[0:1, :], scores[1:2, :]
    keep_ref[...] = jnp.where(worker, far, own)
    send_ref[...] = jnp.where(worker, own, far)


def add_kernel(one_ref, other_ref, out_ref):
    out_ref[...] = one_ref[...] + other_ref[...]


def on_device(activations, out_grads, projections, sample_index, queries):
    clips = lax.axis_size("dp")
    tokens, units = activations.shape[1:]
    rank = projections.shape[1] // 2
    own_queries, entries = queries.shape
    pairs = entries // LANES
    mates = clips // 2
    slots = 8
    vmem = pl.BlockSpec(memory_space=pltpu.VMEM)
    swap = [(0, 1), (1, 0)]
    both = ("dp", "tensor")

    def place(a, m, t):
        return (a * mates + m) * 2 + t

    spots = [(a, m) for a in range(2) for m in range(mates)]
    back = [(place(a, m, a), place(1 - a, m, a)) for a, m in spots]
    back += [(place(a, m, 1 - a), place(a, m, a)) for a, m in spots]
    across = [(d, (d + mates) % clips) for d in range(clips)]
    small = pl.CostEstimate(flops=1, bytes_accessed=1, transcendentals=0)
    few = pltpu.CompilerParams(vmem_limit_bytes=8 << 20)

    first = pl.pallas_call(
        first_kernel,
        out_specs=vmem,
        out_shape=jax.ShapeDtypeStruct((8, LANES), F32),
        compiler_params=pltpu.CompilerParams(vmem_limit_bytes=1 << 20),
        cost_estimate=pl.CostEstimate(flops=1 << 30, bytes_accessed=1, transcendentals=0),
        name="first",
    )()
    sent, first = lax.optimization_barrier((queries, first))
    halves = [queries]
    for r in range(1, mates):
        halves.append(lax.ppermute(sent, "dp", [(d, d ^ r) for d in range(clips)]))
    partial = pl.pallas_call(
        functools.partial(project_kernel, rank),
        in_specs=[vmem] * 4,
        out_specs=[vmem] * PIECES,
        out_shape=[jax.ShapeDtypeStruct((tokens // PIECES, 2 * rank), F32)] * PIECES,
        compiler_params=pltpu.CompilerParams(vmem_limit_bytes=16 << 20),
        cost_estimate=pl.CostEstimate(
            flops=8 * tokens * units * rank, bytes_accessed=4 * tokens * units, transcendentals=0
        ),
        name="project",
    )(first, activations, out_grads, projections)

    other = [lax.ppermute(part, "tensor", swap) for part in partial]
    count = pl.pallas_call(
        functools.partial(count_kernel, rank),
        in_specs=[vmem],
        out_specs=vmem,
        out_shape=jax.ShapeDtypeStruct((tokens, 2 * rank), F32),
        compiler_params=pltpu.CompilerParams(vmem_limit_bytes=8 << 20),
        cost_estimate=pl.CostEstimate(flops=1, bytes_accessed=1, transcendentals=0),
        name="count",
    )(sample_index)
    sketch = pl.pallas_call(
        functools.partial(sketch_kernel, rank),
        in_specs=[vmem] * (1 + 2 * len(partial)),
        out_specs=vmem,
        out_shape=jax.ShapeDtypeStruct((pairs, LANES), BF16),
        scratch_shapes=[pltpu.VMEM((rank, rank), F32)],
        compiler_params=pltpu.CompilerParams(vmem_limit_bytes=8 << 20),
        cost_estimate=pl.CostEstimate(flops=1, bytes_accessed=1, transcendentals=0),
        name="sketch",
    )(count, *partial, *other)

    far_sketch = lax.ppermute(sketch, "dp", across)
    width = mates * own_queries
    mark = pl.pallas_call(
        mark_kernel,
        in_specs=[vmem] * mates,
        out_specs=vmem,
        out_shape=jax.ShapeDtypeStruct((8, LANES), F32),
        compiler_params=few,
        cost_estimate=pl.CostEstimate(flops=1 << 31, bytes_accessed=1, transcendentals=0),
        name="mark",
    )(sketch, *halves[1:])
    flat = pl.pallas_call(
        flatten_kernel,
        in_specs=[vmem] * 3,
        out_specs=vmem,
        out_shape=jax.ShapeDtypeStruct((slots, entries), BF16),
        scratch_shapes=[pltpu.VMEM((pairs * slots, LANES), F32)],
        compiler_params=few,
        cost_estimate=small,
        name="flatten",
    )(mark, sketch, far_sketch)
    row = jax.ShapeDtypeStruct((1, width), F32)
    keep, send = pl.pallas_call(
        score_kernel,
        in_specs=[vmem] * (1 + mates),
        out_specs=[vmem] * 2,
        out_shape=[row] * 2,
        compiler_params=pltpu.CompilerParams(vmem_limit_bytes=(8 + mates // 4) << 20),
        cost_estimate=small,
        name="score",
    )(flat, *halves)
    scores = pl.pallas_call(
        add_kernel,
        in_specs=[vmem] * 2,
        out_specs=vmem,
        out_shape=row,
        compiler_params=few,
        cost_estimate=small,
        name="add",
    )(keep, lax.ppermute(send, "tensor", swap))
    return lax.ppermute(scores, both, back)


def solution(mesh):
    in_specs = (
        P(("groups", "dp"), None, "tensor"),
        P(("groups", "dp"), None, "tensor"),
        P("tensor", None),
        P(("groups", "dp"), None),
        P(("groups", "dp"), "tensor"),
    )
    out_specs = P(("groups", "dp"), "tensor")
    return jax.shard_map(
        on_device, mesh=mesh, in_specs=in_specs, out_specs=out_specs, check_vma=False
    )
```

```python
import functools

import jax
import jax.numpy as jnp
from jax import lax
from jax.experimental import pallas as pl
from jax.experimental.pallas import tpu as pltpu
from jax.sharding import PartitionSpec as P

F32 = jnp.float32
BF16 = jnp.bfloat16
LANES = 128
PIECES = 2


def first_kernel(out_ref):
    out_ref[...] = jnp.zeros_like(out_ref)


def project_kernel(rank, first_ref, acts_ref, grads_ref, proj_ref, *outs):
    rows = outs[0].shape[0]
    column = lax.broadcasted_iota(jnp.int32, (rows, 2 * rank), 1)
    for i, out_ref in enumerate(outs):
        part = slice(i * rows, (i + 1) * rows)
        term = jnp.dot(
            jnp.concatenate([acts_ref[0, part, :], grads_ref[0, part, :]], axis=0),
            proj_ref[...],
            preferred_element_type=F32,
        )
        out_ref[...] = jnp.where(column < rank, term[0:rows], term[rows:])


def count_kernel(rank, picks_ref, out_ref):
    tokens, width = out_ref.shape
    samples = picks_ref.shape[1]
    token = lax.broadcasted_iota(jnp.int32, (tokens, samples), 0)
    hits = jnp.where(token == picks_ref[...], 1.0, 0.0).astype(BF16)
    count = jnp.dot(hits, jnp.ones((samples, width), BF16), preferred_element_type=F32)
    column = lax.broadcasted_iota(jnp.int32, (tokens, width), 1)
    out_ref[...] = jnp.where(column < rank, count, 1.0)


def sketch_kernel(rank, count_ref, *refs):
    parts, (out_ref, held) = refs[:-2], refs[-2:]
    chunks = len(parts) // 2
    total = jnp.concatenate([parts[i][...] + parts[chunks + i][...] for i in range(chunks)], axis=0)
    total = total * count_ref[...]
    high = total.astype(BF16)
    low = (total - high.astype(F32)).astype(BF16)
    gram = lax.dot_general(
        jnp.concatenate([high, high, low], axis=0),
        jnp.concatenate([high, low, high], axis=0),
        (((0,), (0,)), ((), ())),
        preferred_element_type=F32,
    )
    held[...] = gram[rank : 2 * rank, 0:rank]
    pairs = out_ref.shape[0]
    even = held[pl.ds(0, pairs, stride=2), :]
    odd = held[pl.ds(1, pairs, stride=2), :]
    out_ref[...] = jnp.concatenate([even, odd], axis=1).astype(BF16)


def flatten_kernel(mates, own_ref, far_ref, first_ref, second_ref, wide):
    pairs = own_ref.shape[0]
    slots = first_ref.shape[0]
    core = lax.axis_index("tensor")
    wide[...] = jnp.zeros_like(wide)
    sketch = jnp.where(lax.axis_index("dp") // mates == core, far_ref[...], own_ref[...])
    wide[pl.ds(0, pairs, stride=slots), :] = sketch.astype(F32)
    for out_ref, half in ((first_ref, core), (second_ref, 1 - core)):
        start = half * (slots * pairs // 2)
        for j in range(pairs // 2):
            rows = wide[pl.ds(pl.multiple_of(start + j * slots, slots), slots), :]
            out_ref[:, j * LANES : (j + 1) * LANES] = rows.astype(BF16)


def score_kernel(first_ref, second_ref, own_ref, other_ref, out_ref):
    contract = (((1,), (1,)), ((), ()))
    out_ref[...] = lax.dot_general(
        first_ref[...], own_ref[...], contract, preferred_element_type=F32
    ) + lax.dot_general(second_ref[...], other_ref[...], contract, preferred_element_type=F32)


def arrange_kernel(*refs):
    parts, out_ref = refs[:-1], refs[-1]
    mates = len(parts)
    own_queries = parts[0].shape[1]
    scores = jnp.concatenate([part[...] for part in parts], axis=1)
    member = lax.rem(lax.axis_index("dp"), mates)
    width = scores.shape[1]
    block = lax.broadcasted_iota(jnp.int32, scores.shape, 1) // own_queries
    step = 1
    while step < mates:
        up = pltpu.roll(scores, step * own_queries, 1)
        down = pltpu.roll(scores, width - step * own_queries, 1)
        exchanged = jnp.where(block & step == 0, down, up)
        scores = jnp.where(member & step == 0, scores, exchanged)
        step *= 2
    out_ref[...] = scores[0:1, :]


def store_kernel(row_ref, out_ref, sem):
    copy = pltpu.make_async_copy(row_ref, out_ref, sem)
    copy.start()
    copy.wait()


def on_device(activations, out_grads, projections, sample_index, queries):
    clips = lax.axis_size("dp")
    tokens, units = activations.shape[1:]
    rank = projections.shape[1] // 2
    own_queries, entries = queries.shape
    pairs = 2 * entries // LANES
    mates = clips // 2
    slots = 8
    vmem = pl.BlockSpec(memory_space=pltpu.VMEM)
    swap = [(0, 1), (1, 0)]
    both = ("dp", "tensor")

    def place(a, m, t):
        return (a * mates + m) * 2 + t

    spots = [(a, m) for a in range(2) for m in range(mates)]
    there = [(place(a, m, 1 - a), place(1 - a, m, 1 - a)) for a, m in spots]
    there += [(place(a, m, a), place(a, m, 1 - a)) for a, m in spots]
    back = [(dst, src) for src, dst in there]

    first = pl.pallas_call(
        first_kernel,
        out_specs=vmem,
        out_shape=jax.ShapeDtypeStruct((8, LANES), F32),
        compiler_params=pltpu.CompilerParams(vmem_limit_bytes=1 << 20),
        cost_estimate=pl.CostEstimate(flops=1 << 30, bytes_accessed=1, transcendentals=0),
        name="first",
    )()
    sent, first = lax.optimization_barrier((queries, first))
    halves = [queries]
    for r in range(1, mates):
        halves.append(lax.ppermute(sent, "dp", [(d, d ^ r) for d in range(clips)]))
    partial = pl.pallas_call(
        functools.partial(project_kernel, rank),
        in_specs=[vmem] * 4,
        out_specs=[vmem] * PIECES,
        out_shape=[jax.ShapeDtypeStruct((tokens // PIECES, 2 * rank), F32)] * PIECES,
        compiler_params=pltpu.CompilerParams(vmem_limit_bytes=16 << 20),
        cost_estimate=pl.CostEstimate(
            flops=8 * tokens * units * rank, bytes_accessed=4 * tokens * units, transcendentals=0
        ),
        name="project",
    )(first, activations, out_grads, projections)

    other = [lax.ppermute(part, "tensor", swap) for part in partial]
    count = pl.pallas_call(
        functools.partial(count_kernel, rank),
        in_specs=[vmem],
        out_specs=vmem,
        out_shape=jax.ShapeDtypeStruct((tokens, 2 * rank), F32),
        compiler_params=pltpu.CompilerParams(vmem_limit_bytes=8 << 20),
        cost_estimate=pl.CostEstimate(flops=1, bytes_accessed=1, transcendentals=0),
        name="count",
    )(sample_index)
    sketch = pl.pallas_call(
        functools.partial(sketch_kernel, rank),
        in_specs=[vmem] * (1 + 2 * len(partial)),
        out_specs=vmem,
        out_shape=jax.ShapeDtypeStruct((pairs, LANES), BF16),
        scratch_shapes=[pltpu.VMEM((rank, rank), F32)],
        compiler_params=pltpu.CompilerParams(vmem_limit_bytes=8 << 20),
        cost_estimate=pl.CostEstimate(flops=1, bytes_accessed=1, transcendentals=0),
        name="sketch",
    )(count, *partial, *other)

    far_sketch = lax.ppermute(sketch, both, there)
    swapped = []
    for half in halves:
        half, sketch = lax.optimization_barrier((half, sketch))
        swapped.append(lax.ppermute(half, "tensor", swap))

    width = mates * own_queries
    flats = pl.pallas_call(
        functools.partial(flatten_kernel, mates),
        in_specs=[vmem] * 2,
        out_specs=[vmem] * 2,
        out_shape=[jax.ShapeDtypeStruct((slots, entries), BF16)] * 2,
        scratch_shapes=[pltpu.VMEM((pairs * slots, LANES), F32)],
        compiler_params=pltpu.CompilerParams(vmem_limit_bytes=8 << 20),
        cost_estimate=pl.CostEstimate(flops=1 << 34, bytes_accessed=64 << 20, transcendentals=0),
        name="flatten",
    )(sketch, far_sketch)
    small = pl.CostEstimate(flops=1, bytes_accessed=1, transcendentals=0)
    few = pltpu.CompilerParams(vmem_limit_bytes=8 << 20)
    parts = [
        pl.pallas_call(
            score_kernel,
            in_specs=[vmem] * 4,
            out_specs=vmem,
            out_shape=jax.ShapeDtypeStruct((slots, own_queries), F32),
            compiler_params=few,
            cost_estimate=small,
            name="score",
        )(*flats, half, other)
        for half, other in zip(halves, swapped)
    ]
    scores = pl.pallas_call(
        arrange_kernel,
        in_specs=[vmem] * mates,
        out_specs=vmem,
        out_shape=jax.ShapeDtypeStruct((1, width), F32),
        compiler_params=few,
        cost_estimate=small,
        name="arrange",
    )(*parts)
    return pl.pallas_call(
        store_kernel,
        in_specs=[vmem],
        out_specs=pl.BlockSpec(memory_space=pl.ANY),
        out_shape=jax.ShapeDtypeStruct((1, width), F32),
        scratch_shapes=[pltpu.SemaphoreType.DMA],
        compiler_params=few,
        name="store",
    )(lax.ppermute(scores, both, back))


def solution(mesh):
    in_specs = (
        P(("groups", "dp"), None, "tensor"),
        P(("groups", "dp"), None, "tensor"),
        P("tensor", None),
        P(("groups", "dp"), None),
        P(("groups", "dp"), "tensor"),
    )
    out_specs = P(("groups", "dp"), "tensor")
    return jax.shard_map(
        on_device, mesh=mesh, in_specs=in_specs, out_specs=out_specs, check_vma=False
    )
```

```python
import functools

import jax
import jax.numpy as jnp
from jax import lax
from jax.experimental import pallas as pl
from jax.experimental.pallas import tpu as pltpu
from jax.sharding import PartitionSpec as P

F32 = jnp.float32
BF16 = jnp.bfloat16
LANES = 128
PIECES = 2


def first_kernel(out_ref):
    out_ref[...] = jnp.zeros_like(out_ref)


def project_kernel(rank, first_ref, acts_ref, grads_hbm, proj_ref, *refs):
    outs, (grads, sems) = refs[:-2], refs[-2:]
    rows = outs[0].shape[0]
    copies = []
    for i in range(len(outs)):
        part = pl.ds(i * rows, rows)
        copies.append(pltpu.make_async_copy(grads_hbm.at[0, part, :], grads.at[part, :], sems.at[i]))
        copies[-1].start()
    left = jnp.dot(acts_ref[0], proj_ref[...], preferred_element_type=F32)
    column = lax.broadcasted_iota(jnp.int32, (rows, 2 * rank), 1)
    for i, out_ref in enumerate(outs):
        part = slice(i * rows, (i + 1) * rows)
        copies[i].wait()
        right = jnp.dot(grads[part, :], proj_ref[...], preferred_element_type=F32)
        out_ref[...] = jnp.where(column < rank, left[part], right)


def count_kernel(rank, picks_ref, out_ref):
    tokens, width = out_ref.shape
    samples = picks_ref.shape[1]
    token = lax.broadcasted_iota(jnp.int32, (tokens, samples), 0)
    hits = jnp.where(token == picks_ref[...], 1.0, 0.0).astype(BF16)
    count = jnp.dot(hits, jnp.ones((samples, width), BF16), preferred_element_type=F32)
    column = lax.broadcasted_iota(jnp.int32, (tokens, width), 1)
    out_ref[...] = jnp.where(column < rank, count, 1.0)


def sketch_kernel(rank, count_ref, *refs):
    parts, (out_ref, held) = refs[:-2], refs[-2:]
    chunks = len(parts) // 2
    total = jnp.concatenate([parts[i][...] + parts[chunks + i][...] for i in range(chunks)], axis=0)
    total = total * count_ref[...]
    high = total.astype(BF16)
    low = (total - high.astype(F32)).astype(BF16)
    gram = lax.dot_general(
        jnp.concatenate([high, high, low], axis=0),
        jnp.concatenate([high, low, high], axis=0),
        (((0,), (0,)), ((), ())),
        preferred_element_type=F32,
    )
    held[...] = gram[rank : 2 * rank, 0:rank]
    pairs = out_ref.shape[0]
    even = held[pl.ds(0, pairs, stride=2), :]
    odd = held[pl.ds(1, pairs, stride=2), :]
    out_ref[...] = jnp.concatenate([even, odd], axis=1).astype(BF16)


def flatten_kernel(mates, own_ref, far_ref, first_ref, second_ref, wide):
    pairs = own_ref.shape[0]
    slots = first_ref.shape[0]
    core = lax.axis_index("tensor")
    wide[...] = jnp.zeros_like(wide)
    sketch = jnp.where(lax.axis_index("dp") // mates == core, far_ref[...], own_ref[...])
    wide[pl.ds(0, pairs, stride=slots), :] = sketch.astype(F32)
    for out_ref, half in ((first_ref, core), (second_ref, 1 - core)):
        start = half * (slots * pairs // 2)
        for j in range(pairs // 2):
            rows = wide[pl.ds(pl.multiple_of(start + j * slots, slots), slots), :]
            out_ref[:, j * LANES : (j + 1) * LANES] = rows


def score_kernel(mates, first_ref, second_ref, *refs):
    queries, out_ref = refs[:-1], refs[-1]
    own_queries, entries = queries[0].shape
    parts = []
    for r in range(mates):
        part = jnp.zeros((own_queries, LANES), F32)
        for flat_ref, query_ref in ((first_ref, queries[2 * r]), (second_ref, queries[2 * r + 1])):
            for j in range(entries // LANES):
                lanes = slice(j * LANES, (j + 1) * LANES)
                part += query_ref[:, lanes].astype(F32) * flat_ref[0:1, lanes]
        parts.append(part)
    width = mates * own_queries
    scores = jnp.sum(jnp.concatenate(parts, axis=0).T, axis=0, keepdims=True)
    scores = jnp.broadcast_to(scores, (8, width))
    member = lax.rem(lax.axis_index("dp"), mates)
    block = lax.broadcasted_iota(jnp.int32, scores.shape, 1) // own_queries
    step = 1
    while step < mates:
        up = pltpu.roll(scores, step * own_queries, 1)
        down = pltpu.roll(scores, width - step * own_queries, 1)
        exchanged = jnp.where(block & step == 0, down, up)
        scores = jnp.where(member & step == 0, scores, exchanged)
        step *= 2
    out_ref[...] = scores[0:1, :]


def on_device(activations, out_grads, projections, sample_index, queries):
    clips = lax.axis_size("dp")
    tokens, units = activations.shape[1:]
    rank = projections.shape[1] // 2
    own_queries, entries = queries.shape
    pairs = 2 * entries // LANES
    mates = clips // 2
    slots = 8
    vmem = pl.BlockSpec(memory_space=pltpu.VMEM)
    swap = [(0, 1), (1, 0)]
    both = ("dp", "tensor")

    def place(a, m, t):
        return (a * mates + m) * 2 + t

    spots = [(a, m) for a in range(2) for m in range(mates)]
    there = [(place(a, m, 1 - a), place(1 - a, m, 1 - a)) for a, m in spots]
    there += [(place(a, m, a), place(a, m, 1 - a)) for a, m in spots]
    back = [(dst, src) for src, dst in there]

    first = pl.pallas_call(
        first_kernel,
        out_specs=vmem,
        out_shape=jax.ShapeDtypeStruct((8, LANES), F32),
        compiler_params=pltpu.CompilerParams(vmem_limit_bytes=1 << 20),
        cost_estimate=pl.CostEstimate(flops=11 << 26, bytes_accessed=1, transcendentals=0),
        name="first",
    )()
    sent, first = lax.optimization_barrier((queries, first))
    halves = [queries]
    for r in range(1, mates):
        halves.append(lax.ppermute(sent, "dp", [(d, d ^ r) for d in range(clips)]))
    partial = pl.pallas_call(
        functools.partial(project_kernel, rank),
        in_specs=[vmem, vmem, pl.BlockSpec(memory_space=pl.ANY), vmem],
        out_specs=[vmem] * PIECES,
        out_shape=[jax.ShapeDtypeStruct((tokens // PIECES, 2 * rank), F32)] * PIECES,
        scratch_shapes=[pltpu.VMEM((tokens, units), BF16), pltpu.SemaphoreType.DMA((PIECES,))],
        compiler_params=pltpu.CompilerParams(vmem_limit_bytes=52000 << 10),
        cost_estimate=pl.CostEstimate(
            flops=8 * tokens * units * rank, bytes_accessed=4 * tokens * units, transcendentals=0
        ),
        name="project",
    )(first, activations, out_grads, projections)

    other = [lax.ppermute(part, "tensor", swap) for part in partial]
    count = pl.pallas_call(
        functools.partial(count_kernel, rank),
        in_specs=[vmem],
        out_specs=vmem,
        out_shape=jax.ShapeDtypeStruct((tokens, 2 * rank), F32),
        compiler_params=pltpu.CompilerParams(vmem_limit_bytes=8 << 20),
        cost_estimate=pl.CostEstimate(flops=1, bytes_accessed=1, transcendentals=0),
        name="count",
    )(sample_index)
    sketch = pl.pallas_call(
        functools.partial(sketch_kernel, rank),
        in_specs=[vmem] * (1 + 2 * len(partial)),
        out_specs=vmem,
        out_shape=jax.ShapeDtypeStruct((pairs, LANES), BF16),
        scratch_shapes=[pltpu.VMEM((rank, rank), F32)],
        compiler_params=pltpu.CompilerParams(vmem_limit_bytes=8 << 20),
        cost_estimate=pl.CostEstimate(flops=1, bytes_accessed=1, transcendentals=0),
        name="sketch",
    )(count, *partial, *other)

    far_sketch = lax.ppermute(sketch, both, there)
    swapped = []
    for half in halves:
        half, sketch = lax.optimization_barrier((half, sketch))
        swapped.append(lax.ppermute(half, "tensor", swap))

    width = mates * own_queries
    flats = pl.pallas_call(
        functools.partial(flatten_kernel, mates),
        in_specs=[vmem] * 2,
        out_specs=[vmem] * 2,
        out_shape=[jax.ShapeDtypeStruct((slots, entries), F32)] * 2,
        scratch_shapes=[pltpu.VMEM((pairs * slots, LANES), F32)],
        compiler_params=pltpu.CompilerParams(vmem_limit_bytes=8 << 20),
        cost_estimate=pl.CostEstimate(flops=1 << 34, bytes_accessed=64 << 20, transcendentals=0),
        name="flatten",
    )(sketch, far_sketch)
    taken = [x for pair in zip(halves, swapped) for x in pair]
    scores = pl.pallas_call(
        functools.partial(score_kernel, mates),
        in_specs=[vmem] * (2 * mates + 2),
        out_specs=vmem,
        out_shape=jax.ShapeDtypeStruct((1, width), F32),
        compiler_params=pltpu.CompilerParams(vmem_limit_bytes=(16 + mates // 2) << 20),
        name="score",
    )(*flats, *taken)
    return lax.ppermute(scores, both, back)


def solution(mesh):
    in_specs = (
        P(("groups", "dp"), None, "tensor"),
        P(("groups", "dp"), None, "tensor"),
        P("tensor", None),
        P(("groups", "dp"), None),
        P(("groups", "dp"), "tensor"),
    )
    out_specs = P(("groups", "dp"), "tensor")
    return jax.shard_map(
        on_device, mesh=mesh, in_specs=in_specs, out_specs=out_specs, check_vma=False
    )
```

```python
import functools

import jax
import jax.numpy as jnp
from jax import lax
from jax.experimental import pallas as pl
from jax.experimental.pallas import tpu as pltpu
from jax.sharding import PartitionSpec as P

F32 = jnp.float32
BF16 = jnp.bfloat16
LANES = 128
PIECES = 2


def first_kernel(out_ref):
    out_ref[...] = jnp.zeros_like(out_ref)


def project_kernel(rank, first_ref, acts_ref, grads_ref, proj_ref, *outs):
    rows = outs[0].shape[0]
    column = lax.broadcasted_iota(jnp.int32, (rows, 2 * rank), 1)
    for i, out_ref in enumerate(outs):
        part = slice(i * rows, (i + 1) * rows)
        term = jnp.dot(
            jnp.concatenate([acts_ref[0, part, :], grads_ref[0, part, :]], axis=0),
            proj_ref[...],
            preferred_element_type=F32,
        )
        out_ref[...] = jnp.where(column < rank, term[0:rows], term[rows:])


def count_kernel(rank, picks_ref, out_ref):
    tokens, width = out_ref.shape
    samples = picks_ref.shape[1]
    token = lax.broadcasted_iota(jnp.int32, (tokens, samples), 0)
    hits = jnp.where(token == picks_ref[...], 1.0, 0.0).astype(BF16)
    count = jnp.dot(hits, jnp.ones((samples, width), BF16), preferred_element_type=F32)
    column = lax.broadcasted_iota(jnp.int32, (tokens, width), 1)
    out_ref[...] = jnp.where(column < rank, count, 1.0)


def sketch_kernel(rank, count_ref, *refs):
    parts, (out_ref, held) = refs[:-2], refs[-2:]
    chunks = len(parts) // 2
    total = jnp.concatenate([parts[i][...] + parts[chunks + i][...] for i in range(chunks)], axis=0)
    total = total * count_ref[...]
    high = total.astype(BF16)
    low = (total - high.astype(F32)).astype(BF16)
    gram = lax.dot_general(
        jnp.concatenate([high, high, low], axis=0),
        jnp.concatenate([high, low, high], axis=0),
        (((0,), (0,)), ((), ())),
        preferred_element_type=F32,
    )
    held[...] = gram[rank : 2 * rank, 0:rank]
    pairs = out_ref.shape[0]
    even = held[pl.ds(0, pairs, stride=2), :]
    odd = held[pl.ds(1, pairs, stride=2), :]
    out_ref[...] = jnp.concatenate([even, odd], axis=1).astype(BF16)


def flatten_kernel(mates, own_ref, far_ref, first_ref, second_ref, wide):
    pairs = own_ref.shape[0]
    slots = first_ref.shape[0]
    core = lax.axis_index("tensor")
    wide[...] = jnp.zeros_like(wide)
    sketch = jnp.where(lax.axis_index("dp") // mates == core, far_ref[...], own_ref[...])
    wide[pl.ds(0, pairs, stride=slots), :] = sketch.astype(F32)
    for out_ref, half in ((first_ref, core), (second_ref, 1 - core)):
        start = half * (slots * pairs // 2)
        for j in range(pairs // 2):
            rows = wide[pl.ds(pl.multiple_of(start + j * slots, slots), slots), :]
            out_ref[:, j * LANES : (j + 1) * LANES] = rows


def score_kernel(mates, first_ref, second_ref, *refs):
    queries, out_ref = refs[:-1], refs[-1]
    own_queries, entries = queries[0].shape
    parts = []
    for r in range(mates):
        part = jnp.zeros((own_queries, LANES), F32)
        for flat_ref, query_ref in ((first_ref, queries[2 * r]), (second_ref, queries[2 * r + 1])):
            for j in range(entries // LANES):
                lanes = slice(j * LANES, (j + 1) * LANES)
                part += query_ref[:, lanes].astype(F32) * flat_ref[0:1, lanes]
        parts.append(part)
    width = mates * own_queries
    scores = jnp.sum(jnp.concatenate(parts, axis=0).T, axis=0, keepdims=True)
    scores = jnp.broadcast_to(scores, (8, width))
    member = lax.rem(lax.axis_index("dp"), mates)
    block = lax.broadcasted_iota(jnp.int32, scores.shape, 1) // own_queries
    step = 1
    while step < mates:
        up = pltpu.roll(scores, step * own_queries, 1)
        down = pltpu.roll(scores, width - step * own_queries, 1)
        exchanged = jnp.where(block & step == 0, down, up)
        scores = jnp.where(member & step == 0, scores, exchanged)
        step *= 2
    out_ref[...] = scores[0:1, :]


def on_device(activations, out_grads, projections, sample_index, queries):
    clips = lax.axis_size("dp")
    tokens, units = activations.shape[1:]
    rank = projections.shape[1] // 2
    own_queries, entries = queries.shape
    pairs = 2 * entries // LANES
    mates = clips // 2
    slots = 8
    vmem = pl.BlockSpec(memory_space=pltpu.VMEM)
    swap = [(0, 1), (1, 0)]
    both = ("dp", "tensor")

    def place(a, m, t):
        return (a * mates + m) * 2 + t

    spots = [(a, m) for a in range(2) for m in range(mates)]
    there = [(place(a, m, 1 - a), place(1 - a, m, 1 - a)) for a, m in spots]
    there += [(place(a, m, a), place(a, m, 1 - a)) for a, m in spots]
    back = [(dst, src) for src, dst in there]

    copied = 2 * (2 * tokens * units + units * 2 * rank)
    first = pl.pallas_call(
        first_kernel,
        out_specs=vmem,
        out_shape=jax.ShapeDtypeStruct((8, LANES), F32),
        compiler_params=pltpu.CompilerParams(vmem_limit_bytes=1 << 20),
        cost_estimate=pl.CostEstimate(flops=274 * copied, bytes_accessed=1, transcendentals=0),
        name="first",
    )()
    sent, first = lax.optimization_barrier((queries, first))
    halves = [queries]
    for r in range(1, mates):
        halves.append(lax.ppermute(sent, "dp", [(d, d ^ r) for d in range(clips)]))
    partial = pl.pallas_call(
        functools.partial(project_kernel, rank),
        in_specs=[vmem] * 4,
        out_specs=[vmem] * PIECES,
        out_shape=[jax.ShapeDtypeStruct((tokens // PIECES, 2 * rank), F32)] * PIECES,
        compiler_params=pltpu.CompilerParams(vmem_limit_bytes=16 << 20),
        cost_estimate=pl.CostEstimate(
            flops=8 * tokens * units * rank, bytes_accessed=4 * tokens * units, transcendentals=0
        ),
        name="project",
    )(first, activations, out_grads, projections)

    other = [lax.ppermute(part, "tensor", swap) for part in partial]
    count = pl.pallas_call(
        functools.partial(count_kernel, rank),
        in_specs=[vmem],
        out_specs=vmem,
        out_shape=jax.ShapeDtypeStruct((tokens, 2 * rank), F32),
        compiler_params=pltpu.CompilerParams(vmem_limit_bytes=8 << 20),
        cost_estimate=pl.CostEstimate(flops=1, bytes_accessed=1, transcendentals=0),
        name="count",
    )(sample_index)
    sketch = pl.pallas_call(
        functools.partial(sketch_kernel, rank),
        in_specs=[vmem] * (1 + 2 * len(partial)),
        out_specs=vmem,
        out_shape=jax.ShapeDtypeStruct((pairs, LANES), BF16),
        scratch_shapes=[pltpu.VMEM((rank, rank), F32)],
        compiler_params=pltpu.CompilerParams(vmem_limit_bytes=8 << 20),
        cost_estimate=pl.CostEstimate(flops=1, bytes_accessed=1, transcendentals=0),
        name="sketch",
    )(count, *partial, *other)

    far_sketch = lax.ppermute(sketch, both, there)
    swapped = []
    for half in halves:
        half, sketch = lax.optimization_barrier((half, sketch))
        swapped.append(lax.ppermute(half, "tensor", swap))

    width = mates * own_queries
    flats = pl.pallas_call(
        functools.partial(flatten_kernel, mates),
        in_specs=[vmem] * 2,
        out_specs=[vmem] * 2,
        out_shape=[jax.ShapeDtypeStruct((slots, entries), F32)] * 2,
        scratch_shapes=[pltpu.VMEM((pairs * slots, LANES), F32)],
        compiler_params=pltpu.CompilerParams(vmem_limit_bytes=8 << 20),
        cost_estimate=pl.CostEstimate(flops=1 << 34, bytes_accessed=64 << 20, transcendentals=0),
        name="flatten",
    )(sketch, far_sketch)
    taken = [x for pair in zip(halves, swapped) for x in pair]
    scores = pl.pallas_call(
        functools.partial(score_kernel, mates),
        in_specs=[vmem] * (2 * mates + 2),
        out_specs=vmem,
        out_shape=jax.ShapeDtypeStruct((1, width), F32),
        compiler_params=pltpu.CompilerParams(vmem_limit_bytes=(16 + mates // 2) << 20),
        name="score",
    )(*flats, *taken)
    return lax.ppermute(scores, both, back)


def solution(mesh):
    in_specs = (
        P(("groups", "dp"), None, "tensor"),
        P(("groups", "dp"), None, "tensor"),
        P("tensor", None),
        P(("groups", "dp"), None),
        P(("groups", "dp"), "tensor"),
    )
    out_specs = P(("groups", "dp"), "tensor")
    return jax.shard_map(
        on_device, mesh=mesh, in_specs=in_specs, out_specs=out_specs, check_vma=False
    )
```

```python
import functools

import jax
import jax.numpy as jnp
from jax import lax
from jax.experimental import pallas as pl
from jax.experimental.pallas import tpu as pltpu
from jax.sharding import PartitionSpec as P

F32 = jnp.float32
BF16 = jnp.bfloat16
LANES = 128
PIECES = 2


def first_kernel(out_ref):
    out_ref[...] = jnp.zeros_like(out_ref)


def project_kernel(rank, first_ref, acts_ref, grads_ref, proj_ref, *outs):
    rows = outs[0].shape[0]
    column = lax.broadcasted_iota(jnp.int32, (rows, 2 * rank), 1)
    for i, out_ref in enumerate(outs):
        part = slice(i * rows, (i + 1) * rows)
        term = jnp.dot(
            jnp.concatenate([acts_ref[0, part, :], grads_ref[0, part, :]], axis=0),
            proj_ref[...],
            preferred_element_type=F32,
        )
        out_ref[...] = jnp.where(column < rank, term[0:rows], term[rows:])


def count_kernel(rank, picks_ref, out_ref):
    tokens, width = out_ref.shape
    samples = picks_ref.shape[1]
    token = lax.broadcasted_iota(jnp.int32, (tokens, samples), 0)
    hits = jnp.where(token == picks_ref[...], 1.0, 0.0).astype(BF16)
    count = jnp.dot(hits, jnp.ones((samples, width), BF16), preferred_element_type=F32)
    column = lax.broadcasted_iota(jnp.int32, (tokens, width), 1)
    out_ref[...] = jnp.where(column < rank, count, 1.0)


def sketch_kernel(rank, count_ref, *refs):
    parts, (out_ref, held) = refs[:-2], refs[-2:]
    chunks = len(parts) // 2
    total = jnp.concatenate([parts[i][...] + parts[chunks + i][...] for i in range(chunks)], axis=0)
    total = total * count_ref[...]
    high = total.astype(BF16)
    low = (total - high.astype(F32)).astype(BF16)
    gram = lax.dot_general(
        jnp.concatenate([high, high, low], axis=0),
        jnp.concatenate([high, low, high], axis=0),
        (((0,), (0,)), ((), ())),
        preferred_element_type=F32,
    )
    held[...] = gram[rank : 2 * rank, 0:rank]
    pairs = out_ref.shape[0]
    even = held[pl.ds(0, pairs, stride=2), :]
    odd = held[pl.ds(1, pairs, stride=2), :]
    out_ref[...] = jnp.concatenate([even, odd], axis=1).astype(BF16)


def flatten_kernel(mates, own_ref, far_ref, first_ref, second_ref, wide):
    pairs = own_ref.shape[0]
    slots = first_ref.shape[0]
    core = lax.axis_index("tensor")
    wide[...] = jnp.zeros_like(wide)
    sketch = jnp.where(lax.axis_index("dp") // mates == core, far_ref[...], own_ref[...])
    wide[pl.ds(0, pairs, stride=slots), :] = sketch.astype(F32)
    for out_ref, half in ((first_ref, core), (second_ref, 1 - core)):
        start = half * (slots * pairs // 2)
        for j in range(pairs // 2):
            rows = wide[pl.ds(pl.multiple_of(start + j * slots, slots), slots), :]
            out_ref[:, j * LANES : (j + 1) * LANES] = rows


def score_kernel(first_ref, second_ref, own_ref, other_ref, out_ref):
    total = None
    for flat_ref, query_ref in ((first_ref, own_ref), (second_ref, other_ref)):
        for j in range(query_ref.shape[1] // LANES):
            lanes = slice(j * LANES, (j + 1) * LANES)
            term = query_ref[:, lanes].astype(F32) * flat_ref[0:1, lanes]
            total = term if total is None else total + term
    out_ref[...] = total


def arrange_kernel(*refs):
    parts, out_ref = refs[:-1], refs[-1]
    mates = len(parts)
    own_queries = parts[0].shape[0]
    width = mates * own_queries
    scores = jnp.concatenate([part[...] for part in parts], axis=0).T
    scores = jnp.broadcast_to(jnp.sum(scores, axis=0, keepdims=True), (8, width))
    member = lax.rem(lax.axis_index("dp"), mates)
    block = lax.broadcasted_iota(jnp.int32, scores.shape, 1) // own_queries
    step = 1
    while step < mates:
        up = pltpu.roll(scores, step * own_queries, 1)
        down = pltpu.roll(scores, width - step * own_queries, 1)
        exchanged = jnp.where(block & step == 0, down, up)
        scores = jnp.where(member & step == 0, scores, exchanged)
        step *= 2
    out_ref[...] = scores[0:1, :]


def on_device(activations, out_grads, projections, sample_index, queries):
    clips = lax.axis_size("dp")
    tokens, units = activations.shape[1:]
    rank = projections.shape[1] // 2
    own_queries, entries = queries.shape
    pairs = 2 * entries // LANES
    mates = clips // 2
    slots = 8
    vmem = pl.BlockSpec(memory_space=pltpu.VMEM)
    swap = [(0, 1), (1, 0)]
    both = ("dp", "tensor")

    def place(a, m, t):
        return (a * mates + m) * 2 + t

    spots = [(a, m) for a in range(2) for m in range(mates)]
    there = [(place(a, m, 1 - a), place(1 - a, m, 1 - a)) for a, m in spots]
    there += [(place(a, m, a), place(a, m, 1 - a)) for a, m in spots]
    back = [(dst, src) for src, dst in there]

    copied = 2 * (2 * tokens * units + units * 2 * rank)
    first = pl.pallas_call(
        first_kernel,
        out_specs=vmem,
        out_shape=jax.ShapeDtypeStruct((8, LANES), F32),
        compiler_params=pltpu.CompilerParams(vmem_limit_bytes=1 << 20),
        cost_estimate=pl.CostEstimate(flops=274 * copied, bytes_accessed=1, transcendentals=0),
        name="first",
    )()
    sent, first = lax.optimization_barrier((queries, first))
    halves = [queries]
    for r in range(1, mates):
        halves.append(lax.ppermute(sent, "dp", [(d, d ^ r) for d in range(clips)]))
    partial = pl.pallas_call(
        functools.partial(project_kernel, rank),
        in_specs=[vmem] * 4,
        out_specs=[vmem] * PIECES,
        out_shape=[jax.ShapeDtypeStruct((tokens // PIECES, 2 * rank), F32)] * PIECES,
        compiler_params=pltpu.CompilerParams(vmem_limit_bytes=16 << 20),
        cost_estimate=pl.CostEstimate(
            flops=8 * tokens * units * rank, bytes_accessed=4 * tokens * units, transcendentals=0
        ),
        name="project",
    )(first, activations, out_grads, projections)

    other = [lax.ppermute(part, "tensor", swap) for part in partial]
    count = pl.pallas_call(
        functools.partial(count_kernel, rank),
        in_specs=[vmem],
        out_specs=vmem,
        out_shape=jax.ShapeDtypeStruct((tokens, 2 * rank), F32),
        compiler_params=pltpu.CompilerParams(vmem_limit_bytes=8 << 20),
        cost_estimate=pl.CostEstimate(flops=1, bytes_accessed=1, transcendentals=0),
        name="count",
    )(sample_index)
    sketch = pl.pallas_call(
        functools.partial(sketch_kernel, rank),
        in_specs=[vmem] * (1 + 2 * len(partial)),
        out_specs=vmem,
        out_shape=jax.ShapeDtypeStruct((pairs, LANES), BF16),
        scratch_shapes=[pltpu.VMEM((rank, rank), F32)],
        compiler_params=pltpu.CompilerParams(vmem_limit_bytes=8 << 20),
        cost_estimate=pl.CostEstimate(flops=1, bytes_accessed=1, transcendentals=0),
        name="sketch",
    )(count, *partial, *other)

    far_sketch = lax.ppermute(sketch, both, there)
    swapped = []
    for half in halves:
        half, sketch = lax.optimization_barrier((half, sketch))
        swapped.append(lax.ppermute(half, "tensor", swap))

    width = mates * own_queries
    flats = pl.pallas_call(
        functools.partial(flatten_kernel, mates),
        in_specs=[vmem] * 2,
        out_specs=[vmem] * 2,
        out_shape=[jax.ShapeDtypeStruct((slots, entries), F32)] * 2,
        scratch_shapes=[pltpu.VMEM((pairs * slots, LANES), F32)],
        compiler_params=pltpu.CompilerParams(vmem_limit_bytes=8 << 20),
        cost_estimate=pl.CostEstimate(flops=1 << 34, bytes_accessed=64 << 20, transcendentals=0),
        name="flatten",
    )(sketch, far_sketch)
    small = pl.CostEstimate(flops=1, bytes_accessed=1, transcendentals=0)
    few = pltpu.CompilerParams(vmem_limit_bytes=8 << 20)
    parts = [
        pl.pallas_call(
            score_kernel,
            in_specs=[vmem] * 4,
            out_specs=vmem,
            out_shape=jax.ShapeDtypeStruct((own_queries, LANES), F32),
            compiler_params=few,
            cost_estimate=small,
            name="score",
        )(*flats, half, other)
        for half, other in zip(halves, swapped)
    ]
    scores = pl.pallas_call(
        arrange_kernel,
        in_specs=[vmem] * mates,
        out_specs=vmem,
        out_shape=jax.ShapeDtypeStruct((1, width), F32),
        compiler_params=few,
        cost_estimate=small,
        name="arrange",
    )(*parts)
    return lax.ppermute(scores, both, back)


def solution(mesh):
    in_specs = (
        P(("groups", "dp"), None, "tensor"),
        P(("groups", "dp"), None, "tensor"),
        P("tensor", None),
        P(("groups", "dp"), None),
        P(("groups", "dp"), "tensor"),
    )
    out_specs = P(("groups", "dp"), "tensor")
    return jax.shard_map(
        on_device, mesh=mesh, in_specs=in_specs, out_specs=out_specs, check_vma=False
    )
```

```python
import functools

import jax
import jax.numpy as jnp
from jax import lax
from jax.experimental import pallas as pl
from jax.experimental.pallas import tpu as pltpu
from jax.sharding import PartitionSpec as P

F32 = jnp.float32
BF16 = jnp.bfloat16
LANES = 128
PIECES = 2


def first_kernel(out_ref):
    out_ref[...] = jnp.zeros_like(out_ref)


def project_kernel(rank, first_ref, acts_ref, grads_ref, proj_ref, *outs):
    rows = outs[0].shape[0]
    column = lax.broadcasted_iota(jnp.int32, (rows, 2 * rank), 1)
    for i, out_ref in enumerate(outs):
        part = slice(i * rows, (i + 1) * rows)
        term = jnp.dot(
            jnp.concatenate([acts_ref[0, part, :], grads_ref[0, part, :]], axis=0),
            proj_ref[...],
            preferred_element_type=F32,
        )
        out_ref[...] = jnp.where(column < rank, term[0:rows], term[rows:])


def count_kernel(rank, picks_ref, out_ref):
    tokens, width = out_ref.shape
    samples = picks_ref.shape[1]
    token = lax.broadcasted_iota(jnp.int32, (tokens, samples), 0)
    hits = jnp.where(token == picks_ref[...], 1.0, 0.0).astype(BF16)
    count = jnp.dot(hits, jnp.ones((samples, width), BF16), preferred_element_type=F32)
    column = lax.broadcasted_iota(jnp.int32, (tokens, width), 1)
    out_ref[...] = jnp.where(column < rank, count, 1.0)


def sketch_kernel(rank, count_ref, *refs):
    parts, (out_ref, held) = refs[:-2], refs[-2:]
    chunks = len(parts) // 2
    total = jnp.concatenate([parts[i][...] + parts[chunks + i][...] for i in range(chunks)], axis=0)
    total = total * count_ref[...]
    high = total.astype(BF16)
    low = (total - high.astype(F32)).astype(BF16)
    gram = lax.dot_general(
        jnp.concatenate([high, high, low], axis=0),
        jnp.concatenate([high, low, high], axis=0),
        (((0,), (0,)), ((), ())),
        preferred_element_type=F32,
    )
    held[...] = gram[rank : 2 * rank, 0:rank]
    pairs = out_ref.shape[0]
    even = held[pl.ds(0, pairs, stride=2), :]
    odd = held[pl.ds(1, pairs, stride=2), :]
    out_ref[...] = jnp.concatenate([even, odd], axis=1).astype(BF16)


def flatten_kernel(mates, own_ref, far_ref, first_ref, second_ref, wide):
    pairs = own_ref.shape[0]
    slots = first_ref.shape[0]
    core = lax.axis_index("tensor")
    wide[...] = jnp.zeros_like(wide)
    sketch = jnp.where(lax.axis_index("dp") // mates == core, far_ref[...], own_ref[...])
    wide[pl.ds(0, pairs, stride=slots), :] = sketch.astype(F32)
    for out_ref, half in ((first_ref, core), (second_ref, 1 - core)):
        start = half * (slots * pairs // 2)
        for j in range(pairs // 2):
            rows = wide[pl.ds(pl.multiple_of(start + j * slots, slots), slots), :]
            out_ref[:, j * LANES : (j + 1) * LANES] = rows


def score_kernel(first_ref, second_ref, own_ref, other_ref, *refs):
    out_ref = refs[-1]
    total = None
    for flat_ref, query_ref in ((first_ref, own_ref), (second_ref, other_ref)):
        for j in range(query_ref.shape[1] // LANES):
            lanes = slice(j * LANES, (j + 1) * LANES)
            term = query_ref[:, lanes].astype(F32) * flat_ref[0:1, lanes]
            total = term if total is None else total + term
    out_ref[...] = total


def arrange_kernel(*refs):
    parts, out_ref = refs[:-1], refs[-1]
    mates = len(parts)
    own_queries = parts[0].shape[0]
    width = mates * own_queries
    scores = jnp.concatenate([part[...] for part in parts], axis=0).T
    scores = jnp.broadcast_to(jnp.sum(scores, axis=0, keepdims=True), (8, width))
    member = lax.rem(lax.axis_index("dp"), mates)
    block = lax.broadcasted_iota(jnp.int32, scores.shape, 1) // own_queries
    step = 1
    while step < mates:
        up = pltpu.roll(scores, step * own_queries, 1)
        down = pltpu.roll(scores, width - step * own_queries, 1)
        exchanged = jnp.where(block & step == 0, down, up)
        scores = jnp.where(member & step == 0, scores, exchanged)
        step *= 2
    out_ref[...] = scores[0:1, :]


def on_device(activations, out_grads, projections, sample_index, queries):
    clips = lax.axis_size("dp")
    tokens, units = activations.shape[1:]
    rank = projections.shape[1] // 2
    own_queries, entries = queries.shape
    pairs = 2 * entries // LANES
    mates = clips // 2
    slots = 8
    vmem = pl.BlockSpec(memory_space=pltpu.VMEM)
    swap = [(0, 1), (1, 0)]
    both = ("dp", "tensor")

    def place(a, m, t):
        return (a * mates + m) * 2 + t

    spots = [(a, m) for a in range(2) for m in range(mates)]
    there = [(place(a, m, 1 - a), place(1 - a, m, 1 - a)) for a, m in spots]
    there += [(place(a, m, a), place(a, m, 1 - a)) for a, m in spots]
    back = [(dst, src) for src, dst in there]

    copied = 2 * (2 * tokens * units + units * 2 * rank)
    first = pl.pallas_call(
        first_kernel,
        out_specs=vmem,
        out_shape=jax.ShapeDtypeStruct((8, LANES), F32),
        compiler_params=pltpu.CompilerParams(vmem_limit_bytes=1 << 20),
        cost_estimate=pl.CostEstimate(flops=274 * copied, bytes_accessed=1, transcendentals=0),
        name="first",
    )()
    sent, first = lax.optimization_barrier((queries, first))
    halves = [queries]
    for r in range(mates - 1, 0, -1):
        halves.append(lax.ppermute(sent, "dp", [(d, d ^ r) for d in range(clips)]))
    partial = pl.pallas_call(
        functools.partial(project_kernel, rank),
        in_specs=[vmem] * 4,
        out_specs=[vmem] * PIECES,
        out_shape=[jax.ShapeDtypeStruct((tokens // PIECES, 2 * rank), F32)] * PIECES,
        compiler_params=pltpu.CompilerParams(vmem_limit_bytes=16 << 20),
        cost_estimate=pl.CostEstimate(
            flops=8 * tokens * units * rank, bytes_accessed=4 * tokens * units, transcendentals=0
        ),
        name="project",
    )(first, activations, out_grads, projections)

    other = [lax.ppermute(part, "tensor", swap) for part in partial]
    count = pl.pallas_call(
        functools.partial(count_kernel, rank),
        in_specs=[vmem],
        out_specs=vmem,
        out_shape=jax.ShapeDtypeStruct((tokens, 2 * rank), F32),
        compiler_params=pltpu.CompilerParams(vmem_limit_bytes=8 << 20),
        cost_estimate=pl.CostEstimate(flops=1, bytes_accessed=1, transcendentals=0),
        name="count",
    )(sample_index)
    sketch = pl.pallas_call(
        functools.partial(sketch_kernel, rank),
        in_specs=[vmem] * (1 + 2 * len(partial)),
        out_specs=vmem,
        out_shape=jax.ShapeDtypeStruct((pairs, LANES), BF16),
        scratch_shapes=[pltpu.VMEM((rank, rank), F32)],
        compiler_params=pltpu.CompilerParams(vmem_limit_bytes=8 << 20),
        cost_estimate=pl.CostEstimate(flops=1, bytes_accessed=1, transcendentals=0),
        name="sketch",
    )(count, *partial, *other)

    far_sketch = lax.ppermute(sketch, both, there)
    swapped = []
    for half in halves:
        half, sketch = lax.optimization_barrier((half, sketch))
        swapped.append(lax.ppermute(half, "tensor", swap))

    width = mates * own_queries
    flats = pl.pallas_call(
        functools.partial(flatten_kernel, mates),
        in_specs=[vmem] * 2,
        out_specs=[vmem] * 2,
        out_shape=[jax.ShapeDtypeStruct((slots, entries), F32)] * 2,
        scratch_shapes=[pltpu.VMEM((pairs * slots, LANES), F32)],
        compiler_params=pltpu.CompilerParams(vmem_limit_bytes=8 << 20),
        cost_estimate=pl.CostEstimate(flops=1 << 34, bytes_accessed=64 << 20, transcendentals=0),
        name="flatten",
    )(sketch, far_sketch)
    small = pl.CostEstimate(flops=1, bytes_accessed=1, transcendentals=0)
    few = pltpu.CompilerParams(vmem_limit_bytes=8 << 20)
    parts = []
    for half, other in zip(halves, swapped):
        before = parts[-1:]
        parts.append(
            pl.pallas_call(
                score_kernel,
                in_specs=[vmem] * (4 + len(before)),
                out_specs=vmem,
                out_shape=jax.ShapeDtypeStruct((own_queries, LANES), F32),
                compiler_params=few,
                cost_estimate=small,
                name="score",
            )(*flats, half, other, *before)
        )
    scores = pl.pallas_call(
        arrange_kernel,
        in_specs=[vmem] * mates,
        out_specs=vmem,
        out_shape=jax.ShapeDtypeStruct((1, width), F32),
        compiler_params=few,
        cost_estimate=small,
        name="arrange",
    )(parts[0], *parts[:0:-1])
    return lax.ppermute(scores, both, back)


def solution(mesh):
    in_specs = (
        P(("groups", "dp"), None, "tensor"),
        P(("groups", "dp"), None, "tensor"),
        P("tensor", None),
        P(("groups", "dp"), None),
        P(("groups", "dp"), "tensor"),
    )
    out_specs = P(("groups", "dp"), "tensor")
    return jax.shard_map(
        on_device, mesh=mesh, in_specs=in_specs, out_specs=out_specs, check_vma=False
    )
```

```python
import functools

import jax
import jax.numpy as jnp
from jax import lax
from jax.experimental import pallas as pl
from jax.experimental.pallas import tpu as pltpu
from jax.sharding import PartitionSpec as P

F32 = jnp.float32
BF16 = jnp.bfloat16
LANES = 128
PIECES = 2


def first_kernel(out_ref):
    out_ref[...] = jnp.zeros_like(out_ref)


def project_kernel(rank, first_ref, acts_ref, grads_ref, proj_ref, *outs):
    rows = outs[0].shape[0]
    column = lax.broadcasted_iota(jnp.int32, (rows, 2 * rank), 1)
    for i, out_ref in enumerate(outs):
        part = slice(i * rows, (i + 1) * rows)
        term = jnp.dot(
            jnp.concatenate([acts_ref[0, part, :], grads_ref[0, part, :]], axis=0),
            proj_ref[...],
            preferred_element_type=F32,
        )
        out_ref[...] = jnp.where(column < rank, term[0:rows], term[rows:])


def count_kernel(rank, picks_ref, out_ref):
    tokens, width = out_ref.shape
    samples = picks_ref.shape[1]
    token = lax.broadcasted_iota(jnp.int32, (tokens, samples), 0)
    hits = jnp.where(token == picks_ref[...], 1.0, 0.0).astype(BF16)
    count = jnp.dot(hits, jnp.ones((samples, width), BF16), preferred_element_type=F32)
    column = lax.broadcasted_iota(jnp.int32, (tokens, width), 1)
    out_ref[...] = jnp.where(column < rank, count, 1.0)


def sketch_kernel(rank, count_ref, *refs):
    parts, (out_ref, held) = refs[:-2], refs[-2:]
    chunks = len(parts) // 2
    total = jnp.concatenate([parts[i][...] + parts[chunks + i][...] for i in range(chunks)], axis=0)
    total = total * count_ref[...]
    high = total.astype(BF16)
    low = (total - high.astype(F32)).astype(BF16)
    gram = lax.dot_general(
        jnp.concatenate([high, high, low], axis=0),
        jnp.concatenate([high, low, high], axis=0),
        (((0,), (0,)), ((), ())),
        preferred_element_type=F32,
    )
    held[...] = gram[rank : 2 * rank, 0:rank]
    pairs = out_ref.shape[0]
    even = held[pl.ds(0, pairs, stride=2), :]
    odd = held[pl.ds(1, pairs, stride=2), :]
    out_ref[...] = jnp.concatenate([even, odd], axis=1).astype(BF16)


def flatten_kernel(mates, own_ref, far_ref, first_ref, second_ref, wide):
    pairs = own_ref.shape[0]
    slots = first_ref.shape[0]
    core = lax.axis_index("tensor")
    wide[...] = jnp.zeros_like(wide)
    sketch = jnp.where(lax.axis_index("dp") // mates == core, far_ref[...], own_ref[...])
    wide[pl.ds(0, pairs, stride=slots), :] = sketch.astype(F32)
    for out_ref, half in ((first_ref, core), (second_ref, 1 - core)):
        start = half * (slots * pairs // 2)
        for j in range(pairs // 2):
            rows = wide[pl.ds(pl.multiple_of(start + j * slots, slots), slots), :]
            out_ref[:, j * LANES : (j + 1) * LANES] = rows


def score_kernel(first_ref, second_ref, own_ref, other_ref, *refs):
    out_ref = refs[-1]
    total = None
    for flat_ref, query_ref in ((first_ref, own_ref), (second_ref, other_ref)):
        for j in range(query_ref.shape[1] // LANES):
            lanes = slice(j * LANES, (j + 1) * LANES)
            term = query_ref[:, lanes].astype(F32) * flat_ref[0:1, lanes]
            total = term if total is None else total + term
    out_ref[...] = total


def arrange_kernel(*refs):
    parts, out_ref, held = refs[:-2], refs[-2], refs[-1]
    mates = len(parts)
    own_queries = parts[0].shape[0]
    member = lax.rem(lax.axis_index("dp"), mates)
    for r, part in enumerate(parts):
        start = pl.multiple_of((member ^ r) * own_queries, own_queries)
        held[pl.ds(start, own_queries), :] = part[...]
    out_ref[...] = jnp.sum(held[...].T, axis=0, keepdims=True)


def on_device(activations, out_grads, projections, sample_index, queries):
    clips = lax.axis_size("dp")
    tokens, units = activations.shape[1:]
    rank = projections.shape[1] // 2
    own_queries, entries = queries.shape
    pairs = 2 * entries // LANES
    mates = clips // 2
    slots = 8
    vmem = pl.BlockSpec(memory_space=pltpu.VMEM)
    swap = [(0, 1), (1, 0)]
    both = ("dp", "tensor")

    def place(a, m, t):
        return (a * mates + m) * 2 + t

    spots = [(a, m) for a in range(2) for m in range(mates)]
    there = [(place(a, m, 1 - a), place(1 - a, m, 1 - a)) for a, m in spots]
    there += [(place(a, m, a), place(a, m, 1 - a)) for a, m in spots]
    back = [(dst, src) for src, dst in there]

    copied = 2 * (2 * tokens * units + units * 2 * rank)
    first = pl.pallas_call(
        first_kernel,
        out_specs=vmem,
        out_shape=jax.ShapeDtypeStruct((8, LANES), F32),
        compiler_params=pltpu.CompilerParams(vmem_limit_bytes=1 << 20),
        cost_estimate=pl.CostEstimate(flops=274 * copied, bytes_accessed=1, transcendentals=0),
        name="first",
    )()
    sent, first = lax.optimization_barrier((queries, first))
    halves = [queries]
    for r in range(mates - 1, 0, -1):
        halves.append(lax.ppermute(sent, "dp", [(d, d ^ r) for d in range(clips)]))
    partial = pl.pallas_call(
        functools.partial(project_kernel, rank),
        in_specs=[vmem] * 4,
        out_specs=[vmem] * PIECES,
        out_shape=[jax.ShapeDtypeStruct((tokens // PIECES, 2 * rank), F32)] * PIECES,
        compiler_params=pltpu.CompilerParams(vmem_limit_bytes=16 << 20),
        cost_estimate=pl.CostEstimate(
            flops=8 * tokens * units * rank, bytes_accessed=4 * tokens * units, transcendentals=0
        ),
        name="project",
    )(first, activations, out_grads, projections)

    other = [lax.ppermute(part, "tensor", swap) for part in partial]
    count = pl.pallas_call(
        functools.partial(count_kernel, rank),
        in_specs=[vmem],
        out_specs=vmem,
        out_shape=jax.ShapeDtypeStruct((tokens, 2 * rank), F32),
        compiler_params=pltpu.CompilerParams(vmem_limit_bytes=8 << 20),
        cost_estimate=pl.CostEstimate(flops=1, bytes_accessed=1, transcendentals=0),
        name="count",
    )(sample_index)
    sketch = pl.pallas_call(
        functools.partial(sketch_kernel, rank),
        in_specs=[vmem] * (1 + 2 * len(partial)),
        out_specs=vmem,
        out_shape=jax.ShapeDtypeStruct((pairs, LANES), BF16),
        scratch_shapes=[pltpu.VMEM((rank, rank), F32)],
        compiler_params=pltpu.CompilerParams(vmem_limit_bytes=8 << 20),
        cost_estimate=pl.CostEstimate(flops=1, bytes_accessed=1, transcendentals=0),
        name="sketch",
    )(count, *partial, *other)

    far_sketch = lax.ppermute(sketch, both, there)
    swapped = []
    for half in halves:
        half, sketch = lax.optimization_barrier((half, sketch))
        swapped.append(lax.ppermute(half, "tensor", swap))

    width = mates * own_queries
    flats = pl.pallas_call(
        functools.partial(flatten_kernel, mates),
        in_specs=[vmem] * 2,
        out_specs=[vmem] * 2,
        out_shape=[jax.ShapeDtypeStruct((slots, entries), F32)] * 2,
        scratch_shapes=[pltpu.VMEM((pairs * slots, LANES), F32)],
        compiler_params=pltpu.CompilerParams(vmem_limit_bytes=8 << 20),
        cost_estimate=pl.CostEstimate(flops=1 << 34, bytes_accessed=64 << 20, transcendentals=0),
        name="flatten",
    )(sketch, far_sketch)
    small = pl.CostEstimate(flops=1, bytes_accessed=1, transcendentals=0)
    few = pltpu.CompilerParams(vmem_limit_bytes=8 << 20)
    parts = []
    for half, other in zip(halves, swapped):
        before = parts[-1:]
        parts.append(
            pl.pallas_call(
                score_kernel,
                in_specs=[vmem] * (4 + len(before)),
                out_specs=vmem,
                out_shape=jax.ShapeDtypeStruct((own_queries, LANES), F32),
                compiler_params=few,
                cost_estimate=small,
                name="score",
            )(*flats, half, other, *before)
        )
    scores = pl.pallas_call(
        arrange_kernel,
        in_specs=[vmem] * mates,
        out_specs=vmem,
        out_shape=jax.ShapeDtypeStruct((1, width), F32),
        scratch_shapes=[pltpu.VMEM((width, LANES), F32)],
        compiler_params=few,
        cost_estimate=small,
        name="arrange",
    )(parts[0], *parts[:0:-1])
    return lax.ppermute(scores, both, back)


def solution(mesh):
    in_specs = (
        P(("groups", "dp"), None, "tensor"),
        P(("groups", "dp"), None, "tensor"),
        P("tensor", None),
        P(("groups", "dp"), None),
        P(("groups", "dp"), "tensor"),
    )
    out_specs = P(("groups", "dp"), "tensor")
    return jax.shard_map(
        on_device, mesh=mesh, in_specs=in_specs, out_specs=out_specs, check_vma=False
    )
```

```python
import functools

import jax
import jax.numpy as jnp
from jax import lax
from jax.experimental import pallas as pl
from jax.experimental.pallas import tpu as pltpu
from jax.sharding import PartitionSpec as P

F32 = jnp.float32
BF16 = jnp.bfloat16
LANES = 128
PIECES = 2


def first_kernel(out_ref):
    out_ref[...] = jnp.zeros_like(out_ref)


def project_kernel(rank, first_ref, acts_ref, grads_ref, proj_ref, *outs):
    rows = outs[0].shape[0]
    column = lax.broadcasted_iota(jnp.int32, (rows, 2 * rank), 1)
    for i, out_ref in enumerate(outs):
        part = slice(i * rows, (i + 1) * rows)
        term = jnp.dot(
            jnp.concatenate([acts_ref[0, part, :], grads_ref[0, part, :]], axis=0),
            proj_ref[...],
            preferred_element_type=F32,
        )
        out_ref[...] = jnp.where(column < rank, term[0:rows], term[rows:])


def count_kernel(rank, picks_ref, out_ref):
    tokens, width = out_ref.shape
    samples = picks_ref.shape[1]
    token = lax.broadcasted_iota(jnp.int32, (tokens, samples), 0)
    hits = jnp.where(token == picks_ref[...], 1.0, 0.0).astype(BF16)
    count = jnp.dot(hits, jnp.ones((samples, width), BF16), preferred_element_type=F32)
    column = lax.broadcasted_iota(jnp.int32, (tokens, width), 1)
    out_ref[...] = jnp.where(column < rank, count, 1.0)


def sketch_kernel(rank, count_ref, *refs):
    parts, (out_ref, held) = refs[:-2], refs[-2:]
    chunks = len(parts) // 2
    total = jnp.concatenate([parts[i][...] + parts[chunks + i][...] for i in range(chunks)], axis=0)
    total = total * count_ref[...]
    high = total.astype(BF16)
    low = (total - high.astype(F32)).astype(BF16)
    gram = lax.dot_general(
        jnp.concatenate([high, high, low], axis=0),
        jnp.concatenate([high, low, high], axis=0),
        (((0,), (0,)), ((), ())),
        preferred_element_type=F32,
    )
    held[...] = gram[rank : 2 * rank, 0:rank]
    pairs = out_ref.shape[0]
    even = held[pl.ds(0, pairs, stride=2), :]
    odd = held[pl.ds(1, pairs, stride=2), :]
    out_ref[...] = jnp.concatenate([even, odd], axis=1).astype(BF16)


def hold_kernel(*refs):
    pass


def flatten_kernel(mates, own_ref, far_ref, first_ref, second_ref, wide):
    pairs = own_ref.shape[0]
    slots = first_ref.shape[0]
    core = lax.axis_index("tensor")
    wide[...] = jnp.zeros_like(wide)
    sketch = jnp.where(lax.axis_index("dp") // mates == core, far_ref[...], own_ref[...])
    wide[pl.ds(0, pairs, stride=slots), :] = sketch.astype(F32)
    for out_ref, half in ((first_ref, core), (second_ref, 1 - core)):
        start = half * (slots * pairs // 2)
        for j in range(pairs // 2):
            rows = wide[pl.ds(pl.multiple_of(start + j * slots, slots), slots), :]
            out_ref[:, j * LANES : (j + 1) * LANES] = rows


def score_kernel(first_ref, second_ref, own_ref, other_ref, *refs):
    out_ref = refs[-1]
    total = None
    for flat_ref, query_ref in ((first_ref, own_ref), (second_ref, other_ref)):
        for j in range(query_ref.shape[1] // LANES):
            lanes = slice(j * LANES, (j + 1) * LANES)
            term = query_ref[:, lanes].astype(F32) * flat_ref[0:1, lanes]
            total = term if total is None else total + term
    out_ref[...] = total


def arrange_kernel(*refs):
    parts, out_ref, held = refs[:-2], refs[-2], refs[-1]
    mates = len(parts)
    own_queries = parts[0].shape[0]
    member = lax.rem(lax.axis_index("dp"), mates)
    for r, part in enumerate(parts):
        start = pl.multiple_of((member ^ r) * own_queries, own_queries)
        held[pl.ds(start, own_queries), :] = part[...]
    out_ref[...] = jnp.sum(held[...].T, axis=0, keepdims=True)


def on_device(activations, out_grads, projections, sample_index, queries):
    clips = lax.axis_size("dp")
    tokens, units = activations.shape[1:]
    rank = projections.shape[1] // 2
    own_queries, entries = queries.shape
    pairs = 2 * entries // LANES
    mates = clips // 2
    slots = 8
    vmem = pl.BlockSpec(memory_space=pltpu.VMEM)
    swap = [(0, 1), (1, 0)]
    both = ("dp", "tensor")

    def place(a, m, t):
        return (a * mates + m) * 2 + t

    spots = [(a, m) for a in range(2) for m in range(mates)]
    there = [(place(a, m, 1 - a), place(1 - a, m, 1 - a)) for a, m in spots]
    there += [(place(a, m, a), place(a, m, 1 - a)) for a, m in spots]
    back = [(dst, src) for src, dst in there]

    copied = 2 * (2 * tokens * units + units * 2 * rank)
    first = pl.pallas_call(
        first_kernel,
        out_specs=vmem,
        out_shape=jax.ShapeDtypeStruct((8, LANES), F32),
        compiler_params=pltpu.CompilerParams(vmem_limit_bytes=1 << 20),
        cost_estimate=pl.CostEstimate(flops=274 * copied, bytes_accessed=1, transcendentals=0),
        name="first",
    )()
    sent, first = lax.optimization_barrier((queries, first))
    halves = [queries]
    for r in range(mates - 1, 0, -1):
        halves.append(lax.ppermute(sent, "dp", [(d, d ^ r) for d in range(clips)]))
    partial = pl.pallas_call(
        functools.partial(project_kernel, rank),
        in_specs=[vmem] * 4,
        out_specs=[vmem] * PIECES,
        out_shape=[jax.ShapeDtypeStruct((tokens // PIECES, 2 * rank), F32)] * PIECES,
        compiler_params=pltpu.CompilerParams(vmem_limit_bytes=16 << 20),
        cost_estimate=pl.CostEstimate(
            flops=8 * tokens * units * rank, bytes_accessed=4 * tokens * units, transcendentals=0
        ),
        name="project",
    )(first, activations, out_grads, projections)

    other = [lax.ppermute(part, "tensor", swap) for part in partial]
    count = pl.pallas_call(
        functools.partial(count_kernel, rank),
        in_specs=[vmem],
        out_specs=vmem,
        out_shape=jax.ShapeDtypeStruct((tokens, 2 * rank), F32),
        compiler_params=pltpu.CompilerParams(vmem_limit_bytes=8 << 20),
        cost_estimate=pl.CostEstimate(flops=1, bytes_accessed=1, transcendentals=0),
        name="count",
    )(sample_index)
    sketch = pl.pallas_call(
        functools.partial(sketch_kernel, rank),
        in_specs=[vmem] * (1 + 2 * len(partial)),
        out_specs=vmem,
        out_shape=jax.ShapeDtypeStruct((pairs, LANES), BF16),
        scratch_shapes=[pltpu.VMEM((rank, rank), F32)],
        compiler_params=pltpu.CompilerParams(vmem_limit_bytes=8 << 20),
        cost_estimate=pl.CostEstimate(flops=1, bytes_accessed=1, transcendentals=0),
        name="sketch",
    )(count, *partial, *other)

    far_sketch = lax.ppermute(sketch, both, there)
    def hold(half, *ended):
        return pl.pallas_call(
            hold_kernel,
            in_specs=[vmem] * (1 + len(ended)),
            out_specs=vmem,
            out_shape=jax.ShapeDtypeStruct(half.shape, BF16),
            input_output_aliases={0: 0},
            compiler_params=pltpu.CompilerParams(vmem_limit_bytes=8 << 20),
            cost_estimate=pl.CostEstimate(flops=1, bytes_accessed=1, transcendentals=0),
            name="hold",
        )(half, *ended)

    last = mates // 2
    sequence = [k for k in range(mates) if k != last] + [last]
    for k in sequence[1:-1]:
        halves[k] = hold(halves[k], sketch)
    halves[last] = hold(halves[last], *[halves[k] for k in sequence[1:-1]])
    swapped = [lax.ppermute(half, "tensor", swap) for half in halves]
    width = mates * own_queries
    flats = pl.pallas_call(
        functools.partial(flatten_kernel, mates),
        in_specs=[vmem] * 2,
        out_specs=[vmem] * 2,
        out_shape=[jax.ShapeDtypeStruct((slots, entries), F32)] * 2,
        scratch_shapes=[pltpu.VMEM((pairs * slots, LANES), F32)],
        compiler_params=pltpu.CompilerParams(vmem_limit_bytes=8 << 20),
        cost_estimate=pl.CostEstimate(flops=1 << 34, bytes_accessed=64 << 20, transcendentals=0),
        name="flatten",
    )(sketch, far_sketch)
    small = pl.CostEstimate(flops=1, bytes_accessed=1, transcendentals=0)
    few = pltpu.CompilerParams(vmem_limit_bytes=8 << 20)
    parts = []
    for k in sequence:
        half, other = halves[k], swapped[k]
        before = parts[-1:]
        parts.append(
            pl.pallas_call(
                score_kernel,
                in_specs=[vmem] * (4 + len(before)),
                out_specs=vmem,
                out_shape=jax.ShapeDtypeStruct((own_queries, LANES), F32),
                compiler_params=few,
                cost_estimate=small,
                name="score",
            )(*flats, half, other, *before)
        )
    scores = pl.pallas_call(
        arrange_kernel,
        in_specs=[vmem] * mates,
        out_specs=vmem,
        out_shape=jax.ShapeDtypeStruct((1, width), F32),
        scratch_shapes=[pltpu.VMEM((width, LANES), F32)],
        compiler_params=few,
        cost_estimate=small,
        name="arrange",
    )(*[parts[sequence.index(-r % mates)] for r in range(mates)])
    return lax.ppermute(scores, both, back)


def solution(mesh):
    in_specs = (
        P(("groups", "dp"), None, "tensor"),
        P(("groups", "dp"), None, "tensor"),
        P("tensor", None),
        P(("groups", "dp"), None),
        P(("groups", "dp"), "tensor"),
    )
    out_specs = P(("groups", "dp"), "tensor")
    return jax.shard_map(
        on_device, mesh=mesh, in_specs=in_specs, out_specs=out_specs, check_vma=False
    )
```

```python
import functools

import jax
import jax.numpy as jnp
from jax import lax
from jax.experimental import pallas as pl
from jax.experimental.pallas import tpu as pltpu
from jax.sharding import PartitionSpec as P

F32 = jnp.float32
BF16 = jnp.bfloat16
LANES = 128
PIECES = 2


def first_kernel(out_ref):
    out_ref[...] = jnp.zeros_like(out_ref)


def project_kernel(rank, first_ref, acts_ref, grads_ref, proj_ref, *outs):
    rows = outs[0].shape[0]
    column = lax.broadcasted_iota(jnp.int32, (rows, 2 * rank), 1)
    for i, out_ref in enumerate(outs):
        part = slice(i * rows, (i + 1) * rows)
        term = jnp.dot(
            jnp.concatenate([acts_ref[0, part, :], grads_ref[0, part, :]], axis=0),
            proj_ref[...],
            preferred_element_type=F32,
        )
        out_ref[...] = jnp.where(column < rank, term[0:rows], term[rows:])


def count_kernel(rank, picks_ref, out_ref):
    tokens, width = out_ref.shape
    samples = picks_ref.shape[1]
    token = lax.broadcasted_iota(jnp.int32, (tokens, samples), 0)
    hits = jnp.where(token == picks_ref[...], 1.0, 0.0).astype(BF16)
    count = jnp.dot(hits, jnp.ones((samples, width), BF16), preferred_element_type=F32)
    column = lax.broadcasted_iota(jnp.int32, (tokens, width), 1)
    out_ref[...] = jnp.where(column < rank, count, 1.0)


def sketch_kernel(rank, count_ref, *refs):
    parts, (out_ref, held) = refs[:-2], refs[-2:]
    chunks = len(parts) // 2
    total = jnp.concatenate([parts[i][...] + parts[chunks + i][...] for i in range(chunks)], axis=0)
    total = total * count_ref[...]
    high = total.astype(BF16)
    low = (total - high.astype(F32)).astype(BF16)
    gram = lax.dot_general(
        jnp.concatenate([high, high, low], axis=0),
        jnp.concatenate([high, low, high], axis=0),
        (((0,), (0,)), ((), ())),
        preferred_element_type=F32,
    )
    held[...] = gram[rank : 2 * rank, 0:rank]
    pairs = out_ref.shape[0]
    even = held[pl.ds(0, pairs, stride=2), :]
    odd = held[pl.ds(1, pairs, stride=2), :]
    out_ref[...] = jnp.concatenate([even, odd], axis=1).astype(BF16)


def hold_kernel(*refs):
    pass


def flatten_kernel(mates, own_ref, far_ref, first_ref, second_ref, wide):
    pairs = own_ref.shape[0]
    slots = first_ref.shape[0]
    core = lax.axis_index("tensor")
    wide[...] = jnp.zeros_like(wide)
    sketch = jnp.where(lax.axis_index("dp") // mates == core, far_ref[...], own_ref[...])
    wide[pl.ds(0, pairs, stride=slots), :] = sketch.astype(F32)
    for out_ref, half in ((first_ref, core), (second_ref, 1 - core)):
        start = half * (slots * pairs // 2)
        for j in range(pairs // 2):
            rows = wide[pl.ds(pl.multiple_of(start + j * slots, slots), slots), :]
            out_ref[:, j * LANES : (j + 1) * LANES] = rows


def score_kernel(first_ref, second_ref, own_ref, other_ref, *refs):
    out_ref = refs[-1]
    total = None
    for flat_ref, query_ref in ((first_ref, own_ref), (second_ref, other_ref)):
        for j in range(query_ref.shape[1] // LANES):
            lanes = slice(j * LANES, (j + 1) * LANES)
            term = query_ref[:, lanes].astype(F32) * flat_ref[0:1, lanes]
            total = term if total is None else total + term
    out_ref[...] = total


def arrange_kernel(*refs):
    parts, out_ref, held = refs[:-2], refs[-2], refs[-1]
    mates = len(parts)
    own_queries = parts[0].shape[0]
    member = lax.rem(lax.axis_index("dp"), mates)
    for r, part in enumerate(parts):
        start = pl.multiple_of((member ^ r) * own_queries, own_queries)
        held[pl.ds(start, own_queries), :] = part[...]
    out_ref[...] = jnp.sum(held[...].T, axis=0, keepdims=True)


def on_device(activations, out_grads, projections, sample_index, queries):
    clips = lax.axis_size("dp")
    tokens, units = activations.shape[1:]
    rank = projections.shape[1] // 2
    own_queries, entries = queries.shape
    pairs = 2 * entries // LANES
    mates = clips // 2
    slots = 8
    vmem = pl.BlockSpec(memory_space=pltpu.VMEM)
    swap = [(0, 1), (1, 0)]
    both = ("dp", "tensor")

    def place(a, m, t):
        return (a * mates + m) * 2 + t

    spots = [(a, m) for a in range(2) for m in range(mates)]
    there = [(place(a, m, 1 - a), place(1 - a, m, 1 - a)) for a, m in spots]
    there += [(place(a, m, a), place(a, m, 1 - a)) for a, m in spots]
    back = [(dst, src) for src, dst in there]

    copied = 2 * (2 * tokens * units + units * 2 * rank)
    first = pl.pallas_call(
        first_kernel,
        out_specs=vmem,
        out_shape=jax.ShapeDtypeStruct((8, LANES), F32),
        compiler_params=pltpu.CompilerParams(vmem_limit_bytes=1 << 20),
        cost_estimate=pl.CostEstimate(flops=274 * copied, bytes_accessed=1, transcendentals=0),
        name="first",
    )()
    sent, first = lax.optimization_barrier((queries, first))
    halves = [queries]
    for r in range(mates - 1, 0, -1):
        halves.append(lax.ppermute(sent, "dp", [(d, d ^ r) for d in range(clips)]))
    partial = pl.pallas_call(
        functools.partial(project_kernel, rank),
        in_specs=[vmem] * 4,
        out_specs=[vmem] * PIECES,
        out_shape=[jax.ShapeDtypeStruct((tokens // PIECES, 2 * rank), F32)] * PIECES,
        compiler_params=pltpu.CompilerParams(vmem_limit_bytes=16 << 20),
        cost_estimate=pl.CostEstimate(
            flops=8 * tokens * units * rank, bytes_accessed=4 * tokens * units, transcendentals=0
        ),
        name="project",
    )(first, activations, out_grads, projections)

    other = [lax.ppermute(part, "tensor", swap) for part in partial]
    count = pl.pallas_call(
        functools.partial(count_kernel, rank),
        in_specs=[vmem],
        out_specs=vmem,
        out_shape=jax.ShapeDtypeStruct((tokens, 2 * rank), F32),
        compiler_params=pltpu.CompilerParams(vmem_limit_bytes=8 << 20),
        cost_estimate=pl.CostEstimate(flops=1, bytes_accessed=1, transcendentals=0),
        name="count",
    )(sample_index)
    sketch = pl.pallas_call(
        functools.partial(sketch_kernel, rank),
        in_specs=[vmem] * (1 + 2 * len(partial)),
        out_specs=vmem,
        out_shape=jax.ShapeDtypeStruct((pairs, LANES), BF16),
        scratch_shapes=[pltpu.VMEM((rank, rank), F32)],
        compiler_params=pltpu.CompilerParams(vmem_limit_bytes=8 << 20),
        cost_estimate=pl.CostEstimate(flops=1, bytes_accessed=1, transcendentals=0),
        name="sketch",
    )(count, *partial, *other)

    far_sketch = lax.ppermute(sketch, both, there)
    def hold(half, *ended):
        return pl.pallas_call(
            hold_kernel,
            in_specs=[vmem] * (1 + len(ended)),
            out_specs=vmem,
            out_shape=jax.ShapeDtypeStruct(half.shape, BF16),
            input_output_aliases={0: 0},
            compiler_params=pltpu.CompilerParams(vmem_limit_bytes=8 << 20),
            cost_estimate=pl.CostEstimate(flops=1, bytes_accessed=1, transcendentals=0),
            name="hold",
        )(half, *ended)

    for k in range(1, mates - 1):
        halves[k] = hold(halves[k], sketch)
    halves[-1] = hold(halves[-1], *halves[1:-1])
    swapped = [lax.ppermute(half, "tensor", swap) for half in halves]
    width = mates * own_queries
    flats = pl.pallas_call(
        functools.partial(flatten_kernel, mates),
        in_specs=[vmem] * 2,
        out_specs=[vmem] * 2,
        out_shape=[jax.ShapeDtypeStruct((slots, entries), F32)] * 2,
        scratch_shapes=[pltpu.VMEM((pairs * slots, LANES), F32)],
        compiler_params=pltpu.CompilerParams(vmem_limit_bytes=8 << 20),
        cost_estimate=pl.CostEstimate(flops=1 << 34, bytes_accessed=64 << 20, transcendentals=0),
        name="flatten",
    )(sketch, far_sketch)
    small = pl.CostEstimate(flops=1, bytes_accessed=1, transcendentals=0)
    few = pltpu.CompilerParams(vmem_limit_bytes=8 << 20)
    parts = []
    for half, other in zip(halves, swapped):
        before = parts[-1:]
        parts.append(
            pl.pallas_call(
                score_kernel,
                in_specs=[vmem] * (4 + len(before)),
                out_specs=vmem,
                out_shape=jax.ShapeDtypeStruct((own_queries, LANES), F32),
                compiler_params=few,
                cost_estimate=small,
                name="score",
            )(*flats, half, other, *before)
        )
    scores = pl.pallas_call(
        arrange_kernel,
        in_specs=[vmem] * mates,
        out_specs=vmem,
        out_shape=jax.ShapeDtypeStruct((1, width), F32),
        scratch_shapes=[pltpu.VMEM((width, LANES), F32)],
        compiler_params=few,
        cost_estimate=small,
        name="arrange",
    )(parts[0], *parts[:0:-1])
    return lax.ppermute(scores, both, back)


def solution(mesh):
    in_specs = (
        P(("groups", "dp"), None, "tensor"),
        P(("groups", "dp"), None, "tensor"),
        P("tensor", None),
        P(("groups", "dp"), None),
        P(("groups", "dp"), "tensor"),
    )
    out_specs = P(("groups", "dp"), "tensor")
    return jax.shard_map(
        on_device, mesh=mesh, in_specs=in_specs, out_specs=out_specs, check_vma=False
    )
```

```python
import functools

import jax
import jax.numpy as jnp
from jax import lax
from jax.experimental import pallas as pl
from jax.experimental.pallas import tpu as pltpu
from jax.sharding import PartitionSpec as P

F32 = jnp.float32
BF16 = jnp.bfloat16
LANES = 128
PIECES = 2


def first_kernel(out_ref):
    out_ref[...] = jnp.zeros_like(out_ref)


def project_kernel(rank, first_ref, acts_ref, grads_ref, proj_ref, *outs):
    rows = outs[0].shape[0]
    column = lax.broadcasted_iota(jnp.int32, (rows, 2 * rank), 1)
    for i, out_ref in enumerate(outs):
        part = slice(i * rows, (i + 1) * rows)
        term = jnp.dot(
            jnp.concatenate([acts_ref[0, part, :], grads_ref[0, part, :]], axis=0),
            proj_ref[...],
            preferred_element_type=F32,
        )
        out_ref[...] = jnp.where(column < rank, term[0:rows], term[rows:])


def count_kernel(rank, picks_ref, out_ref):
    tokens, width = out_ref.shape
    samples = picks_ref.shape[1]
    token = lax.broadcasted_iota(jnp.int32, (tokens, samples), 0)
    hits = jnp.where(token == picks_ref[...], 1.0, 0.0).astype(BF16)
    count = jnp.dot(hits, jnp.ones((samples, width), BF16), preferred_element_type=F32)
    column = lax.broadcasted_iota(jnp.int32, (tokens, width), 1)
    out_ref[...] = jnp.where(column < rank, count, 1.0)


def sketch_kernel(rank, count_ref, *refs):
    parts, (out_ref, held) = refs[:-2], refs[-2:]
    chunks = len(parts) // 2
    total = jnp.concatenate([parts[i][...] + parts[chunks + i][...] for i in range(chunks)], axis=0)
    total = total * count_ref[...]
    held[...] = lax.dot_general(
        total[:, rank : 2 * rank],
        total[:, 0:rank],
        (((0,), (0,)), ((), ())),
        precision=lax.Precision.HIGHEST,
        preferred_element_type=F32,
    )
    pairs = out_ref.shape[0]
    even = held[pl.ds(0, pairs, stride=2), :]
    odd = held[pl.ds(1, pairs, stride=2), :]
    out_ref[...] = jnp.concatenate([even, odd], axis=1).astype(BF16)


def hold_kernel(*refs):
    pass


def flatten_kernel(mates, own_ref, far_ref, first_ref, second_ref, wide):
    pairs = own_ref.shape[0]
    slots = first_ref.shape[0]
    core = lax.axis_index("tensor")
    wide[...] = jnp.zeros_like(wide)
    sketch = jnp.where(lax.axis_index("dp") // mates == core, far_ref[...], own_ref[...])
    wide[pl.ds(0, pairs, stride=slots), :] = sketch.astype(F32)
    for out_ref, half in ((first_ref, core), (second_ref, 1 - core)):
        start = half * (slots * pairs // 2)
        for j in range(pairs // 2):
            rows = wide[pl.ds(pl.multiple_of(start + j * slots, slots), slots), :]
            out_ref[:, j * LANES : (j + 1) * LANES] = rows


def products(first_ref, second_ref, own_ref, other_ref):
    total = None
    for flat_ref, query_ref in ((first_ref, own_ref), (second_ref, other_ref)):
        for j in range(query_ref.shape[1] // LANES):
            lanes = slice(j * LANES, (j + 1) * LANES)
            term = query_ref[:, lanes].astype(F32) * flat_ref[0:1, lanes]
            total = term if total is None else total + term
    return total


def score_kernel(first_ref, second_ref, own_ref, other_ref, *refs):
    refs[-1][...] = products(first_ref, second_ref, own_ref, other_ref)


def arrange_kernel(rounds, *refs):
    parts, out_ref, held = refs[4:-2], refs[-2], refs[-1]
    mates = len(rounds)
    own_queries = parts[0].shape[0]
    member = lax.rem(lax.axis_index("dp"), mates)
    sums = [part[...] for part in parts] + [products(*refs[:4])]
    for r, part in zip(rounds, sums):
        start = pl.multiple_of((member ^ r) * own_queries, own_queries)
        held[pl.ds(start, own_queries), :] = part
    out_ref[...] = jnp.sum(held[...].T, axis=0, keepdims=True)


def on_device(activations, out_grads, projections, sample_index, queries):
    clips = lax.axis_size("dp")
    tokens, units = activations.shape[1:]
    rank = projections.shape[1] // 2
    own_queries, entries = queries.shape
    pairs = 2 * entries // LANES
    mates = clips // 2
    slots = 8
    vmem = pl.BlockSpec(memory_space=pltpu.VMEM)
    swap = [(0, 1), (1, 0)]
    both = ("dp", "tensor")

    def place(a, m, t):
        return (a * mates + m) * 2 + t

    spots = [(a, m) for a in range(2) for m in range(mates)]
    there = [(place(a, m, 1 - a), place(1 - a, m, 1 - a)) for a, m in spots]
    there += [(place(a, m, a), place(a, m, 1 - a)) for a, m in spots]
    back = [(dst, src) for src, dst in there]

    copied = 2 * (2 * tokens * units + units * 2 * rank)
    first = pl.pallas_call(
        first_kernel,
        out_specs=vmem,
        out_shape=jax.ShapeDtypeStruct((8, LANES), F32),
        compiler_params=pltpu.CompilerParams(vmem_limit_bytes=1 << 20),
        cost_estimate=pl.CostEstimate(flops=274 * copied, bytes_accessed=1, transcendentals=0),
        name="first",
    )()
    sent, first = lax.optimization_barrier((queries, first))
    halves = [queries]
    for r in range(mates - 1, 0, -1):
        halves.append(lax.ppermute(sent, "dp", [(d, d ^ r) for d in range(clips)]))
    partial = pl.pallas_call(
        functools.partial(project_kernel, rank),
        in_specs=[vmem] * 4,
        out_specs=[vmem] * PIECES,
        out_shape=[jax.ShapeDtypeStruct((tokens // PIECES, 2 * rank), F32)] * PIECES,
        compiler_params=pltpu.CompilerParams(vmem_limit_bytes=16 << 20),
        cost_estimate=pl.CostEstimate(
            flops=8 * tokens * units * rank, bytes_accessed=4 * tokens * units, transcendentals=0
        ),
        name="project",
    )(first, activations, out_grads, projections)

    other = [lax.ppermute(part, "tensor", swap) for part in partial]
    count = pl.pallas_call(
        functools.partial(count_kernel, rank),
        in_specs=[vmem],
        out_specs=vmem,
        out_shape=jax.ShapeDtypeStruct((tokens, 2 * rank), F32),
        compiler_params=pltpu.CompilerParams(vmem_limit_bytes=8 << 20),
        cost_estimate=pl.CostEstimate(flops=1, bytes_accessed=1, transcendentals=0),
        name="count",
    )(sample_index)
    sketch = pl.pallas_call(
        functools.partial(sketch_kernel, rank),
        in_specs=[vmem] * (1 + 2 * len(partial)),
        out_specs=vmem,
        out_shape=jax.ShapeDtypeStruct((pairs, LANES), BF16),
        scratch_shapes=[pltpu.VMEM((rank, rank), F32)],
        compiler_params=pltpu.CompilerParams(vmem_limit_bytes=8 << 20),
        cost_estimate=pl.CostEstimate(flops=1, bytes_accessed=1, transcendentals=0),
        name="sketch",
    )(count, *partial, *other)

    far_sketch = lax.ppermute(sketch, both, there)
    def hold(half, *ended):
        return pl.pallas_call(
            hold_kernel,
            in_specs=[vmem] * (1 + len(ended)),
            out_specs=vmem,
            out_shape=jax.ShapeDtypeStruct(half.shape, BF16),
            input_output_aliases={0: 0},
            compiler_params=pltpu.CompilerParams(vmem_limit_bytes=8 << 20),
            cost_estimate=pl.CostEstimate(flops=1, bytes_accessed=1, transcendentals=0),
            name="hold",
        )(half, *ended)

    for k in range(1, mates - 1):
        halves[k] = hold(halves[k], sketch)
    halves[-1] = hold(halves[-1], *halves[1:-1])
    swapped = [lax.ppermute(half, "tensor", swap) for half in halves]
    width = mates * own_queries
    flats = pl.pallas_call(
        functools.partial(flatten_kernel, mates),
        in_specs=[vmem] * 2,
        out_specs=[vmem] * 2,
        out_shape=[jax.ShapeDtypeStruct((slots, entries), F32)] * 2,
        scratch_shapes=[pltpu.VMEM((pairs * slots, LANES), F32)],
        compiler_params=pltpu.CompilerParams(vmem_limit_bytes=8 << 20),
        cost_estimate=pl.CostEstimate(flops=1 << 34, bytes_accessed=64 << 20, transcendentals=0),
        name="flatten",
    )(sketch, far_sketch)
    small = pl.CostEstimate(flops=1, bytes_accessed=1, transcendentals=0)
    few = pltpu.CompilerParams(vmem_limit_bytes=8 << 20)
    parts = []
    for half, other in zip(halves[:-1], swapped[:-1]):
        before = parts[-1:]
        parts.append(
            pl.pallas_call(
                score_kernel,
                in_specs=[vmem] * (4 + len(before)),
                out_specs=vmem,
                out_shape=jax.ShapeDtypeStruct((own_queries, LANES), F32),
                compiler_params=few,
                cost_estimate=small,
                name="score",
            )(*flats, half, other, *before)
        )
    scores = pl.pallas_call(
        functools.partial(arrange_kernel, [-k % mates for k in range(mates)]),
        in_specs=[vmem] * (mates + 3),
        out_specs=vmem,
        out_shape=jax.ShapeDtypeStruct((1, width), F32),
        scratch_shapes=[pltpu.VMEM((width, LANES), F32)],
        compiler_params=few,
        cost_estimate=small,
        name="arrange",
    )(*flats, halves[-1], swapped[-1], *parts)
    return lax.ppermute(scores, both, back)


def solution(mesh):
    in_specs = (
        P(("groups", "dp"), None, "tensor"),
        P(("groups", "dp"), None, "tensor"),
        P("tensor", None),
        P(("groups", "dp"), None),
        P(("groups", "dp"), "tensor"),
    )
    out_specs = P(("groups", "dp"), "tensor")
    return jax.shard_map(
        on_device, mesh=mesh, in_specs=in_specs, out_specs=out_specs, check_vma=False
    )
```

```python
import functools

import jax
import jax.numpy as jnp
from jax import lax
from jax.experimental import pallas as pl
from jax.experimental.pallas import tpu as pltpu
from jax.sharding import PartitionSpec as P

F32 = jnp.float32
BF16 = jnp.bfloat16
LANES = 128
PIECES = 2


def first_kernel(out_ref):
    out_ref[...] = jnp.zeros_like(out_ref)


def project_kernel(rank, first_ref, acts_ref, grads_ref, proj_ref, *outs):
    rows = outs[0].shape[0]
    column = lax.broadcasted_iota(jnp.int32, (rows, 2 * rank), 1)
    for i, out_ref in enumerate(outs):
        part = slice(i * rows, (i + 1) * rows)
        term = jnp.dot(
            jnp.concatenate([acts_ref[0, part, :], grads_ref[0, part, :]], axis=0),
            proj_ref[...],
            preferred_element_type=F32,
        )
        out_ref[...] = jnp.where(column < rank, term[0:rows], term[rows:])


def count_kernel(rank, picks_ref, out_ref):
    tokens, width = out_ref.shape
    samples = picks_ref.shape[1]
    token = lax.broadcasted_iota(jnp.int32, (tokens, samples), 0)
    hits = jnp.where(token == picks_ref[...], 1.0, 0.0).astype(BF16)
    count = jnp.dot(hits, jnp.ones((samples, width), BF16), preferred_element_type=F32)
    column = lax.broadcasted_iota(jnp.int32, (tokens, width), 1)
    out_ref[...] = jnp.where(column < rank, count, 1.0)


def sketch_kernel(rank, count_ref, *refs):
    parts, (out_ref, held) = refs[:-2], refs[-2:]
    chunks = len(parts) // 2
    total = jnp.concatenate([parts[i][...] + parts[chunks + i][...] for i in range(chunks)], axis=0)
    total = total * count_ref[...]
    held[...] = lax.dot_general(
        total[:, rank : 2 * rank],
        total[:, 0:rank],
        (((0,), (0,)), ((), ())),
        precision=lax.Precision.HIGHEST,
        preferred_element_type=F32,
    )
    pairs = out_ref.shape[0]
    even = held[pl.ds(0, pairs, stride=2), :]
    odd = held[pl.ds(1, pairs, stride=2), :]
    out_ref[...] = jnp.concatenate([even, odd], axis=1).astype(BF16)


def hold_kernel(*refs):
    pass


def flatten_kernel(mates, own_ref, far_ref, first_ref, second_ref, wide):
    pairs = own_ref.shape[0]
    slots = first_ref.shape[0]
    core = lax.axis_index("tensor")
    wide[...] = jnp.zeros_like(wide)
    sketch = jnp.where(lax.axis_index("dp") // mates == core, far_ref[...], own_ref[...])
    wide[pl.ds(0, pairs, stride=slots), :] = sketch.astype(F32)
    for out_ref, half in ((first_ref, core), (second_ref, 1 - core)):
        start = half * (slots * pairs // 2)
        for j in range(pairs // 2):
            rows = wide[pl.ds(pl.multiple_of(start + j * slots, slots), slots), :]
            out_ref[:, j * LANES : (j + 1) * LANES] = rows


def score_kernel(first_ref, second_ref, own_ref, other_ref, *refs):
    out_ref = refs[-1]
    total = None
    for flat_ref, query_ref in ((first_ref, own_ref), (second_ref, other_ref)):
        for j in range(query_ref.shape[1] // LANES):
            lanes = slice(j * LANES, (j + 1) * LANES)
            term = query_ref[:, lanes].astype(F32) * flat_ref[0:1, lanes]
            total = term if total is None else total + term
    out_ref[...] = total


def arrange_kernel(*refs):
    parts, out_ref, held = refs[:-2], refs[-2], refs[-1]
    mates = len(parts)
    own_queries = parts[0].shape[0]
    member = lax.rem(lax.axis_index("dp"), mates)
    for r, part in enumerate(parts):
        start = pl.multiple_of((member ^ r) * own_queries, own_queries)
        held[pl.ds(start, own_queries), :] = part[...]
    out_ref[...] = jnp.sum(held[...].T, axis=0, keepdims=True)


def on_device(activations, out_grads, projections, sample_index, queries):
    clips = lax.axis_size("dp")
    tokens, units = activations.shape[1:]
    rank = projections.shape[1] // 2
    own_queries, entries = queries.shape
    pairs = 2 * entries // LANES
    mates = clips // 2
    slots = 8
    vmem = pl.BlockSpec(memory_space=pltpu.VMEM)
    swap = [(0, 1), (1, 0)]
    both = ("dp", "tensor")

    def place(a, m, t):
        return (a * mates + m) * 2 + t

    spots = [(a, m) for a in range(2) for m in range(mates)]
    there = [(place(a, m, 1 - a), place(1 - a, m, 1 - a)) for a, m in spots]
    there += [(place(a, m, a), place(a, m, 1 - a)) for a, m in spots]
    back = [(dst, src) for src, dst in there]

    copied = 2 * (2 * tokens * units + units * 2 * rank)
    first = pl.pallas_call(
        first_kernel,
        out_specs=vmem,
        out_shape=jax.ShapeDtypeStruct((8, LANES), F32),
        compiler_params=pltpu.CompilerParams(vmem_limit_bytes=1 << 20),
        cost_estimate=pl.CostEstimate(flops=274 * copied, bytes_accessed=1, transcendentals=0),
        name="first",
    )()
    sent, first = lax.optimization_barrier((queries, first))
    halves = [queries]
    for r in range(mates - 1, 0, -1):
        halves.append(lax.ppermute(sent, "dp", [(d, d ^ r) for d in range(clips)]))
    partial = pl.pallas_call(
        functools.partial(project_kernel, rank),
        in_specs=[vmem] * 4,
        out_specs=[vmem] * PIECES,
        out_shape=[jax.ShapeDtypeStruct((tokens // PIECES, 2 * rank), F32)] * PIECES,
        compiler_params=pltpu.CompilerParams(vmem_limit_bytes=16 << 20),
        cost_estimate=pl.CostEstimate(
            flops=8 * tokens * units * rank, bytes_accessed=4 * tokens * units, transcendentals=0
        ),
        name="project",
    )(first, activations, out_grads, projections)

    other = [lax.ppermute(part, "tensor", swap) for part in partial]
    count = pl.pallas_call(
        functools.partial(count_kernel, rank),
        in_specs=[vmem],
        out_specs=vmem,
        out_shape=jax.ShapeDtypeStruct((tokens, 2 * rank), F32),
        compiler_params=pltpu.CompilerParams(vmem_limit_bytes=8 << 20),
        cost_estimate=pl.CostEstimate(flops=1, bytes_accessed=1, transcendentals=0),
        name="count",
    )(sample_index)
    sketch = pl.pallas_call(
        functools.partial(sketch_kernel, rank),
        in_specs=[vmem] * (1 + 2 * len(partial)),
        out_specs=vmem,
        out_shape=jax.ShapeDtypeStruct((pairs, LANES), BF16),
        scratch_shapes=[pltpu.VMEM((rank, rank), F32)],
        compiler_params=pltpu.CompilerParams(vmem_limit_bytes=8 << 20),
        cost_estimate=pl.CostEstimate(flops=1, bytes_accessed=1, transcendentals=0),
        name="sketch",
    )(count, *partial, *other)

    far_sketch = lax.ppermute(sketch, both, there)
    def hold(half, *ended):
        return pl.pallas_call(
            hold_kernel,
            in_specs=[vmem] * (1 + len(ended)),
            out_specs=vmem,
            out_shape=jax.ShapeDtypeStruct(half.shape, BF16),
            input_output_aliases={0: 0},
            compiler_params=pltpu.CompilerParams(vmem_limit_bytes=8 << 20),
            cost_estimate=pl.CostEstimate(flops=1, bytes_accessed=1, transcendentals=0),
            name="hold",
        )(half, *ended)

    for k in range(1, mates - 1):
        halves[k] = hold(halves[k], sketch)
    halves[-1] = hold(halves[-1], *halves[1:-1])
    swapped = [lax.ppermute(half, "tensor", swap) for half in halves]
    width = mates * own_queries
    flats = pl.pallas_call(
        functools.partial(flatten_kernel, mates),
        in_specs=[vmem] * 2,
        out_specs=[vmem] * 2,
        out_shape=[jax.ShapeDtypeStruct((slots, entries), F32)] * 2,
        scratch_shapes=[pltpu.VMEM((pairs * slots, LANES), F32)],
        compiler_params=pltpu.CompilerParams(vmem_limit_bytes=8 << 20),
        cost_estimate=pl.CostEstimate(flops=1 << 34, bytes_accessed=64 << 20, transcendentals=0),
        name="flatten",
    )(sketch, far_sketch)
    small = pl.CostEstimate(flops=1, bytes_accessed=1, transcendentals=0)
    few = pltpu.CompilerParams(vmem_limit_bytes=8 << 20)
    parts = []
    for half, other in zip(halves, swapped):
        before = parts[-1:]
        parts.append(
            pl.pallas_call(
                score_kernel,
                in_specs=[vmem] * (4 + len(before)),
                out_specs=vmem,
                out_shape=jax.ShapeDtypeStruct((own_queries, LANES), F32),
                compiler_params=few,
                cost_estimate=small,
                name="score",
            )(*flats, half, other, *before)
        )
    scores = pl.pallas_call(
        arrange_kernel,
        in_specs=[vmem] * mates,
        out_specs=vmem,
        out_shape=jax.ShapeDtypeStruct((1, width), F32),
        scratch_shapes=[pltpu.VMEM((width, LANES), F32)],
        compiler_params=few,
        cost_estimate=small,
        name="arrange",
    )(parts[0], *parts[:0:-1])
    return lax.ppermute(scores, both, back)


def solution(mesh):
    in_specs = (
        P(("groups", "dp"), None, "tensor"),
        P(("groups", "dp"), None, "tensor"),
        P("tensor", None),
        P(("groups", "dp"), None),
        P(("groups", "dp"), "tensor"),
    )
    out_specs = P(("groups", "dp"), "tensor")
    return jax.shard_map(
        on_device, mesh=mesh, in_specs=in_specs, out_specs=out_specs, check_vma=False
    )
```

```python
import functools

import jax
import jax.numpy as jnp
from jax import lax
from jax.experimental import pallas as pl
from jax.experimental.pallas import tpu as pltpu
from jax.sharding import PartitionSpec as P

F32 = jnp.float32
BF16 = jnp.bfloat16
LANES = 128
PIECES = 2


def first_kernel(out_ref):
    out_ref[...] = jnp.zeros_like(out_ref)


def project_kernel(rank, first_ref, acts_ref, grads_ref, proj_ref, *outs):
    rows = outs[0].shape[0]
    column = lax.broadcasted_iota(jnp.int32, (rows, 2 * rank), 1)
    for i, out_ref in enumerate(outs):
        part = slice(i * rows, (i + 1) * rows)
        term = jnp.dot(
            jnp.concatenate([acts_ref[0, part, :], grads_ref[0, part, :]], axis=0),
            proj_ref[...],
            preferred_element_type=F32,
        )
        out_ref[...] = jnp.where(column < rank, term[0:rows], term[rows:])


def count_kernel(rank, picks_ref, out_ref):
    tokens, width = out_ref.shape
    samples = picks_ref.shape[1]
    token = lax.broadcasted_iota(jnp.int32, (tokens, samples), 0)
    hits = jnp.where(token == picks_ref[...], 1.0, 0.0).astype(BF16)
    count = jnp.dot(hits, jnp.ones((samples, width), BF16), preferred_element_type=F32)
    column = lax.broadcasted_iota(jnp.int32, (tokens, width), 1)
    out_ref[...] = jnp.where(column < rank, count, 1.0)


def sketch_kernel(rank, count_ref, *refs):
    parts, (out_ref, held) = refs[:-2], refs[-2:]
    chunks = len(parts) // 2
    total = jnp.concatenate([parts[i][...] + parts[chunks + i][...] for i in range(chunks)], axis=0)
    total = total * count_ref[...]
    high = total.astype(BF16)
    low = (total - high.astype(F32)).astype(BF16)
    gram = lax.dot_general(
        jnp.concatenate([high, high, low], axis=0),
        jnp.concatenate([high, low, high], axis=0),
        (((0,), (0,)), ((), ())),
        preferred_element_type=F32,
    )
    held[...] = gram[rank : 2 * rank, 0:rank]
    pairs = out_ref.shape[0]
    even = held[pl.ds(0, pairs, stride=2), :]
    odd = held[pl.ds(1, pairs, stride=2), :]
    out_ref[...] = jnp.concatenate([even, odd], axis=1).astype(BF16)


def hold_kernel(*refs):
    pass


def flatten_kernel(mates, own_ref, far_ref, first_ref, second_ref, wide):
    pairs = own_ref.shape[0]
    slots = first_ref.shape[0]
    core = lax.axis_index("tensor")
    wide[...] = jnp.zeros_like(wide)
    sketch = jnp.where(lax.axis_index("dp") // mates == core, far_ref[...], own_ref[...])
    wide[pl.ds(0, pairs, stride=slots), :] = sketch.astype(F32)
    for out_ref, half in ((first_ref, core), (second_ref, 1 - core)):
        start = half * (slots * pairs // 2)
        for j in range(pairs // 2):
            rows = wide[pl.ds(pl.multiple_of(start + j * slots, slots), slots), :]
            out_ref[:, j * LANES : (j + 1) * LANES] = rows


def score_kernel(first_ref, second_ref, own_ref, other_ref, *refs):
    out_ref = refs[-1]
    total = None
    for flat_ref, query_ref in ((first_ref, own_ref), (second_ref, other_ref)):
        for j in range(query_ref.shape[1] // LANES):
            lanes = slice(j * LANES, (j + 1) * LANES)
            term = query_ref[:, lanes].astype(F32) * flat_ref[0:1, lanes]
            total = term if total is None else total + term
    out_ref[...] = total


def arrange_kernel(*refs):
    parts, out_ref, held = refs[:-2], refs[-2], refs[-1]
    mates = len(parts)
    own_queries = parts[0].shape[0]
    member = lax.rem(lax.axis_index("dp"), mates)
    for r, part in enumerate(parts):
        start = pl.multiple_of((member ^ r) * own_queries, own_queries)
        held[pl.ds(start, own_queries), :] = part[...]
    row = lax.dot_general(
        jnp.ones((8, LANES), F32),
        held[...],
        (((1,), (1,)), ((), ())),
        precision=lax.Precision.HIGHEST,
        preferred_element_type=F32,
    )
    out_ref[...] = row[0:1, :]


def on_device(activations, out_grads, projections, sample_index, queries):
    clips = lax.axis_size("dp")
    tokens, units = activations.shape[1:]
    rank = projections.shape[1] // 2
    own_queries, entries = queries.shape
    pairs = 2 * entries // LANES
    mates = clips // 2
    slots = 8
    vmem = pl.BlockSpec(memory_space=pltpu.VMEM)
    swap = [(0, 1), (1, 0)]
    both = ("dp", "tensor")

    def place(a, m, t):
        return (a * mates + m) * 2 + t

    spots = [(a, m) for a in range(2) for m in range(mates)]
    there = [(place(a, m, 1 - a), place(1 - a, m, 1 - a)) for a, m in spots]
    there += [(place(a, m, a), place(a, m, 1 - a)) for a, m in spots]
    back = [(dst, src) for src, dst in there]

    copied = 2 * (2 * tokens * units + units * 2 * rank)
    first = pl.pallas_call(
        first_kernel,
        out_specs=vmem,
        out_shape=jax.ShapeDtypeStruct((8, LANES), F32),
        compiler_params=pltpu.CompilerParams(vmem_limit_bytes=1 << 20),
        cost_estimate=pl.CostEstimate(flops=274 * copied, bytes_accessed=1, transcendentals=0),
        name="first",
    )()
    sent, first = lax.optimization_barrier((queries, first))
    halves = [queries]
    for r in range(mates - 1, 0, -1):
        halves.append(lax.ppermute(sent, "dp", [(d, d ^ r) for d in range(clips)]))
    partial = pl.pallas_call(
        functools.partial(project_kernel, rank),
        in_specs=[vmem] * 4,
        out_specs=[vmem] * PIECES,
        out_shape=[jax.ShapeDtypeStruct((tokens // PIECES, 2 * rank), F32)] * PIECES,
        compiler_params=pltpu.CompilerParams(vmem_limit_bytes=16 << 20),
        cost_estimate=pl.CostEstimate(
            flops=8 * tokens * units * rank, bytes_accessed=4 * tokens * units, transcendentals=0
        ),
        name="project",
    )(first, activations, out_grads, projections)

    other = [lax.ppermute(part, "tensor", swap) for part in partial]
    count = pl.pallas_call(
        functools.partial(count_kernel, rank),
        in_specs=[vmem],
        out_specs=vmem,
        out_shape=jax.ShapeDtypeStruct((tokens, 2 * rank), F32),
        compiler_params=pltpu.CompilerParams(vmem_limit_bytes=8 << 20),
        cost_estimate=pl.CostEstimate(flops=1, bytes_accessed=1, transcendentals=0),
        name="count",
    )(sample_index)
    sketch = pl.pallas_call(
        functools.partial(sketch_kernel, rank),
        in_specs=[vmem] * (1 + 2 * len(partial)),
        out_specs=vmem,
        out_shape=jax.ShapeDtypeStruct((pairs, LANES), BF16),
        scratch_shapes=[pltpu.VMEM((rank, rank), F32)],
        compiler_params=pltpu.CompilerParams(vmem_limit_bytes=8 << 20),
        cost_estimate=pl.CostEstimate(flops=1, bytes_accessed=1, transcendentals=0),
        name="sketch",
    )(count, *partial, *other)

    far_sketch = lax.ppermute(sketch, both, there)
    def hold(half, *ended):
        return pl.pallas_call(
            hold_kernel,
            in_specs=[vmem] * (1 + len(ended)),
            out_specs=vmem,
            out_shape=jax.ShapeDtypeStruct(half.shape, BF16),
            input_output_aliases={0: 0},
            compiler_params=pltpu.CompilerParams(vmem_limit_bytes=8 << 20),
            cost_estimate=pl.CostEstimate(flops=1, bytes_accessed=1, transcendentals=0),
            name="hold",
        )(half, *ended)

    for k in range(1, mates - 1):
        halves[k] = hold(halves[k], sketch)
    halves[-1] = hold(halves[-1], *halves[1:-1])
    swapped = [lax.ppermute(half, "tensor", swap) for half in halves]
    width = mates * own_queries
    flats = pl.pallas_call(
        functools.partial(flatten_kernel, mates),
        in_specs=[vmem] * 2,
        out_specs=[vmem] * 2,
        out_shape=[jax.ShapeDtypeStruct((slots, entries), F32)] * 2,
        scratch_shapes=[pltpu.VMEM((pairs * slots, LANES), F32)],
        compiler_params=pltpu.CompilerParams(vmem_limit_bytes=8 << 20),
        cost_estimate=pl.CostEstimate(flops=1 << 34, bytes_accessed=64 << 20, transcendentals=0),
        name="flatten",
    )(sketch, far_sketch)
    small = pl.CostEstimate(flops=1, bytes_accessed=1, transcendentals=0)
    few = pltpu.CompilerParams(vmem_limit_bytes=8 << 20)
    parts = []
    for half, other in zip(halves, swapped):
        before = parts[-1:]
        parts.append(
            pl.pallas_call(
                score_kernel,
                in_specs=[vmem] * (4 + len(before)),
                out_specs=vmem,
                out_shape=jax.ShapeDtypeStruct((own_queries, LANES), F32),
                compiler_params=few,
                cost_estimate=small,
                name="score",
            )(*flats, half, other, *before)
        )
    scores = pl.pallas_call(
        arrange_kernel,
        in_specs=[vmem] * mates,
        out_specs=vmem,
        out_shape=jax.ShapeDtypeStruct((1, width), F32),
        scratch_shapes=[pltpu.VMEM((width, LANES), F32)],
        compiler_params=few,
        cost_estimate=small,
        name="arrange",
    )(parts[0], *parts[:0:-1])
    return lax.ppermute(scores, both, back)


def solution(mesh):
    in_specs = (
        P(("groups", "dp"), None, "tensor"),
        P(("groups", "dp"), None, "tensor"),
        P("tensor", None),
        P(("groups", "dp"), None),
        P(("groups", "dp"), "tensor"),
    )
    out_specs = P(("groups", "dp"), "tensor")
    return jax.shard_map(
        on_device, mesh=mesh, in_specs=in_specs, out_specs=out_specs, check_vma=False
    )
```

```python
import functools

import jax
import jax.numpy as jnp
from jax import lax
from jax.experimental import pallas as pl
from jax.experimental.pallas import tpu as pltpu
from jax.sharding import PartitionSpec as P

F32 = jnp.float32
BF16 = jnp.bfloat16
LANES = 128
PIECES = 2


def first_kernel(out_ref):
    out_ref[...] = jnp.zeros_like(out_ref)


def project_kernel(rank, first_ref, acts_ref, grads_ref, proj_ref, *outs):
    rows = outs[0].shape[0]
    column = lax.broadcasted_iota(jnp.int32, (rows, 2 * rank), 1)
    for i, out_ref in enumerate(outs):
        part = slice(i * rows, (i + 1) * rows)
        term = jnp.dot(
            jnp.concatenate([acts_ref[0, part, :], grads_ref[0, part, :]], axis=0),
            proj_ref[...],
            preferred_element_type=F32,
        )
        out_ref[...] = jnp.where(column < rank, term[0:rows], term[rows:])


def count_kernel(rank, picks_ref, out_ref):
    tokens, width = out_ref.shape
    samples = picks_ref.shape[1]
    token = lax.broadcasted_iota(jnp.int32, (tokens, samples), 0)
    hits = jnp.where(token == picks_ref[...], 1.0, 0.0).astype(BF16)
    count = jnp.dot(hits, jnp.ones((samples, width), BF16), preferred_element_type=F32)
    column = lax.broadcasted_iota(jnp.int32, (tokens, width), 1)
    out_ref[...] = jnp.where(column < rank, count, 1.0)


def sketch_kernel(rank, count_ref, *refs):
    parts, (out_ref, held) = refs[:-2], refs[-2:]
    chunks = len(parts) // 2
    total = jnp.concatenate([parts[i][...] + parts[chunks + i][...] for i in range(chunks)], axis=0)
    total = total * count_ref[...]
    high = total.astype(BF16)
    low = (total - high.astype(F32)).astype(BF16)
    gram = lax.dot_general(
        jnp.concatenate([high, high, low], axis=0),
        jnp.concatenate([high, low, high], axis=0),
        (((0,), (0,)), ((), ())),
        preferred_element_type=F32,
    )
    held[...] = gram[rank : 2 * rank, 0:rank]
    pairs = out_ref.shape[0]
    even = held[pl.ds(0, pairs, stride=2), :]
    odd = held[pl.ds(1, pairs, stride=2), :]
    out_ref[...] = jnp.concatenate([even, odd], axis=1).astype(BF16)


def hold_kernel(*refs):
    pass


def flatten_kernel(mates, own_ref, far_ref, first_ref, second_ref, wide):
    pairs = own_ref.shape[0]
    slots = first_ref.shape[0]
    core = lax.axis_index("tensor")
    wide[...] = jnp.zeros_like(wide)
    sketch = jnp.where(lax.axis_index("dp") // mates == core, far_ref[...], own_ref[...])
    wide[pl.ds(0, pairs, stride=slots), :] = sketch.astype(F32)
    for out_ref, half in ((first_ref, core), (second_ref, 1 - core)):
        start = half * (slots * pairs // 2)
        for j in range(pairs // 2):
            rows = wide[pl.ds(pl.multiple_of(start + j * slots, slots), slots), :]
            out_ref[:, j * LANES : (j + 1) * LANES] = rows


def score_kernel(first_ref, second_ref, own_ref, other_ref, *refs):
    out_ref = refs[-1]
    totals = [None] * 4
    for i, (flat_ref, query_ref) in enumerate(((first_ref, own_ref), (second_ref, other_ref))):
        for j in range(query_ref.shape[1] // LANES):
            lanes = slice(j * LANES, (j + 1) * LANES)
            term = query_ref[:, lanes].astype(F32) * flat_ref[0:1, lanes]
            at = 2 * i + j % 2
            totals[at] = term if totals[at] is None else totals[at] + term
    total = (totals[0] + totals[1]) + (totals[2] + totals[3])
    out_ref[...] = total


def arrange_kernel(*refs):
    parts, out_ref, held = refs[:-2], refs[-2], refs[-1]
    mates = len(parts)
    own_queries = parts[0].shape[0]
    member = lax.rem(lax.axis_index("dp"), mates)
    for r, part in enumerate(parts):
        start = pl.multiple_of((member ^ r) * own_queries, own_queries)
        held[pl.ds(start, own_queries), :] = part[...]
    out_ref[...] = jnp.sum(held[...].T, axis=0, keepdims=True)


def on_device(activations, out_grads, projections, sample_index, queries):
    clips = lax.axis_size("dp")
    tokens, units = activations.shape[1:]
    rank = projections.shape[1] // 2
    own_queries, entries = queries.shape
    pairs = 2 * entries // LANES
    mates = clips // 2
    slots = 8
    vmem = pl.BlockSpec(memory_space=pltpu.VMEM)
    swap = [(0, 1), (1, 0)]
    both = ("dp", "tensor")

    def place(a, m, t):
        return (a * mates + m) * 2 + t

    spots = [(a, m) for a in range(2) for m in range(mates)]
    there = [(place(a, m, 1 - a), place(1 - a, m, 1 - a)) for a, m in spots]
    there += [(place(a, m, a), place(a, m, 1 - a)) for a, m in spots]
    back = [(dst, src) for src, dst in there]

    copied = 2 * (2 * tokens * units + units * 2 * rank)
    first = pl.pallas_call(
        first_kernel,
        out_specs=vmem,
        out_shape=jax.ShapeDtypeStruct((8, LANES), F32),
        compiler_params=pltpu.CompilerParams(vmem_limit_bytes=1 << 20),
        cost_estimate=pl.CostEstimate(flops=274 * copied, bytes_accessed=1, transcendentals=0),
        name="first",
    )()
    sent, first = lax.optimization_barrier((queries, first))
    halves = [queries]
    for r in range(mates - 1, 0, -1):
        halves.append(lax.ppermute(sent, "dp", [(d, d ^ r) for d in range(clips)]))
    partial = pl.pallas_call(
        functools.partial(project_kernel, rank),
        in_specs=[vmem] * 4,
        out_specs=[vmem] * PIECES,
        out_shape=[jax.ShapeDtypeStruct((tokens // PIECES, 2 * rank), F32)] * PIECES,
        compiler_params=pltpu.CompilerParams(vmem_limit_bytes=16 << 20),
        cost_estimate=pl.CostEstimate(
            flops=8 * tokens * units * rank, bytes_accessed=4 * tokens * units, transcendentals=0
        ),
        name="project",
    )(first, activations, out_grads, projections)

    other = [lax.ppermute(part, "tensor", swap) for part in partial]
    count = pl.pallas_call(
        functools.partial(count_kernel, rank),
        in_specs=[vmem],
        out_specs=vmem,
        out_shape=jax.ShapeDtypeStruct((tokens, 2 * rank), F32),
        compiler_params=pltpu.CompilerParams(vmem_limit_bytes=8 << 20),
        cost_estimate=pl.CostEstimate(flops=1, bytes_accessed=1, transcendentals=0),
        name="count",
    )(sample_index)
    sketch = pl.pallas_call(
        functools.partial(sketch_kernel, rank),
        in_specs=[vmem] * (1 + 2 * len(partial)),
        out_specs=vmem,
        out_shape=jax.ShapeDtypeStruct((pairs, LANES), BF16),
        scratch_shapes=[pltpu.VMEM((rank, rank), F32)],
        compiler_params=pltpu.CompilerParams(vmem_limit_bytes=8 << 20),
        cost_estimate=pl.CostEstimate(flops=1, bytes_accessed=1, transcendentals=0),
        name="sketch",
    )(count, *partial, *other)

    far_sketch = lax.ppermute(sketch, both, there)
    def hold(half, *ended):
        return pl.pallas_call(
            hold_kernel,
            in_specs=[vmem] * (1 + len(ended)),
            out_specs=vmem,
            out_shape=jax.ShapeDtypeStruct(half.shape, BF16),
            input_output_aliases={0: 0},
            compiler_params=pltpu.CompilerParams(vmem_limit_bytes=8 << 20),
            cost_estimate=pl.CostEstimate(flops=1, bytes_accessed=1, transcendentals=0),
            name="hold",
        )(half, *ended)

    for k in range(1, mates - 1):
        halves[k] = hold(halves[k], sketch)
    halves[-1] = hold(halves[-1], *halves[1:-1])
    swapped = [lax.ppermute(half, "tensor", swap) for half in halves]
    width = mates * own_queries
    flats = pl.pallas_call(
        functools.partial(flatten_kernel, mates),
        in_specs=[vmem] * 2,
        out_specs=[vmem] * 2,
        out_shape=[jax.ShapeDtypeStruct((slots, entries), F32)] * 2,
        scratch_shapes=[pltpu.VMEM((pairs * slots, LANES), F32)],
        compiler_params=pltpu.CompilerParams(vmem_limit_bytes=8 << 20),
        cost_estimate=pl.CostEstimate(flops=1 << 34, bytes_accessed=64 << 20, transcendentals=0),
        name="flatten",
    )(sketch, far_sketch)
    small = pl.CostEstimate(flops=1, bytes_accessed=1, transcendentals=0)
    few = pltpu.CompilerParams(vmem_limit_bytes=8 << 20)
    parts = []
    for half, other in zip(halves, swapped):
        before = parts[-1:]
        parts.append(
            pl.pallas_call(
                score_kernel,
                in_specs=[vmem] * (4 + len(before)),
                out_specs=vmem,
                out_shape=jax.ShapeDtypeStruct((own_queries, LANES), F32),
                compiler_params=few,
                cost_estimate=small,
                name="score",
            )(*flats, half, other, *before)
        )
    scores = pl.pallas_call(
        arrange_kernel,
        in_specs=[vmem] * mates,
        out_specs=vmem,
        out_shape=jax.ShapeDtypeStruct((1, width), F32),
        scratch_shapes=[pltpu.VMEM((width, LANES), F32)],
        compiler_params=few,
        cost_estimate=small,
        name="arrange",
    )(parts[0], *parts[:0:-1])
    return lax.ppermute(scores, both, back)


def solution(mesh):
    in_specs = (
        P(("groups", "dp"), None, "tensor"),
        P(("groups", "dp"), None, "tensor"),
        P("tensor", None),
        P(("groups", "dp"), None),
        P(("groups", "dp"), "tensor"),
    )
    out_specs = P(("groups", "dp"), "tensor")
    return jax.shard_map(
        on_device, mesh=mesh, in_specs=in_specs, out_specs=out_specs, check_vma=False
    )
```
